32 devices in a mesh: expert: 4 (over x, core), shard: 8 (over z, y).
Axes of the slice: x: 2, y: 2, z: 4, core: 2. Of those that a mesh axis runs over, the one named last changes fastest.
Arguments:
- tokens_in: bfloat16 [4096, 2048], P(('expert', 'shard')), may hold values from -6 to 6
- cotangent: bfloat16 [4096, 2048], P(('expert', 'shard')), may hold values from -6 to 6
- norm1_gain: float32 [2048], replicated, may hold values from 0.5 to 1.5
- kv_weight: bfloat16 [2048, 4096], P('shard'), may hold values from -0.125 to 0.125
- query_weight: bfloat16 [4, 2048, 2048], P('expert', 'shard'), may hold values from -0.125 to 0.125
- attn_out_weight: bfloat16 [4, 2048, 2048], P('expert', 'shard'), may hold values from -1 to 1
- attn_router: bfloat16 [2048, 4], replicated, may hold values from -0.09375 to 0.09375
- norm2_gain: float32 [2048], replicated, may hold values from 0.5 to 1.5
- in_weight: bfloat16 [4, 2048, 11264], P('expert', 'shard'), may hold values from -0.125 to 0.125
- out_weight: bfloat16 [4, 5632, 2048], P('expert', 'shard'), may hold values from -0.078125 to 0.078125
- mlp_router: bfloat16 [2048, 4], replicated, may hold values from -0.09375 to 0.09375
- attn_routes: int32 [4096, 2], P(('expert', 'shard')), may hold values from 0 to 3, all different within a row; in each aligned block of 128 rows (0 to 127, 128 to 255, ...) at most 80 rows name the same one
- mlp_routes: int32 [4096, 2], P(('expert', 'shard')), may hold values from 0 to 3, all different within a row; in each aligned block of 128 rows (0 to 127, 128 to 255, ...) at most 80 rows name the same one
- place_order: int32 [4, 1024], P('expert', 'shard'), may hold values from 0 to 1023, each once within a row
- seq_lengths: int32 [4, 4], P('expert'), may hold values from 1 to 512, 1024 in all within a row
Outputs:
- output: bfloat16 [4096, 2048], P(('expert', 'shard'))
- grad_input: float32 [4096, 2048], P(('expert', 'shard'))
- grad_norm1: float32 [2048], replicated
- grad_kv_weight: float32 [2048, 4096], P('shard')
- grad_query_weight: float32 [4, 2048, 2048], P('expert', 'shard')
- grad_attn_out: float32 [4, 2048, 2048], P('expert', 'shard')
- grad_router_attn: float32 [2048, 4], replicated
- grad_norm2: float32 [2048], replicated
- grad_in_weight: float32 [4, 2048, 11264], P('expert', 'shard')
- grad_out_weight: float32 [4, 5632, 2048], P('expert', 'shard')
- grad_router_mlp: float32 [2048, 4], replicated
The draws below stay inside these ranges and needn't reach their ends.
Inputs may be any that keep to these rules, and one draw needn't show every extreme that they name: `attn_routes`: in the 128 rows of one device no expert is named by more than 80 rows, and in some devices one expert is named by exactly 80; a row's two experts differ. `mlp_routes`: in the 128 rows of one device no expert is named by more than 80 rows, and in some devices one expert is named by exactly 80; a row's two experts differ. `place_order`: each row is a permutation of the places of its group. `seq_lengths`: each row sums to 1024 and its largest entry is 512.
All inputs are finite; a program needn't handle non-finite values.
Results may differ from the reference program's by a relative error of at most 0.023.
Values may be sent and summed in bfloat16 or wider, within the bound.
No kernel may reach another device: no remote copies, remote signals or barrier semaphores. Data moves between devices by JAX's collectives and lax.ppermute only.
A program may use at most 512 MiB of HBM per device.

```python
import math
from functools import partial
import jax
import jax.numpy as jnp
import numpy as np
from jax import lax

D = 2048
HD = 128
FF = 5632
TOK_DEV = 128
SEQS = 4
E = 4
HQ = 2048
TOKENS = 4096
GROUP_TOK = 1024
LEN_MAX = 512
CAP = 80
N_EXPERT = 4
N_SHARD = 8


def block_levels(stream_key, shape, pieces, least, top_value):
    def one(axis_at, shards_of):
        steps = jax.random.uniform(jax.random.fold_in(jax.random.fold_in(stream_key, 6), axis_at), (shards_of,), jnp.float32, least / len(pieces), top_value / len(pieces))
        return jnp.repeat(jnp.exp(steps), shape[axis_at] // shards_of).reshape((-1,) + (1,) * (len(shape) - axis_at - 1))

    level = one(*pieces[0])
    for cut in pieces[1:]:
        level = level * one(*cut)
    return level


def length_profile(number_of, total, bound, slope):
    portions = [(1 << 20) // math.isqrt(grade ** slope) + 1 for grade in range(2, number_of + 1)]
    spare, given = total - bound - (number_of - 1), [1] * (number_of - 1)
    while spare > 0:
        free = [i for i in range(number_of - 1) if given[i] < bound]
        whole, budget = sum([portions[i] for i in free]), spare
        for i in free:
            addition = min(bound - given[i], max(1, budget * portions[i] // whole), spare)
            given[i] = given[i] + addition
            spare = spare - addition
    return np.array([bound] + given)


def uneven(key, amount, total, bound, slope):
    if amount == 2:
        one = jax.random.randint(key, (), max(1, total - bound), min(bound, total - 1) + 1)
        return jnp.stack([one, total - one])
    sizes = jnp.asarray(length_profile(amount, total, bound, slope), jnp.int32)
    twos = (amount - 1) // 2
    giver, receiver = sizes[1:1 + 2 * twos:2], sizes[2:2 + 2 * twos:2]
    room = jnp.minimum(giver - 1, bound - receiver)
    moved = jax.random.randint(jax.random.fold_in(key, 1), (twos,), 0, 1 << 20) % (room + 1)
    sizes = sizes.at[1:1 + 2 * twos:2].set(giver - moved).at[2:2 + 2 * twos:2].set(receiver + moved)
    return sizes[jax.random.permutation(jax.random.fold_in(key, 2), amount)]


def routed_block(rng, own, number, rows, number_of, top, limit, lean):
    ranking = jax.random.permutation(rng, number_of)
    heavy_load, common = shares(number_of, rows * top, limit, lean, True), shares(number_of, rows * top, limit, lean, False)
    places = jnp.arange(number_of)

    def named(tallies, rotation):
        used = int((tallies > 0).sum())
        fixed = max(1, used // 4)
        moved = fixed + (places - fixed + rotation * (used - fixed)) % max(1, number_of - fixed)
        return jnp.zeros((number_of,), jnp.int32).at[ranking[jnp.where(places < fixed, places, moved)]].set(jnp.asarray(tallies, jnp.int32))

    tallies = jnp.where(number % 4 == 0, named(heavy_load, number // 4), named(common, number - number // 4 - 1))
    mixed = jax.random.permutation(jax.random.fold_in(own, 3), number_of)
    giver, taker = mixed[0:number_of // 2 * 2:2], mixed[1:number_of // 2 * 2:2]
    room = jnp.minimum(tallies[giver] - 1, limit - tallies[taker]) // 2
    room = jnp.where((giver == ranking[0]) | (taker == ranking[0]) | (tallies[taker] == 0), 0, jnp.maximum(room, 0))
    moved = jax.random.randint(jax.random.fold_in(own, 4), (number_of // 2,), 0, 1 << 20) % (room + 1)
    tallies = tallies.at[giver].add(-moved).at[taker].add(moved)
    members = jnp.searchsorted(jnp.cumsum(tallies), jnp.arange(rows * top), side="right").astype(jnp.int32)
    grid = members.reshape(top, rows).T
    grid = grid[jax.random.permutation(jax.random.fold_in(own, 1), rows)]
    rotation = jax.random.randint(jax.random.fold_in(own, 2), (rows, 1), 0, top)
    return jnp.take_along_axis(grid, (jnp.arange(top)[None, :] + rotation) % top, axis=1)


def shares(number_of, total, reach, lean, full):
    portions = [(1 << 20) // math.isqrt(grade ** lean) + 1 for grade in range(1, number_of + 1)]
    largest = reach if full else min(reach, max(-(-total // number_of), total * portions[0] // sum(portions)))
    least = 1 if total - largest >= number_of - 1 else 0
    given, spare = [largest] + [least] * (number_of - 1), total - largest - least * (number_of - 1)
    while spare > 0:
        candidates = [i for i in range(1, number_of) if given[i] < largest] or [i for i in range(1, number_of) if given[i] < reach]
        whole, budget = sum([portions[i] for i in candidates]), spare
        for i in candidates:
            addition = min(reach - given[i], max(1, budget * portions[i] // whole), spare)
            given[i] = given[i] + addition
            spare = spare - addition
    return np.array(given)


def bell_draw(stream_key, extent, spread, reach, shards=(), kind=jnp.bfloat16):
    gain = block_levels(stream_key, extent, shards, -0.22, 0.18) if shards else 1.0
    array = jax.random.normal(stream_key, extent, jnp.float32) * spread * gain
    return jnp.minimum(jnp.maximum(array, -reach), reach).astype(kind)


def setup_inputs(seed: int = 0) -> dict:
    streams_of = jax.random.split(jax.random.key(seed), 16)
    tokens_in = bell_draw(streams_of[0], (TOKENS, D), 1.0, 6.0, ((0, 32),))
    cotangent = bell_draw(streams_of[1], (TOKENS, D), 1.0, 6.0, ((0, 32),))
    norm1_gain = jnp.clip(1.0 + 0.1 * jax.random.normal(streams_of[2], (D,), jnp.float32), 0.5, 1.5)
    kv_weight = bell_draw(streams_of[3], (D, 2 * HQ), D ** -0.5, 0.125, ((0, 8),))
    query_weight = bell_draw(streams_of[4], (E, D, HQ), D ** -0.5, 0.125, ((0, 4), (1, 8)))
    attn_out_weight = bell_draw(streams_of[5], (E, HQ, D), (max(4, 8 * HQ // LEN_MAX)) ** -0.5, 1.0, ((0, 4), (1, 8)))
    attn_router = bell_draw(streams_of[6], (D, E), (2 * D) ** -0.5, 0.09375)
    norm2_gain = jnp.clip(1.0 + 0.1 * jax.random.normal(streams_of[7], (D,), jnp.float32), 0.5, 1.5)
    in_weight = bell_draw(streams_of[8], (E, D, 2 * FF), D ** -0.5, 0.125, ((0, 4), (1, 8)))
    out_weight = bell_draw(streams_of[9], (E, FF, D), FF ** -0.5, 0.078125, ((0, 4), (1, 8)))
    mlp_router = bell_draw(streams_of[10], (D, E), (2 * D) ** -0.5, 0.09375)
    attn_routes_keys = jax.random.split(jax.random.fold_in(streams_of[11], 1), TOKENS // TOK_DEV)
    attn_routes_turns = jax.random.permutation(jax.random.fold_in(streams_of[11], 3), TOKENS // TOK_DEV)
    attn_routes = jax.vmap(lambda own, number: routed_block(jax.random.fold_in(streams_of[11], 2), own, number, TOK_DEV, E, 2, CAP, 2))(attn_routes_keys, attn_routes_turns).reshape((TOKENS, 2))
    mlp_routes_keys = jax.random.split(jax.random.fold_in(streams_of[12], 1), TOKENS // TOK_DEV)
    mlp_routes_turns = jax.random.permutation(jax.random.fold_in(streams_of[12], 3), TOKENS // TOK_DEV)
    mlp_routes = jax.vmap(lambda own, number: routed_block(jax.random.fold_in(streams_of[12], 2), own, number, TOK_DEV, E, 2, CAP, 2))(mlp_routes_keys, mlp_routes_turns).reshape((TOKENS, 2))
    place_order = jax.vmap(lambda own: jax.random.permutation(own, GROUP_TOK))(jax.random.split(streams_of[13], N_EXPERT)).reshape((N_EXPERT, GROUP_TOK)).astype(jnp.int32)
    seq_lengths = jax.vmap(lambda own: uneven(own, SEQS, GROUP_TOK, LEN_MAX, 1))(jax.random.split(streams_of[14], N_EXPERT)).reshape((N_EXPERT, SEQS)).astype(jnp.int32)
    return {"tokens_in": tokens_in, "cotangent": cotangent, "norm1_gain": norm1_gain, "kv_weight": kv_weight, "query_weight": query_weight, "attn_out_weight": attn_out_weight, "attn_router": attn_router, "norm2_gain": norm2_gain, "in_weight": in_weight, "out_weight": out_weight, "mlp_router": mlp_router, "attn_routes": attn_routes, "mlp_routes": mlp_routes, "place_order": place_order, "seq_lengths": seq_lengths}


EPS = 1e-05
THETA = 10000.0
NEG = -1e+30

@jax.custom_vjp
def low(v):
    return lax.optimization_barrier(v.astype(jnp.bfloat16)).astype(jnp.float32)

@jax.custom_vjp
def low_back(v):
    return v

def low_keep(v):
    return (low(v), None)

def low_pass(kept, grad):
    return (grad,)

def back_keep(v):
    return (v, None)

def back_low(kept, grad):
    return (low(grad),)
low.defvjp(low_keep, low_pass)
low_back.defvjp(back_keep, back_low)

def matmul(left_side, right_side):
    return jnp.dot(left_side, right_side, precision=lax.Precision.HIGHEST)

def expert_product(buffer, weight):
    return jnp.einsum('erd,edf->erf', buffer, weight, precision=lax.Precision.HIGHEST)

def norm_rows(values, norm_gain):
    row_scale = lax.rsqrt(lax.optimization_barrier(jnp.mean(values * values, axis=-1, keepdims=True)) + EPS)
    return values * row_scale * norm_gain

def seq_of(places, lengths):
    seq_ends = jnp.cumsum(lengths)
    passed = seq_ends[None, :] <= places[:, None]
    return (passed, lax.optimization_barrier(jnp.sum(passed.astype(jnp.int32), axis=1)))

def rope_tables(places, lengths):
    passed, seq_ids = seq_of(places, lengths)
    starts = lax.optimization_barrier(jnp.sum(jnp.where(passed, lengths[None, :], 0), axis=1))
    where_in = (places - starts).astype(jnp.float32)
    frequency = THETA ** (-jnp.arange(0, HD // 2, dtype=jnp.float32) * (2.0 / HD))
    angles = where_in[:, None] * frequency[None, :]
    return (jnp.cos(angles), jnp.sin(angles), seq_ids)

def rotate(values, cosine, sine_table):
    half_width = values.shape[-1] // 2
    leading = values[..., :half_width]
    trailing = values[..., half_width:]
    return jnp.concatenate([leading * cosine - trailing * sine_table, trailing * cosine + leading * sine_table], axis=-1)

def slot_index(routes, experts):
    blocks = routes.reshape(N_SHARD, -1)
    onehot = (blocks[:, :, None] == jnp.arange(experts, dtype=jnp.int32)[None, None, :]).astype(jnp.int32)
    before = jnp.cumsum(onehot, axis=1) - onehot
    slot_rank = lax.optimization_barrier(jnp.sum(before * onehot, axis=2))
    device = jnp.arange(N_SHARD, dtype=jnp.int32)[:, None]
    return (blocks * (N_SHARD * CAP) + device * CAP + slot_rank).reshape(-1).astype(jnp.int32)

def dispatch(slot_rows, slot_pos, experts):
    buffer = jnp.zeros((experts * N_SHARD * CAP, slot_rows.shape[1]), slot_rows.dtype)
    return buffer.at[slot_pos].set(slot_rows).reshape(experts, N_SHARD * CAP, -1)

def combine(buffer, slot_pos):
    return buffer.reshape(-1, buffer.shape[-1])[slot_pos]

def pair_gates(logits, routes, experts):
    hot = (routes[:, :, None] == jnp.arange(experts, dtype=jnp.int32)[None, None, :]).astype(jnp.float32)
    picked = lax.optimization_barrier(jnp.sum(logits[:, None, :] * hot, axis=-1))
    return jax.nn.softmax(picked, axis=-1)

def head_attention(allowed, inputs):
    query_part, key_part, value_part = inputs
    scores = low_back(matmul(query_part, key_part.T)) * HD ** (-0.5)
    scores = jnp.where(allowed, scores, NEG)
    row_top = lax.optimization_barrier(jnp.max(scores, axis=1, keepdims=True))
    exp_scores = jnp.exp(scores - row_top)
    prob_vals = exp_scores / lax.optimization_barrier(jnp.sum(exp_scores, axis=1, keepdims=True))
    return matmul(low(prob_vals), value_part)

def group_layer(weights, inputs):
    norm1_gain, kv_weight, query_weight, attn_out_weight, attn_router, norm2_gain, in_weight, out_weight, mlp_router = weights
    stream, places, lengths, attn_routes, mlp_routes = inputs
    experts = query_weight.shape[0]
    group_rows = stream.shape[0]
    cosine, sine_table, seq_ids = rope_tables(places, lengths)
    hidden1 = low(norm_rows(stream, norm1_gain))
    kv_proj = low_back(matmul(hidden1, kv_weight))
    query_width = kv_proj.shape[1] // 2
    key_rows = low(rotate(kv_proj[:, :query_width].reshape(group_rows, -1, HD), cosine[:, None], sine_table[:, None]))
    value_rows = low(kv_proj[:, query_width:].reshape(group_rows, -1, HD))
    gates_attn = pair_gates(matmul(hidden1, attn_router), attn_routes, experts)
    index_attn = slot_index(attn_routes, experts)
    rows_attn = low_back(dispatch(jnp.repeat(hidden1, 2, axis=0), index_attn, experts))
    query_raw = low(low_back(expert_product(rows_attn, query_weight)))
    query_tok = combine(query_raw, index_attn).reshape(group_rows, 2, -1, HD)
    query_rows = low(rotate(query_tok, cosine[:, None, None], sine_table[:, None, None]))
    query_heads = jnp.moveaxis(query_rows.reshape(2 * group_rows, -1, HD), 1, 0)
    key_heads = jnp.moveaxis(key_rows, 1, 0)
    value_heads = jnp.moveaxis(value_rows, 1, 0)
    query_seq = jnp.repeat(seq_ids, 2)
    query_place = jnp.repeat(places, 2)
    allowed = (query_seq[:, None] == seq_ids[None, :]) & (places[None, :] <= query_place[:, None])
    attn_heads = lax.map(jax.checkpoint(partial(head_attention, allowed)), (query_heads, key_heads, value_heads))
    attn_vec = jnp.moveaxis(attn_heads, 0, 1).reshape(2 * group_rows, -1)
    attn_sent = low(low_back(attn_vec))
    proj_attn = low(low_back(expert_product(dispatch(attn_sent, index_attn, experts), attn_out_weight)))
    back_attn = combine(proj_attn, index_attn).reshape(group_rows, 2, -1)
    middle = stream + lax.optimization_barrier(jnp.sum(gates_attn[..., None] * back_attn, axis=1))
    hidden2 = low(norm_rows(middle, norm2_gain))
    gates_mlp = pair_gates(matmul(hidden2, mlp_router), mlp_routes, experts)
    index_mlp = slot_index(mlp_routes, experts)
    rows_mlp = low_back(dispatch(jnp.repeat(hidden2, 2, axis=0), index_mlp, experts))
    joint_proj = low_back(expert_product(rows_mlp, in_weight))
    inner_width = joint_proj.shape[-1] // 2
    activated = low(jax.nn.silu(joint_proj[..., :inner_width]) * joint_proj[..., inner_width:])
    proj_mlp = low(low_back(expert_product(activated, out_weight)))
    back_mlp = combine(proj_mlp, index_mlp).reshape(group_rows, 2, -1)
    return middle + lax.optimization_barrier(jnp.sum(gates_mlp[..., None] * back_mlp, axis=1))

def reference(tokens_in, cotangent, norm1_gain, kv_weight, query_weight, attn_out_weight, attn_router, norm2_gain, in_weight, out_weight, mlp_router, attn_routes, mlp_routes, place_order, seq_lengths):
    groups = place_order.shape[0]
    weights = tuple((weight_arg.astype(jnp.float32) for weight_arg in (norm1_gain, kv_weight, query_weight, attn_out_weight, attn_router, norm2_gain, in_weight, out_weight, mlp_router)))
    stream = tokens_in.astype(jnp.float32)

    def whole(stream_in, weight_set):

        def group_step(carry_val, inputs):
            return (carry_val, jax.checkpoint(group_layer)(weight_set, inputs))
        _, layer_out = lax.scan(group_step, jnp.zeros((), jnp.float32), (stream_in.reshape(groups, -1, stream_in.shape[1]), place_order, seq_lengths, attn_routes.reshape(groups, -1, 2), mlp_routes.reshape(groups, -1, 2)))
        return layer_out.reshape(stream_in.shape)
    result, pullback = jax.vjp(whole, stream, weights)
    grad_stream, grad_set = pullback(cotangent.astype(jnp.float32))
    return (result.astype(jnp.bfloat16), grad_stream, grad_set[0], grad_set[1], grad_set[2], grad_set[3], grad_set[4], grad_set[5], grad_set[6], grad_set[7], grad_set[8])
```

```python
import functools

import jax
import jax.numpy as jnp
from jax import lax
from jax.experimental import pallas as pl
from jax.experimental.pallas import tpu as pltpu
from jax.sharding import PartitionSpec as P

HD = 128


EPS = 1e-05
THETA = 10000.0
NEG = -1e30
F32 = jnp.float32
BF16 = jnp.bfloat16
VMEM_LIMIT = 60 * 1024 * 1024


def dot(left, right, contract=((1,), (0,))):
    return lax.dot_general(left, right, (contract, ((), ())), preferred_element_type=F32)


def norm_rows(values, norm_gain):
    row_scale = lax.rsqrt(jnp.mean(values * values, axis=-1, keepdims=True) + EPS)
    return (values * row_scale * norm_gain, row_scale)


def norm_back(grad_rows, values, row_scale, norm_gain):
    gain_grad = jnp.sum(grad_rows * values * row_scale, axis=0)
    scaled_grad = grad_rows * norm_gain
    mean_term = jnp.mean(scaled_grad * values, axis=-1, keepdims=True)
    return (
        row_scale * scaled_grad - values * row_scale * row_scale * row_scale * mean_term,
        gain_grad,
    )


def seq_of(places, lengths):
    seq_ends = jnp.cumsum(lengths)
    passed = seq_ends[None, :] <= places[:, None]
    return (passed, jnp.sum(passed.astype(jnp.int32), axis=1))


def rope_tables(places, lengths):
    passed, seq_ids = seq_of(places, lengths)
    starts = jnp.sum(jnp.where(passed, lengths[None, :], 0), axis=1)
    where_in = (places - starts).astype(F32)
    frequency = THETA ** (-jnp.arange(0, HD // 2, dtype=F32) * (2.0 / HD))
    angles = where_in[:, None] * frequency[None, :]
    return (jnp.cos(angles), jnp.sin(angles), seq_ids)


def rotate(values, cosine, sine_table):
    half_width = values.shape[-1] // 2
    leading = values[..., :half_width]
    trailing = values[..., half_width:]
    return jnp.concatenate(
        [leading * cosine - trailing * sine_table, trailing * cosine + leading * sine_table],
        axis=-1,
    )


def ring_cycle(count):
    if count == 8:
        return [0, 2, 4, 6, 7, 5, 3, 1]
    if count == 16:
        return [0, 1, 2, 3, 7, 6, 5, 9, 10, 11, 15, 14, 13, 12, 8, 4]
    return list(range(count))


def ring_move(value, hops):
    cycle = ring_cycle(lax.axis_size("shard"))
    count = len(cycle)
    return lax.ppermute(
        value, "shard", [(cycle[i], cycle[(i + hops) % count]) for i in range(count)]
    )


def after(value, *others):
    return lax.optimization_barrier((value,) + others)[0] if others else value


def ring_gather(block, ties=()):
    count = lax.axis_size("shard")
    far = count // 2
    ahead, behind = [block], [block]
    for step in range(far):
        if step < len(ties):
            ahead[-1] = after(ahead[-1], *ties[step])
        if step < far - 1:
            ahead.append(ring_move(ahead[-1], 1))
            behind.append(ring_move(behind[-1], -1))
    cut = block.shape[0] // 2
    last = [ring_move(ahead[-1][:cut], 1), ring_move(behind[-1][cut:], -1)]
    return jnp.concatenate(ahead + last + behind[:0:-1], axis=0)


def direct_gather(block):
    count = lax.axis_size("shard")
    return jnp.stack([block] + [ring_move(block, r) for r in range(1, count)])


def ring_scatter(partial, ties=()):
    count = lax.axis_size("shard")
    far = count // 2
    rows = partial.shape[0] // count
    cut = rows // 2
    tie = lambda value, step: after(value, *ties[step]) if step < len(ties) else value
    partial = tie(partial, 0)
    part = [partial[r * rows : (r + 1) * rows] for r in range(count)]
    low = ring_move(part[far][:cut], -1)
    high = ring_move(part[far][cut:], 1)
    empty = jnp.zeros_like(low)
    back = part[far - 1] + jnp.concatenate([low, empty], axis=0)
    fore = part[far + 1] + jnp.concatenate([empty, high], axis=0)
    for r in range(far - 2, 0, -1):
        back = tie(back, far - 1 - r)
        back = part[r] + ring_move(back, -1)
        fore = part[count - r] + ring_move(fore, 1)
    back = tie(back, far - 1)
    return part[0].astype(F32) + ring_move(back, -1).astype(F32) + ring_move(fore, 1).astype(F32)


def direct_scatter(partial):
    count = lax.axis_size("shard")
    total = partial[0]
    for r in range(1, count):
        total = total + ring_move(partial[r], -r)
    return total


def core_swap(value):
    return lax.ppermute(value, "expert", [(i, i ^ 1) for i in range(lax.axis_size("expert"))])


def chip_shift(value, hops):
    count = lax.axis_size("expert")
    chips = count // 2
    return lax.ppermute(
        value, "expert", [(i, (i // 2 + hops) % chips * 2 + i % 2) for i in range(count)]
    )


def expert_order():
    index = lax.axis_index("expert")
    chips = lax.axis_size("expert") // 2
    return [
        (index // 2 + dx) % chips * 2 + (index % 2 + dc) % 2
        for dx in range(chips)
        for dc in range(2)
    ]


def expert_gather(value):
    chips = lax.axis_size("expert") // 2
    own = [value] + [chip_shift(value, -dx) for dx in range(1, chips)]
    return [piece for item in own for piece in (item, core_swap(item))]


def after_all(values, *others):
    return [after(item, *others) for item in values]


def far_halves(sums):
    cut = sums[0].shape[0] // 2
    return [item[:cut] for item in sums], [item[cut:] for item in sums]


def whole_halves(first, second):
    return [jnp.concatenate(pair, axis=0) for pair in zip(first, second)]


def expert_sums(pieces, firsts):
    return [
        (pieces[k].astype(F32) + core_swap(pieces[k + 1]).astype(F32)).astype(BF16) for k in firsts
    ]


def far_exchange(sums):
    return [chip_shift(item, dx + 1) for dx, item in enumerate(sums)]


def sum_f32(parts):
    return sum(item.astype(F32) for item in parts)


def expert_reduce(pieces):
    sums = expert_sums(pieces, range(0, len(pieces), 2))
    return sum_f32(sums[:1] + far_exchange(sums[1:]))


def shard_exchange(pieces):
    return lax.all_to_all(pieces, "shard", split_axis=0, concat_axis=0, tiled=True)


def sum_all(value):
    for axis in ("expert", "shard"):
        count = lax.axis_size(axis)
        step = 1
        while step < count:
            value = value + lax.ppermute(value, axis, [(i, i ^ step) for i in range(count)])
            step *= 2
    return value


def turn(values, cosine, sine_table):
    return values * cosine + pltpu.roll(values, HD // 2, 1) * sine_table


def whole(shape):
    zeros = (0,) * len(shape)
    return pl.BlockSpec(shape, lambda *_: zeros, pipeline_mode=pl.Buffered(1))


def tiles(shape):
    return pl.BlockSpec(shape, lambda i: (i,) + (0,) * (len(shape) - 1))


def named_by(routes, order, slot, k):
    return (routes[:, slot : slot + 1] == order[0, k]).astype(F32)


def columns(parts):
    lane = lax.broadcasted_iota(jnp.int32, (parts[0].shape[0], len(parts)), 1)
    total = jnp.zeros(lane.shape, F32)
    for k, part in enumerate(parts):
        total = jnp.where(lane == k, part, total)
    return total


def attend_kernel(experts, order, hidden, *refs):
    query_w, refs = refs[:experts], refs[experts:]
    kv_w, refs = refs[0], refs[1:]
    out_w, refs = refs[:experts], refs[experts:]
    router, routes_ref, bounds, place_row, cosine, sine_table = refs[:6]
    mixed, query_out, keys, values, wide, gates_out = refs[6:]
    step = pl.program_id(0)
    tile = mixed.shape[0]
    total_rows, span = keys.shape

    @pl.when(step == 0)
    def _():
        @pl.loop(0, total_rows // tile)
        def _(i):
            here = pl.ds(pl.multiple_of(i * tile, tile), tile)
            both = dot(hidden[here, :], kv_w[...])
            for h in range(span // HD):
                cols = slice(h * HD, (h + 1) * HD)
                keys[here, cols] = turn(both[:, cols], cosine[here, :], sine_table[here, :]).astype(BF16)
            values[here, :] = both[:, span:].astype(BF16)

    here = pl.ds(pl.multiple_of(step * tile, tile), tile)
    rows_in = hidden[here, :]
    routes = routes_ref[...]
    hot = [[named_by(routes, order, j, k) for k in range(experts)] for j in range(2)]
    logits = dot(rows_in, router[...])
    picked = [sum(hot[j][k] * logits[:, k : k + 1] for k in range(experts)) for j in range(2)]
    top = jnp.maximum(picked[0], picked[1])
    raised = [jnp.exp(value - top) for value in picked]
    gates = [value / (raised[0] + raised[1]) for value in raised]
    gates_out[...] = columns([hot[0][k] * gates[0] + hot[1][k] * gates[1] for k in range(experts)])
    query_all = [dot(rows_in, query_w[k][...]) for k in range(experts)]
    allowed = (place_row[...] >= bounds[:, 0:1]) & (place_row[...] <= bounds[:, 1:2])
    cos_here, sin_here = cosine[here, :], sine_table[here, :]
    vectors = []
    for j in range(2):
        raw = sum(hot[j][k] * query_all[k] for k in range(experts))
        heads = []
        for h in range(span // HD):
            cols = slice(h * HD, (h + 1) * HD)
            query = turn(raw[:, cols], cos_here, sin_here).astype(BF16)
            query_out[:, j * span + h * HD : j * span + (h + 1) * HD] = query
            scores = dot(query, keys[:, cols], ((1,), (1,))) * HD**-0.5
            scores = jnp.where(allowed, scores, NEG)
            row_top = jnp.max(scores, axis=1, keepdims=True)
            exp_scores = jnp.exp(scores - row_top)
            row_total = jnp.sum(exp_scores, axis=1, keepdims=True)
            heads.append(dot(exp_scores.astype(BF16), values[:, cols]) / row_total)
        vectors.append((jnp.concatenate(heads, axis=1) if len(heads) > 1 else heads[0]) * gates[j])
    total = 0.0
    for k in range(experts):
        part = (hot[0][k] * vectors[0] + hot[1][k] * vectors[1]).astype(BF16)
        wide[:, k * span : (k + 1) * span] = part
        total = total + dot(part, out_w[k][...])
    mixed[...] = total.astype(BF16)


def attend(hidden, query_w, kv_w, out_w, router, routes, order, bounds, place_row, cosine, sine_table):
    total_rows, width = hidden.shape
    experts = len(query_w)
    span = query_w[0].shape[1]
    tile = 256
    return pl.pallas_call(
        functools.partial(attend_kernel, experts),
        grid=(total_rows // tile,),
        in_specs=[pl.BlockSpec(memory_space=pltpu.SMEM), whole(hidden.shape)]
        + [whole(w.shape) for w in query_w]
        + [whole(kv_w.shape)]
        + [whole(w.shape) for w in out_w]
        + [
            whole(router.shape),
            tiles((tile, 2)),
            tiles((tile, 2)),
            whole(place_row.shape),
            whole(cosine.shape),
            whole(sine_table.shape),
        ],
        out_specs=[
            tiles((tile, width)),
            tiles((tile, 2 * span)),
            whole((total_rows, span)),
            whole((total_rows, span)),
            tiles((tile, experts * span)),
            tiles((tile, experts)),
        ],
        out_shape=[
            jax.ShapeDtypeStruct((total_rows, width), BF16),
            jax.ShapeDtypeStruct((total_rows, 2 * span), BF16),
            jax.ShapeDtypeStruct((total_rows, span), BF16),
            jax.ShapeDtypeStruct((total_rows, span), BF16),
            jax.ShapeDtypeStruct((total_rows, experts * span), BF16),
            jax.ShapeDtypeStruct((total_rows, experts), F32),
        ],
        compiler_params=pltpu.CompilerParams(vmem_limit_bytes=VMEM_LIMIT),
        cost_estimate=pl.CostEstimate(
            flops=2 * total_rows * width * span * (2 * experts + 2) + 16 * total_rows * total_rows * span,
            bytes_accessed=2 * width * span * (2 * experts + 2) + 8 * total_rows * width,
            transcendentals=2 * total_rows * total_rows * span // HD,
        ),
        name="attend",
    )(order, hidden, *query_w, kv_w, *out_w, router, routes, bounds, place_row, cosine, sine_table)


def attend_back_kernel(experts, steps, order, grad_mid, *refs):
    query_w, refs = refs[:experts], refs[experts:]
    kv_w, refs = refs[0], refs[1:]
    out_w, refs = refs[:experts], refs[experts:]
    routes_ref, gates_ref, bounds_row, place_col, cosine, sine_table, query_ref, keys, values, wide = refs[:10]
    grad_rows, grad_first, gate_sums, key_sum, value_sum = refs[10:]
    step = pl.program_id(0)
    tile = grad_rows.shape[0]
    total_rows, span = keys.shape

    @pl.when(step == 0)
    def _():
        key_sum[...] = jnp.zeros_like(key_sum)
        value_sum[...] = jnp.zeros_like(value_sum)

    @pl.when(step < steps)
    def _():
        here = pl.ds(pl.multiple_of(step * tile, tile), tile)
        routes = routes_ref[here, :]
        gates = gates_ref[here, :]
        hot = [[named_by(routes, order, j, k) for k in range(experts)] for j in range(2)]
        allowed = (place_col[...] >= bounds_row[0:1, here]) & (place_col[...] <= bounds_row[1:2, here])
        rows_in = grad_mid[...]
        slot_grads = [0.0, 0.0]
        sums = []
        for k in range(experts):
            grad = dot(rows_in, out_w[k][...], ((1,), (1,)))
            part = wide[:, k * span : (k + 1) * span].astype(F32)
            sums.append(jnp.sum(part * grad, axis=1, keepdims=True))
            for j in range(2):
                slot_grads[j] = slot_grads[j] + (hot[j][k] * gates[:, k : k + 1]) * grad
        gate_sums[...] = columns(sums)
        cos_here, sin_here = cosine[here, :], sine_table[here, :]
        slot_queries = []
        for j in range(2):
            heads = []
            for h in range(span // HD):
                cols = slice(h * HD, (h + 1) * HD)
                query = query_ref[:, j * span + h * HD : j * span + (h + 1) * HD]
                grad = slot_grads[j][:, cols].astype(BF16)
                scores = dot(keys[:, cols], query, ((1,), (1,))) * HD**-0.5
                scores = jnp.where(allowed, scores, NEG)
                exp_scores = jnp.exp(scores - jnp.max(scores, axis=0, keepdims=True))
                probs = exp_scores * (1.0 / jnp.sum(exp_scores, axis=0, keepdims=True))
                value_sum[:, cols] += dot(probs.astype(BF16), grad)
                grad_probs = dot(values[:, cols], grad, ((1,), (1,)))
                mean = jnp.sum(probs * grad_probs, axis=0, keepdims=True)
                grad_scores = (probs * (grad_probs - mean)).astype(BF16)
                key_sum[:, cols] += dot(grad_scores, query)
                grad_query = dot(grad_scores, keys[:, cols], ((0,), (0,))) * HD**-0.5
                heads.append(turn(grad_query, cos_here, -sin_here))
            slot_queries.append(jnp.concatenate(heads, axis=1) if len(heads) > 1 else heads[0])
        for k in range(experts):
            grad_first[here, k * span : (k + 1) * span] = (
                hot[0][k] * slot_queries[0] + hot[1][k] * slot_queries[1]
            ).astype(BF16)

    @pl.when(step == steps - 1)
    def _():
        for h in range(span // HD):
            cols = slice(h * HD, (h + 1) * HD)
            grad_first[:, experts * span + h * HD : experts * span + (h + 1) * HD] = turn(
                key_sum[:, cols] * HD**-0.5, cosine[...], -sine_table[...]
            ).astype(BF16)
        grad_first[:, (experts + 1) * span :] = value_sum[...].astype(BF16)

    @pl.when(step >= steps)
    def _():
        here = pl.ds(pl.multiple_of((step - steps) * tile, tile), tile)
        total = dot(grad_first[here, experts * span :], kv_w[...], ((1,), (1,)))
        for k in range(experts):
            total = total + dot(
                grad_first[here, k * span : (k + 1) * span], query_w[k][...], ((1,), (1,))
            )
        grad_rows[...] = total.astype(BF16)


def attend_back(
    grad_mid, query_w, kv_w, out_w, routes, order, gates, bounds_row, place_col, cosine, sine_table,
    query, keys, values, wide,
):
    total_rows, width = grad_mid.shape
    experts = len(query_w)
    span = query_w[0].shape[1]
    tile = 256
    steps = total_rows // tile

    def early(shape):
        return pl.BlockSpec(shape, lambda i: (jnp.minimum(i, steps - 1), 0))

    return pl.pallas_call(
        functools.partial(attend_back_kernel, experts, steps),
        grid=(2 * steps,),
        in_specs=[pl.BlockSpec(memory_space=pltpu.SMEM), early((tile, width))]
        + [whole(w.shape) for w in query_w]
        + [whole(kv_w.shape)]
        + [whole(w.shape) for w in out_w]
        + [
            whole(routes.shape),
            whole(gates.shape),
            whole(bounds_row.shape),
            whole(place_col.shape),
            whole(cosine.shape),
            whole(sine_table.shape),
            early((tile, 2 * span)),
            whole(keys.shape),
            whole(values.shape),
            early((tile, experts * span)),
        ],
        out_specs=[
            pl.BlockSpec((tile, width), lambda i: (jnp.maximum(i - steps, 0), 0)),
            whole((total_rows, (experts + 2) * span)),
            early((tile, experts)),
        ],
        out_shape=[
            jax.ShapeDtypeStruct((total_rows, width), BF16),
            jax.ShapeDtypeStruct((total_rows, (experts + 2) * span), BF16),
            jax.ShapeDtypeStruct((total_rows, experts), F32),
        ],
        scratch_shapes=[pltpu.VMEM((total_rows, span), F32), pltpu.VMEM((total_rows, span), F32)],
        compiler_params=pltpu.CompilerParams(vmem_limit_bytes=VMEM_LIMIT),
        cost_estimate=pl.CostEstimate(
            flops=2 * total_rows * width * span * (2 * experts + 2) + 40 * total_rows * total_rows * span,
            bytes_accessed=2 * width * span * (2 * experts + 2) + 8 * total_rows * width,
            transcendentals=2 * total_rows * total_rows * span // HD,
        ),
        name="attend_back",
    )(
        order, grad_mid, *query_w, kv_w, *out_w, routes, gates, bounds_row, place_col, cosine, sine_table,
        query, keys, values, wide,
    )


def split_kernel(block, gate, up):
    half = block.shape[1] // 2
    gate[...] = block[:, :half].T.reshape(gate.shape)
    up[...] = block[:, half:].T.reshape(up.shape)


def split_columns(weight, shards):
    depth, both = weight.shape
    inner = both // (2 * shards)
    tile = 128
    out = jax.ShapeDtypeStruct((shards, inner, depth), BF16)
    spec = pl.BlockSpec((shards, inner, tile), lambda i: (0, 0, i))
    return pl.pallas_call(
        split_kernel,
        grid=(depth // tile,),
        in_specs=[tiles((tile, both))],
        out_specs=[spec, spec],
        out_shape=[out, out],
        compiler_params=pltpu.CompilerParams(vmem_limit_bytes=VMEM_LIMIT),
        cost_estimate=pl.CostEstimate(flops=0, bytes_accessed=4 * depth * both, transcendentals=0),
        name="split_columns",
    )(weight)


def join_kernel(gate, up, out):
    shards, inner, tile = gate.shape
    half = shards * inner
    out[:, :half] = gate[...].reshape(half, tile).T.astype(F32)
    out[:, half:] = up[...].reshape(half, tile).T.astype(F32)


def join_columns(gate, up):
    shards, inner, depth = gate.shape
    tile = 128
    spec = pl.BlockSpec((shards, inner, tile), lambda i: (0, 0, i))
    return pl.pallas_call(
        join_kernel,
        grid=(depth // tile,),
        in_specs=[spec, spec],
        out_specs=tiles((tile, 2 * shards * inner)),
        out_shape=jax.ShapeDtypeStruct((depth, 2 * shards * inner), F32),
        compiler_params=pltpu.CompilerParams(vmem_limit_bytes=VMEM_LIMIT),
        cost_estimate=pl.CostEstimate(
            flops=0, bytes_accessed=12 * shards * depth * inner, transcendentals=0
        ),
        name="join_columns",
    )(gate, up)


def forward_kernel(capacity, hidden, rank, gates, gate_w, up_w, down_w, rows_out, gate_out, up_out, act_out, result):
    blocks, rows = rank.shape[1:]
    slot = lax.broadcasted_iota(jnp.int32, (capacity, rows), 0)
    scales = []
    for b in range(blocks):
        hit = slot == rank[0, b : b + 1, :]
        to, at = slice(b * capacity, (b + 1) * capacity), slice(b * rows, (b + 1) * rows)
        rows_out[to, :] = dot(hit.astype(BF16), hidden[at, :]).astype(BF16)
        scales.append(jnp.sum(jnp.where(hit, gates[0, b : b + 1, :], 0.0), axis=1, keepdims=True))
    scale = jnp.concatenate(scales, axis=0)
    gate = dot(rows_out[...], gate_w[...], ((1,), (1,)))
    up = dot(rows_out[...], up_w[...], ((1,), (1,)))
    act = (gate * jax.nn.sigmoid(gate) * up * scale).astype(BF16)
    gate_out[...] = gate.astype(BF16)
    up_out[...] = up.astype(BF16)
    act_out[...] = act
    result[...] = dot(act, down_w[...]).astype(BF16)


def backward_kernel(
    capacity, cot, rank, gates, gate_ref, up_ref, act, gate_w, up_w, down_w,
    cot_out, grad_gate_out, grad_up_out, grad_rows, gate_sums,
):
    blocks, rows = rank.shape[1:]
    slot = lax.broadcasted_iota(jnp.int32, (capacity, rows), 0)
    scales = []
    for b in range(blocks):
        hit = slot == rank[0, b : b + 1, :]
        to, at = slice(b * capacity, (b + 1) * capacity), slice(b * rows, (b + 1) * rows)
        cot_out[to, :] = dot(hit.astype(BF16), cot[at, :]).astype(BF16)
        scales.append(jnp.sum(jnp.where(hit, gates[0, b : b + 1, :], 0.0), axis=1, keepdims=True))
    scale = jnp.concatenate(scales, axis=0)
    back = dot(cot_out[...], down_w[...], ((1,), (1,)))
    sums = jnp.sum(act[...].astype(F32) * back, axis=1, keepdims=True)
    for b in range(blocks):
        hit = slot == rank[0, b : b + 1, :]
        part = sums[b * capacity : (b + 1) * capacity, :]
        gate_sums[0, b : b + 1, :] = jnp.sum(jnp.where(hit, part, 0.0), axis=0, keepdims=True)
    gate = gate_ref[...].astype(F32)
    sigmoid_gate = jax.nn.sigmoid(gate)
    grad_act = back * scale
    grad_up = (grad_act * gate * sigmoid_gate).astype(BF16)
    grad_gate = (
        grad_act * up_ref[...].astype(F32) * sigmoid_gate * (1.0 + gate * (1.0 - sigmoid_gate))
    ).astype(BF16)
    grad_up_out[...] = grad_up
    grad_gate_out[...] = grad_gate
    grad_rows[...] = (dot(grad_gate, gate_w[...]) + dot(grad_up, up_w[...])).astype(BF16)


def expert_call(kernel, name, products, block_args, part_args, weights, out_cols, sums, rank, gates, capacity):
    shards, rows = rank.shape
    inner, width = weights[0].shape
    blocks = 4
    steps = shards // blocks
    slots = shards * capacity
    part = blocks * capacity
    small = tiles((1, blocks, rows))
    sums_shape = [jax.ShapeDtypeStruct((steps, blocks, rows), F32)] * sums
    return pl.pallas_call(
        functools.partial(kernel, capacity),
        grid=(steps,),
        in_specs=[tiles((blocks * rows, width)) for _ in block_args]
        + [small, small]
        + [tiles((part, item.shape[1])) for item in part_args]
        + [whole(item.shape) for item in weights],
        out_specs=[tiles((part, cols)) for cols in out_cols] + [small] * sums,
        out_shape=[jax.ShapeDtypeStruct((slots, cols), BF16) for cols in out_cols] + sums_shape,
        compiler_params=pltpu.CompilerParams(vmem_limit_bytes=VMEM_LIMIT),
        cost_estimate=pl.CostEstimate(
            flops=2 * products * slots * width * inner,
            bytes_accessed=6 * width * inner + 2 * shards * rows * width + 4 * slots * (width + inner),
            transcendentals=slots * inner,
        ),
        name=name,
    )(
        *block_args, rank.reshape(steps, blocks, rows), gates.reshape(steps, blocks, rows), *part_args, *weights
    )


def combine_kernel(capacity, rank, *refs):
    parts, out = refs[:-1], refs[-1]
    rows = out.shape[0]
    total = 0.0
    slot = lax.broadcasted_iota(jnp.int32, (rows, capacity), 1)
    for k, part in enumerate(parts):
        pick = (slot == rank[:, k : k + 1]).astype(BF16)
        total = total + dot(pick, part[...])
    out[...] = total.astype(BF16)


def combine(rank_cols, parts, rows, capacity):
    total_rows, experts = rank_cols.shape
    width = parts[0].shape[1]
    return pl.pallas_call(
        functools.partial(combine_kernel, capacity),
        grid=(total_rows // rows,),
        in_specs=[tiles((rows, experts))] + [tiles((capacity, width)) for _ in parts],
        out_specs=tiles((rows, width)),
        out_shape=jax.ShapeDtypeStruct((total_rows, width), BF16),
        compiler_params=pltpu.CompilerParams(vmem_limit_bytes=VMEM_LIMIT),
        cost_estimate=pl.CostEstimate(
            flops=2 * total_rows * 256 * experts * width,
            bytes_accessed=2 * total_rows * width + 2 * experts * capacity * total_rows // rows * width,
            transcendentals=0,
        ),
        name="combine",
    )(rank_cols, *parts)


def pair_gates(hidden, router, hot):
    logits = dot(hidden, router)
    picked = jnp.sum(logits[:, None, :] * hot, axis=-1)
    return jax.nn.softmax(picked, axis=-1)


def logit_grads(gates, scaled_grads):
    return scaled_grads - gates * jnp.sum(scaled_grads, axis=-1, keepdims=True)


def exact(left, right):
    return jnp.dot(left, right, precision=lax.Precision.HIGHEST)


def body(
    tokens_in,
    cotangent,
    norm1_gain,
    kv_weight,
    query_weight,
    attn_out_weight,
    attn_router,
    norm2_gain,
    in_weight,
    out_weight,
    mlp_router,
    attn_routes,
    mlp_routes,
    place_order,
    seq_lengths,
):
    experts = lax.axis_size("expert")
    shards = lax.axis_size("shard")
    rows, width = tokens_in.shape
    total_rows = rows * shards
    capacity = -(-5 * rows // (2 * experts) // 16) * 16
    span = query_weight.shape[2] // shards
    inner = out_weight.shape[1]
    depth = in_weight.shape[1]
    order = jnp.stack(expert_order())
    own_expert = order[0]

    chunk = depth // experts
    kv_chunk = lax.dynamic_slice_in_dim(kv_weight, own_expert * chunk, chunk, axis=0)
    kv_chunk = kv_chunk.reshape(chunk, 2, shards, span).transpose(2, 0, 1, 3)
    query_blocks = query_weight[0].reshape(depth, shards, span).transpose(1, 0, 2)
    first_blocks = jnp.concatenate([query_blocks, kv_chunk.reshape(shards, 2 * chunk, span)], axis=1)

    info = jnp.concatenate(
        [place_order, attn_routes.T, mlp_routes.T, jnp.zeros((3, rows), jnp.int32)], axis=0
    )
    info = direct_gather(info)
    info, first_blocks = lax.optimization_barrier((info, first_blocks))
    first_cols = shard_exchange(first_blocks)
    inverse = jnp.argsort(order)
    first_all = expert_gather(first_cols)
    query_w = [item[:, :depth].reshape(width, span) for item in first_all]
    kv_w = jnp.take(jnp.stack([item[:, depth:] for item in first_all]), inverse, axis=0)
    kv_w = kv_w.reshape(experts, shards, chunk, 2 * span).transpose(1, 0, 2, 3).reshape(width, 2 * span)
    attn_out_w = expert_gather(attn_out_weight[0])

    stream = tokens_in.astype(F32)
    normed1, row_scale1 = norm_rows(stream, norm1_gain)
    hidden1_own = normed1.astype(BF16)
    hidden1 = ring_gather(after(hidden1_own, first_blocks), [(), (), (first_cols, attn_out_w[2])])
    lengths = seq_lengths[0]
    places = info[:, 0].reshape(total_rows)
    cosine, sine_table, seq_ids = rope_tables(places, lengths)
    starts = jnp.sum(
        jnp.where(jnp.arange(lengths.shape[0])[None, :] < seq_ids[:, None], lengths[None, :], 0), axis=1
    )
    cosine = jnp.concatenate([cosine, cosine], axis=1)
    sine_table = jnp.concatenate([-sine_table, sine_table], axis=1)
    bounds = jnp.stack([starts, places])

    def routes_of(first):
        return info[:, first : first + 2].transpose(0, 2, 1).reshape(total_rows, 2)

    routes_attn = routes_of(1)
    hot_mlp = (routes_of(3)[:, :, None] == order[None, None, :]).astype(F32)
    attn_router_rel = jnp.take(attn_router, order, axis=1)
    mlp_router_rel = jnp.take(mlp_router, order, axis=1)

    gate_blocks, up_blocks = split_columns(in_weight[0], shards)
    gate_cols = shard_exchange(after(gate_blocks, hidden1)).transpose(1, 0, 2).reshape(inner, width)
    up_cols = shard_exchange(after(up_blocks, gate_cols)).transpose(1, 0, 2).reshape(inner, width)
    gate_weights = expert_gather(gate_cols)
    up_weights = expert_gather(up_cols)
    down_weights = expert_gather(after(out_weight[0], hidden1))

    router_wide = jnp.pad(attn_router_rel, ((0, 0), (0, 128 - experts)))
    mixed, query, keys, values, vec_wide, gates_attn = attend(
        hidden1, query_w, kv_w, attn_out_w, router_wide, routes_attn, order[None], bounds.T,
        places[None], cosine, sine_table,
    )
    middle = stream + ring_scatter(mixed, [(gate_cols, down_weights[2]), (), (), (up_cols,)])

    normed2, row_scale2 = norm_rows(middle, norm2_gain)
    hidden2_own = normed2.astype(BF16)
    hidden2 = ring_gather(hidden2_own, [(gate_weights[2],)])
    cot = ring_gather(after(cotangent, hidden2))
    gates_mlp = pair_gates(hidden2, mlp_router_rel, hot_mlp)
    gates_wide = jnp.sum(hot_mlp * gates_mlp[..., None], axis=1).reshape(shards, rows, experts)
    named = jnp.sum(hot_mlp, axis=1).reshape(shards, rows, experts)
    earlier = (jnp.arange(rows)[:, None] > jnp.arange(rows)[None, :]).astype(BF16)
    rank = jnp.einsum("tu,bue->bte", earlier, named.astype(BF16), preferred_element_type=F32)
    rank = jnp.where(named > 0, rank, -1.0).astype(jnp.int32)
    rank_cols = rank.reshape(total_rows, experts)
    rank_rows = rank.transpose(2, 0, 1)
    gate_rows = gates_wide.transpose(2, 0, 1)

    weights = list(zip(gate_weights, up_weights, down_weights))
    rows_in, gates_low, ups_low, acts, results = zip(
        *[
            expert_call(
                forward_kernel, "expert_forward", 3, [hidden2], [], weights[k],
                [width, inner, inner, inner, width], 0, rank_rows[k], gate_rows[k], capacity,
            )
            for k in range(experts)
        ]
    )
    result_rows = ring_scatter(combine(rank_cols, results, rows, capacity))
    output = (middle + result_rows).astype(BF16)
    backs, gate_w_grads = {}, {}
    cot_now = after(cot, *results)
    for k in range(experts - 1, -1, -1):
        backs[k] = expert_call(
            backward_kernel, "expert_backward", 3, [cot_now], [gates_low[k], ups_low[k], acts[k]],
            weights[k], [width, inner, inner, width], 1, rank_rows[k], gate_rows[k], capacity,
        )
        cot_now = after(cot_now, backs[k][3])
        if k >= 2:
            gate_w_grads[k] = dot(backs[k][1], rows_in[k], ((0,), (0,))).astype(BF16)
            cot_now = after(cot_now, gate_w_grads[k])
    rows_cot, grad_gates, grad_ups, grads, gate_sums = zip(*[backs[k] for k in range(experts)])
    gate_far = far_halves(expert_sums(gate_w_grads, range(2, experts, 2)))
    gate_came = far_exchange(gate_far[0])
    combined = combine(rank_cols, [after(grads[0], *gate_far[0])] + list(grads[1:]), rows, capacity)
    late = after(rows_in[2], combined)
    up_w_grads = {
        k: dot(grad_ups[k], after(rows_in[k], late), ((0,), (0,))).astype(BF16)
        for k in range(experts - 1, 1, -1)
    }
    up_far = far_halves(expert_sums(up_w_grads, range(2, experts, 2)))
    second = far_exchange(after_all(gate_far[1], combined))
    third = far_exchange(after_all(up_far[0], *second))
    back_rows = ring_scatter(combined, [(result_rows, *gate_came), (), (*second, *up_far[0])])
    gate_came = whole_halves(gate_came, second)
    late = after(rows_in[0], *up_far[0])
    for k in (1, 0):
        gate_w_grads[k] = dot(grad_gates[k], after(rows_in[k], late), ((0,), (0,))).astype(BF16)
        up_w_grads[k] = dot(grad_ups[k], after(rows_in[k], late), ((0,), (0,))).astype(BF16)
    down_w_grads = {
        k: dot(acts[k], after(rows_cot[k], late), ((0,), (0,))).astype(BF16)
        for k in range(experts - 1, -1, -1)
    }
    down_far = far_halves(expert_sums(down_w_grads, range(2, experts, 2)))
    gate_sum = (expert_sums(gate_w_grads, [0])[0].astype(F32) + sum_f32(gate_came)).astype(BF16)
    up_near = expert_sums(up_w_grads, [0])[0].astype(F32)
    gate_sums = jnp.stack([item.reshape(shards, rows) for item in gate_sums], axis=1)

    logit_grad_mlp = logit_grads(gates_wide[0], direct_scatter(gate_sums).T)
    grad_hidden2 = back_rows + exact(logit_grad_mlp, mlp_router_rel.astype(F32).T)
    grad_router_mlp = exact(hidden2_own.astype(F32).T, logit_grad_mlp)
    grad_middle, grad_gain2 = norm_back(grad_hidden2, middle, row_scale2, norm2_gain)
    grad_middle = grad_middle + cotangent.astype(F32)

    fourth = far_exchange(after_all(up_far[1], *third))
    fifth = far_exchange(after_all(down_far[0], *fourth))
    grad_mid = ring_gather(grad_middle.astype(BF16), [third, (gate_sum,), fourth])
    up_sum = (up_near + sum_f32(whole_halves(third, fourth))).astype(BF16)
    gate_grad = shard_exchange(gate_sum.reshape(inner, shards, depth).transpose(1, 0, 2))
    grad_mid = after(grad_mid, gate_grad, up_sum, *fifth)
    up_grad = shard_exchange(
        after(up_sum, gate_grad).reshape(inner, shards, depth).transpose(1, 0, 2)
    )
    sixth = far_exchange(after_all(down_far[1], *fifth))
    grad_rows1, grad_first, gate_sums_attn = attend_back(
        grad_mid, query_w, kv_w, attn_out_w, routes_attn, order[None], gates_attn, bounds,
        places[:, None], cosine, sine_table, query, keys, values, vec_wide,
    )
    back_rows1 = ring_scatter(grad_rows1, [sixth, (up_grad,)])
    down_came = whole_halves(fifth, sixth)
    gate_sums_attn = direct_scatter(
        gate_sums_attn.reshape(shards, rows, experts).transpose(0, 2, 1)
    ).T
    grad_first_w = dot(hidden1, grad_first, ((0,), (0,))).astype(BF16)
    grad_second_w = dot(vec_wide, grad_mid, ((0,), (0,))).astype(BF16)

    logit_grad_attn = logit_grads(gates_attn[:rows], gate_sums_attn)
    grad_router_attn = exact(hidden1_own.astype(F32).T, logit_grad_attn)
    grad_hidden1 = back_rows1 + exact(logit_grad_attn, attn_router_rel.astype(F32).T)
    grad_stream, _ = norm_back(grad_hidden1, stream, row_scale1, norm1_gain)
    grad_gain1 = jnp.sum(grad_rows1.astype(F32) * hidden1.astype(F32), axis=0) / norm1_gain
    grad_gain1 = grad_gain1 + jnp.sum(
        exact(logit_grad_attn, attn_router_rel.astype(F32).T) * stream * row_scale1, axis=0
    )
    grad_input = grad_stream + grad_middle

    in_grad = join_columns(gate_grad, up_grad)[None]
    out_grad = (expert_sums(down_w_grads, [0])[0].astype(F32) + sum_f32(down_came))[None]
    attn_grad = expert_reduce(jnp.split(grad_second_w, experts, axis=0))[None]
    kv_grad = grad_first_w[:, experts * span :].reshape(shards, experts, chunk, 2 * span)
    kv_grad = jnp.take(kv_grad, order, axis=1).reshape(shards, experts, 2 * chunk, span)
    first_grad = expert_reduce(
        [
            jnp.concatenate(
                [
                    grad_first_w[:, k * span : (k + 1) * span].reshape(shards, depth, span),
                    kv_grad[:, k],
                ],
                axis=1,
            )
            for k in range(experts)
        ]
    )
    first_grad = shard_exchange(first_grad.astype(BF16))
    query_grad = first_grad[:, :depth].transpose(1, 0, 2).reshape(1, depth, shards * span).astype(F32)
    kv_grad = first_grad[:, depth:].reshape(shards, chunk, 2, span)
    kv_grad = kv_grad.transpose(1, 2, 0, 3).reshape(chunk, 2 * shards * span)
    kv_grad = jnp.take(jnp.stack(expert_gather(kv_grad)), inverse, axis=0)
    kv_grad = kv_grad.reshape(depth, 2 * shards * span).astype(F32)

    mlp_small = sum_all(
        jnp.concatenate([grad_gain2[None], jnp.take(grad_router_mlp.T, inverse, axis=0)], axis=0)
    )
    attn_small = sum_all(
        jnp.concatenate([grad_gain1[None], jnp.take(grad_router_attn.T, inverse, axis=0)], axis=0)
    )
    return (
        output,
        grad_input,
        attn_small[0],
        kv_grad,
        query_grad,
        attn_grad,
        attn_small[1:].T,
        mlp_small[0],
        in_grad,
        out_grad,
        mlp_small[1:].T,
    )


def solution(mesh):
    return jax.shard_map(
        body,
        mesh=mesh,
        in_specs=(
            P(("expert", "shard"), None),
            P(("expert", "shard"), None),
            P(),
            P("shard", None),
            P("expert", "shard", None),
            P("expert", "shard", None),
            P(),
            P(),
            P("expert", "shard", None),
            P("expert", "shard", None),
            P(),
            P(("expert", "shard"), None),
            P(("expert", "shard"), None),
            P("expert", "shard"),
            P("expert", None),
        ),
        out_specs=(
            P(("expert", "shard"), None),
            P(("expert", "shard"), None),
            P(),
            P("shard", None),
            P("expert", "shard", None),
            P("expert", "shard", None),
            P(),
            P(),
            P("expert", "shard", None),
            P("expert", "shard", None),
            P(),
        ),
        check_vma=False,
    )
```

```python
import functools

import jax
import jax.numpy as jnp
from jax import lax
from jax.experimental import pallas as pl
from jax.experimental.pallas import tpu as pltpu
from jax.sharding import PartitionSpec as P

HD = 128


EPS = 1e-05
THETA = 10000.0
NEG = -1e30
F32 = jnp.float32
BF16 = jnp.bfloat16
VMEM_LIMIT = 60 * 1024 * 1024


def dot(left, right, contract=((1,), (0,))):
    return lax.dot_general(left, right, (contract, ((), ())), preferred_element_type=F32)


def norm_rows(values, norm_gain):
    row_scale = lax.rsqrt(jnp.mean(values * values, axis=-1, keepdims=True) + EPS)
    return (values * row_scale * norm_gain, row_scale)


def norm_back(grad_rows, values, row_scale, norm_gain):
    gain_grad = jnp.sum(grad_rows * values * row_scale, axis=0)
    scaled_grad = grad_rows * norm_gain
    mean_term = jnp.mean(scaled_grad * values, axis=-1, keepdims=True)
    return (
        row_scale * scaled_grad - values * row_scale * row_scale * row_scale * mean_term,
        gain_grad,
    )


def seq_of(places, lengths):
    seq_ends = jnp.cumsum(lengths)
    passed = seq_ends[None, :] <= places[:, None]
    return (passed, jnp.sum(passed.astype(jnp.int32), axis=1))


def rope_tables(places, lengths):
    passed, seq_ids = seq_of(places, lengths)
    starts = jnp.sum(jnp.where(passed, lengths[None, :], 0), axis=1)
    where_in = (places - starts).astype(F32)
    frequency = THETA ** (-jnp.arange(0, HD // 2, dtype=F32) * (2.0 / HD))
    angles = where_in[:, None] * frequency[None, :]
    return (jnp.cos(angles), jnp.sin(angles), seq_ids)


def rotate(values, cosine, sine_table):
    half_width = values.shape[-1] // 2
    leading = values[..., :half_width]
    trailing = values[..., half_width:]
    return jnp.concatenate(
        [leading * cosine - trailing * sine_table, trailing * cosine + leading * sine_table],
        axis=-1,
    )


def ring_cycle(count):
    if count == 8:
        return [0, 2, 4, 6, 7, 5, 3, 1]
    if count == 16:
        return [0, 1, 2, 3, 7, 6, 5, 9, 10, 11, 15, 14, 13, 12, 8, 4]
    return list(range(count))


def ring_move(value, hops):
    cycle = ring_cycle(lax.axis_size("shard"))
    count = len(cycle)
    return lax.ppermute(
        value, "shard", [(cycle[i], cycle[(i + hops) % count]) for i in range(count)]
    )


def after(value, *others):
    return lax.optimization_barrier((value,) + others)[0] if others else value


class Transfer:
    def __init__(self, move, source, value=None):
        self.move, self.source, self.value = move, source, value

    def begin(self):
        self.value = self.move(self.value)


def tie(values, others):
    if len(values) + len(others) < 2:
        return list(values)
    held = [item.value if isinstance(item, Transfer) else item for item in others]
    tied = lax.optimization_barrier((*values, *held))
    for item, value in zip(others, tied[len(values) :]):
        if isinstance(item, Transfer):
            item.value = value
    return list(tied[: len(values)])


def begin(values, transfers):
    for item in transfers:
        item.value = item.source()
    values = tie(values, transfers)
    for item in transfers:
        item.begin()
    return values


class RingGather:
    def __init__(self, block):
        self.ahead, self.behind = [block], [block]
        self.last = []

    def tie(self, values, begins=(), ends=()):
        heads = self.last or [self.ahead[-1], self.behind[-1]]
        for item in begins:
            item.value = item.source()
        tied = tie([*heads, *values], [*begins, *ends])
        if self.last:
            self.last = tied[:2]
        else:
            self.ahead[-1], self.behind[-1] = tied[:2]
        for item in begins:
            item.begin()
        return tied[2:]

    def step(self):
        far = lax.axis_size("shard") // 2
        if len(self.ahead) < far:
            self.ahead.append(ring_move(self.ahead[-1], 1))
            self.behind.append(ring_move(self.behind[-1], -1))
        elif not self.last:
            cut = self.ahead[0].shape[0] // 2
            self.last = [ring_move(self.ahead[-1][:cut], 1), ring_move(self.behind[-1][cut:], -1)]

    def blocks(self):
        while not self.last:
            self.step()
        return self.ahead + self.last + self.behind[:0:-1]


class RingScatter:
    def __init__(self, partial):
        count = lax.axis_size("shard")
        rows = partial.shape[0] // count
        self.far, self.done = count // 2, 0
        self.part = [partial[r * rows : (r + 1) * rows] for r in range(count)]
        cut = rows // 2
        self.back, self.fore = self.part[self.far][:cut], self.part[self.far][cut:]

    def tie(self, values, begins=(), ends=()):
        for item in begins:
            item.value = item.source()
        tied = tie([self.back, self.fore, *values], [*begins, *ends])
        self.back, self.fore = tied[:2]
        for item in begins:
            item.begin()
        return tied[2:]

    def step(self):
        if self.done == self.far:
            return
        self.back, self.fore = ring_move(self.back, -1), ring_move(self.fore, 1)
        if self.done == 0:
            empty = jnp.zeros_like(self.back)
            self.back = jnp.concatenate([self.back, empty], axis=0)
            self.fore = jnp.concatenate([empty, self.fore], axis=0)
        if self.done < self.far - 1:
            self.back = self.part[self.far - 1 - self.done] + self.back
            self.fore = self.part[self.far + 1 + self.done] + self.fore
        self.done += 1

    def total(self):
        while self.done < self.far:
            self.step()
        return self.part[0].astype(F32) + self.back.astype(F32) + self.fore.astype(F32)


def ring_gather(block, plan={}):
    ring = RingGather(block)
    for step in range(lax.axis_size("shard") // 2):
        begins, ends = plan.get(step, ((), ()))
        ring.tie([], begins)
        ring.step()
        ring.tie([], (), ends)
    return ring.blocks()


def ring_scatter(partial, plan={}):
    ring = RingScatter(partial)
    for step in range(lax.axis_size("shard") // 2):
        begins, ends = plan.get(step, ((), ()))
        ring.tie([], begins)
        ring.step()
        ring.tie([], (), ends)
    return ring.total()


def direct_gather(block):
    count = lax.axis_size("shard")
    return jnp.stack([block] + [ring_move(block, r) for r in range(1, count)])


def core_swap(value):
    return lax.ppermute(value, "expert", [(i, i ^ 1) for i in range(lax.axis_size("expert"))])


def chip_shift(value, hops):
    count = lax.axis_size("expert")
    chips = count // 2
    return lax.ppermute(
        value, "expert", [(i, (i // 2 + hops) % chips * 2 + i % 2) for i in range(count)]
    )


def expert_order():
    index = lax.axis_index("expert")
    chips = lax.axis_size("expert") // 2
    return [
        (index // 2 + dx) % chips * 2 + (index % 2 + dc) % 2
        for dx in range(chips)
        for dc in range(2)
    ]


def expert_gather(value):
    chips = lax.axis_size("expert") // 2
    own = [value] + [chip_shift(value, -dx) for dx in range(1, chips)]
    return [piece for item in own for piece in (item, core_swap(item))]


def after_all(values, *others):
    return [after(item, *others) for item in values]


PARTS = 4


def part_of(value, which, parts=PARTS):
    size = value.shape[1 if value.ndim == 2 else 0] // parts
    here = slice(which * size, (which + 1) * size)
    return value[:, here] if value.ndim == 2 else value[here]


def fetch_far(source, which=0, parts=1):
    chips = lax.axis_size("expert") // 2
    take = lambda: part_of(source(), which, parts)
    return [Transfer(lambda v, dx=dx: chip_shift(v, -dx), take) for dx in range(1, chips)]


def hand_far(source, which=0, parts=1):
    chips = lax.axis_size("expert") // 2
    return [
        Transfer(
            lambda v, dx=dx: chip_shift(v, dx), lambda dx=dx: part_of(source()[dx - 1], which, parts)
        )
        for dx in range(1, chips)
    ]


def total_of(near, parts):
    came = [sum_f32([item.value for item in part]) for part in parts]
    return near + jnp.concatenate(came, axis=1)


def with_swaps(items):
    return [piece for item in items for piece in (item, core_swap(item))]


def expert_sums(pieces, firsts):
    return [
        (pieces[k].astype(F32) + core_swap(pieces[k + 1]).astype(F32)).astype(BF16) for k in firsts
    ]


def far_exchange(sums):
    return [chip_shift(item, dx + 1) for dx, item in enumerate(sums)]


def sum_f32(parts):
    return sum(item.astype(F32) for item in parts)


def expert_reduce(pieces):
    sums = expert_sums(pieces, range(0, len(pieces), 2))
    return sum_f32(sums[:1] + far_exchange(sums[1:]))


def shard_exchange(pieces):
    return lax.all_to_all(pieces, "shard", split_axis=0, concat_axis=0, tiled=True)


def sum_pairs(value, axis, step):
    count = lax.axis_size(axis)
    return value + lax.ppermute(value, axis, [(i, i ^ step) for i in range(count)])


def powers(count):
    return [1 << i for i in range(count.bit_length() - 1)]


def turn(values, cosine, sine_table):
    return values * cosine + pltpu.roll(values, HD // 2, 1) * sine_table


def whole(shape):
    zeros = (0,) * len(shape)
    return pl.BlockSpec(shape, lambda *_: zeros, pipeline_mode=pl.Buffered(1))


def tiles(shape):
    return pl.BlockSpec(shape, lambda i: (i,) + (0,) * (len(shape) - 1))


def named_by(routes, order, slot, k):
    return (routes[:, slot : slot + 1] == order[0, k]).astype(F32)


def columns(parts):
    lane = lax.broadcasted_iota(jnp.int32, (parts[0].shape[0], len(parts)), 1)
    total = jnp.zeros(lane.shape, F32)
    for k, part in enumerate(parts):
        total = jnp.where(lane == k, part, total)
    return total


def lay(blocks, target):
    start = 0
    for block in blocks:
        target[start : start + block.shape[0], :] = block[...]
        start += block.shape[0]


def cost(microseconds):
    return pl.CostEstimate(flops=microseconds * 115 * 10**6, bytes_accessed=1 << 16, transcendentals=0)


def attend_kernel(layout, count, chunk, order, *refs):
    blocks, refs = refs[:count], refs[count:]
    (first_w,), refs = regroup(refs, [layout])
    experts = len(layout)
    out_w, refs = refs[:experts], refs[experts:]
    router, routes_ref, bounds, place_row, cosine, sine_table = refs[:6]
    mixed, query_out, keys, values, wide, gates_out, hidden, kv_w = refs[6:]
    step = pl.program_id(0)
    tile = mixed.shape[0]
    total_rows, span = keys.shape
    width = hidden.shape[1]
    shards = sum(piece.shape[0] for piece in first_w[0])
    depth = width // shards

    @pl.when(step == 0)
    def _():
        lay(blocks, hidden)
        for k in range(experts):
            for s, block in enumerate([piece.at[i] for piece in first_w[k] for i in range(piece.shape[0])]):
                to = pl.ds(pl.multiple_of(s * depth + order[0, k] * chunk, chunk), chunk)
                for half in range(2):
                    kv_w[half, to, :] = block[depth + half * chunk : depth + (half + 1) * chunk, :]

        @pl.loop(0, total_rows // tile)
        def _(i):
            here = pl.ds(pl.multiple_of(i * tile, tile), tile)
            raw = dot(hidden[here, :], kv_w[0])
            for h in range(span // HD):
                cols = slice(h * HD, (h + 1) * HD)
                keys[here, cols] = turn(raw[:, cols], cosine[here, :], sine_table[here, :]).astype(BF16)
            values[here, :] = dot(hidden[here, :], kv_w[1]).astype(BF16)

    here = pl.ds(pl.multiple_of(step * tile, tile), tile)
    rows_in = hidden[here, :]
    routes = routes_ref[...]
    hot = [[named_by(routes, order, j, k) for k in range(experts)] for j in range(2)]
    logits = dot(rows_in, router[...])
    picked = [sum(hot[j][k] * logits[:, k : k + 1] for k in range(experts)) for j in range(2)]
    top = jnp.maximum(picked[0], picked[1])
    raised = [jnp.exp(value - top) for value in picked]
    gates = [value / (raised[0] + raised[1]) for value in raised]
    gates_out[...] = columns([hot[0][k] * gates[0] + hot[1][k] * gates[1] for k in range(experts)])
    query_all = []
    for pieces in first_w:
        at, total = 0, 0.0
        for piece in pieces:
            size = piece.shape[0] * depth
            total = total + dot(rows_in[:, at : at + size], piece[:, :depth, :].reshape(size, span))
            at += size
        query_all.append(total)
    allowed = (place_row[...] >= bounds[:, 0:1]) & (place_row[...] <= bounds[:, 1:2])
    cos_here, sin_here = cosine[here, :], sine_table[here, :]
    vectors = []
    for j in range(2):
        raw = sum(hot[j][k] * query_all[k] for k in range(experts))
        heads = []
        for h in range(span // HD):
            cols = slice(h * HD, (h + 1) * HD)
            query = turn(raw[:, cols], cos_here, sin_here).astype(BF16)
            query_out[:, j * span + h * HD : j * span + (h + 1) * HD] = query
            scores = dot(query, keys[:, cols], ((1,), (1,))) * HD**-0.5
            scores = jnp.where(allowed, scores, NEG)
            row_top = jnp.max(scores, axis=1, keepdims=True)
            exp_scores = jnp.exp(scores - row_top)
            row_total = jnp.sum(exp_scores, axis=1, keepdims=True)
            heads.append(dot(exp_scores.astype(BF16), values[:, cols]) / row_total)
        vectors.append((jnp.concatenate(heads, axis=1) if len(heads) > 1 else heads[0]) * gates[j])
    total = 0.0
    for k in range(experts):
        part = (hot[0][k] * vectors[0] + hot[1][k] * vectors[1]).astype(BF16)
        wide[:, k * span : (k + 1) * span] = part
        total = total + dot(part, out_w[k][...])
    mixed[...] = total.astype(BF16)


def attend(blocks, first_w, out_w, router, routes, order, bounds, place_row, cosine, sine_table, chunk):
    total_rows, width = routes.shape[0], blocks[0].shape[1]
    experts = len(first_w)
    span = first_w[0][0].shape[2]
    layout = [len(pieces) for pieces in first_w]
    first_w = [piece for pieces in first_w for piece in pieces]
    tile = 256

    def struct(*shape):
        return jax.ShapeDtypeStruct(shape, BF16)

    return pl.pallas_call(
        functools.partial(attend_kernel, layout, len(blocks), chunk),
        grid=(total_rows // tile,),
        in_specs=[pl.BlockSpec(memory_space=pltpu.SMEM)]
        + [whole(w.shape) for w in [*blocks, *first_w, *out_w, router]]
        + [
            tiles((tile, 2)),
            tiles((tile, 2)),
            whole(place_row.shape),
            whole(cosine.shape),
            whole(sine_table.shape),
        ],
        out_specs=[
            tiles((tile, width)),
            tiles((tile, 2 * span)),
            whole((total_rows, span)),
            whole((total_rows, span)),
            tiles((tile, experts * span)),
            tiles((tile, experts)),
            whole((total_rows, width)),
            whole((2, width, span)),
        ],
        out_shape=[
            struct(total_rows, width),
            struct(total_rows, 2 * span),
            struct(total_rows, span),
            struct(total_rows, span),
            struct(total_rows, experts * span),
            jax.ShapeDtypeStruct((total_rows, experts), F32),
            struct(total_rows, width),
            struct(2, width, span),
        ],
        compiler_params=pltpu.CompilerParams(vmem_limit_bytes=VMEM_LIMIT),
        cost_estimate=cost(35),
        name="attend",
    )(order, *blocks, *first_w, *out_w, router, routes, bounds, place_row, cosine, sine_table)


def attend_back_kernel(layout, steps, count, order, *refs):
    blocks, refs = refs[:count], refs[count:]
    (first_w,), refs = regroup(refs, [layout])
    experts = len(layout)
    kv_w, refs = refs[0], refs[1:]
    out_w, refs = refs[:experts], refs[experts:]
    router, hidden, refs = refs[0], refs[1], refs[2:]
    routes_ref, gates_ref, bounds_row, place_col, cosine, sine_table, query_ref, keys, values, wide = refs[:10]
    grad_rows, grad_first, small, grad_mid, key_sum, value_sum, logit_grads = refs[10:]
    step = pl.program_id(0)
    tile = grad_rows.shape[0]
    total_rows, span = keys.shape

    @pl.when(step == 0)
    def _():
        lay(blocks, grad_mid)
        small[...] = jnp.zeros_like(small)
        key_sum[...] = jnp.zeros_like(key_sum)
        value_sum[...] = jnp.zeros_like(value_sum)

    @pl.when(step < steps)
    def _():
        here = pl.ds(pl.multiple_of(step * tile, tile), tile)
        routes = routes_ref[here, :]
        gates = gates_ref[here, :]
        hot = [[named_by(routes, order, j, k) for k in range(experts)] for j in range(2)]
        allowed = (place_col[...] >= bounds_row[0:1, here]) & (place_col[...] <= bounds_row[1:2, here])
        rows_in = grad_mid[here, :]
        slot_grads = [0.0, 0.0]
        sums = []
        for k in range(experts):
            grad = dot(rows_in, out_w[k][...], ((1,), (1,)))
            part = wide[:, k * span : (k + 1) * span].astype(F32)
            sums.append(jnp.sum(part * grad, axis=1, keepdims=True))
            for j in range(2):
                slot_grads[j] = slot_grads[j] + (hot[j][k] * gates[:, k : k + 1]) * grad
        sums = columns(sums)
        wide_grads = sums - gates * jnp.sum(sums, axis=1, keepdims=True)
        wide_grads = jnp.concatenate([wide_grads, jnp.zeros((tile, HD - experts), F32)], axis=1)
        logit_grads[here, :] = wide_grads.astype(BF16)
        cos_here, sin_here = cosine[here, :], sine_table[here, :]
        slot_queries = []
        for j in range(2):
            heads = []
            for h in range(span // HD):
                cols = slice(h * HD, (h + 1) * HD)
                query = query_ref[:, j * span + h * HD : j * span + (h + 1) * HD]
                grad = slot_grads[j][:, cols].astype(BF16)
                scores = dot(keys[:, cols], query, ((1,), (1,))) * HD**-0.5
                scores = jnp.where(allowed, scores, NEG)
                exp_scores = jnp.exp(scores - jnp.max(scores, axis=0, keepdims=True))
                probs = exp_scores * (1.0 / jnp.sum(exp_scores, axis=0, keepdims=True))
                value_sum[:, cols] += dot(probs.astype(BF16), grad)
                grad_probs = dot(values[:, cols], grad, ((1,), (1,)))
                mean = jnp.sum(probs * grad_probs, axis=0, keepdims=True)
                grad_scores = (probs * (grad_probs - mean)).astype(BF16)
                key_sum[:, cols] += dot(grad_scores, query)
                grad_query = dot(grad_scores, keys[:, cols], ((0,), (0,))) * HD**-0.5
                heads.append(turn(grad_query, cos_here, -sin_here))
            slot_queries.append(jnp.concatenate(heads, axis=1) if len(heads) > 1 else heads[0])
        for k in range(experts):
            grad_first[here, k * span : (k + 1) * span] = (
                hot[0][k] * slot_queries[0] + hot[1][k] * slot_queries[1]
            ).astype(BF16)

    @pl.when(step == steps - 1)
    def _():
        for h in range(span // HD):
            cols = slice(h * HD, (h + 1) * HD)
            grad_first[:, experts * span + h * HD : experts * span + (h + 1) * HD] = turn(
                key_sum[:, cols] * HD**-0.5, cosine[...], -sine_table[...]
            ).astype(BF16)
        grad_first[:, (experts + 1) * span :] = value_sum[...].astype(BF16)

    @pl.when(step >= steps)
    def _():
        here = pl.ds(pl.multiple_of((step - steps) * tile, tile), tile)
        total = dot(grad_first[here, experts * span : (experts + 1) * span], kv_w[0], ((1,), (1,)))
        total = total + dot(grad_first[here, (experts + 1) * span :], kv_w[1], ((1,), (1,)))
        total = total + dot(logit_grads[here, :], router[...], ((1,), (1,)))
        width = total.shape[1]
        depth = width // sum(piece.shape[0] for piece in first_w[0])
        for k, pieces in enumerate(first_w):
            grad = grad_first[here, k * span : (k + 1) * span]
            back = [
                dot(grad, piece[:, :depth, :].reshape(piece.shape[0] * depth, span), ((1,), (1,)))
                for piece in pieces
            ]
            total = total + (jnp.concatenate(back, axis=1) if len(back) > 1 else back[0])
        grad_rows[...] = total.astype(BF16)
        rows_in = hidden[...]
        small[:-8, :] += dot(logit_grads[here, :], rows_in, ((0,), (0,)))[: small.shape[0] - 8, :]
        small[-8:, :] += jnp.sum((total * rows_in.astype(F32)).reshape(-1, 8, total.shape[1]), axis=0)


def attend_back(
    blocks, first_w, kv_w, out_w, router, hidden, routes, order, gates, bounds_row, place_col, cosine,
    sine_table, query, keys, values, wide,
):
    small_rows = -(-len(first_w) // 8) * 8 + 8
    total_rows, width = routes.shape[0], blocks[0].shape[1]
    experts = len(first_w)
    span = first_w[0][0].shape[2]
    layout = [len(pieces) for pieces in first_w]
    first_w = [piece for pieces in first_w for piece in pieces]
    tile = 256 if total_rows <= 1024 else 128
    steps = total_rows // tile

    def early(shape):
        return pl.BlockSpec(shape, lambda i: (jnp.minimum(i, steps - 1), 0))

    return pl.pallas_call(
        functools.partial(attend_back_kernel, layout, steps, len(blocks)),
        grid=(2 * steps,),
        in_specs=[pl.BlockSpec(memory_space=pltpu.SMEM)]
        + [whole(w.shape) for w in [*blocks, *first_w, kv_w, *out_w, router]]
        + [pl.BlockSpec((tile, width), lambda i: (jnp.maximum(i - steps, 0), 0))]
        + [
            whole(routes.shape),
            whole(gates.shape),
            whole(bounds_row.shape),
            whole(place_col.shape),
            whole(cosine.shape),
            whole(sine_table.shape),
            early((tile, 2 * span)),
            whole(keys.shape),
            whole(values.shape),
            early((tile, experts * span)),
        ],
        out_specs=[
            pl.BlockSpec((tile, width), lambda i: (jnp.maximum(i - steps, 0), 0)),
            whole((total_rows, (experts + 2) * span)),
            whole((small_rows, width)),
            whole((total_rows, width)),
        ],
        out_shape=[
            jax.ShapeDtypeStruct((total_rows, width), BF16),
            jax.ShapeDtypeStruct((total_rows, (experts + 2) * span), BF16),
            jax.ShapeDtypeStruct((small_rows, width), F32),
            jax.ShapeDtypeStruct((total_rows, width), BF16),
        ],
        scratch_shapes=[
            pltpu.VMEM((total_rows, span), F32),
            pltpu.VMEM((total_rows, span), F32),
            pltpu.VMEM((total_rows, HD), BF16),
        ],
        compiler_params=pltpu.CompilerParams(vmem_limit_bytes=VMEM_LIMIT),
        cost_estimate=cost(45),
        name="attend_back",
    )(
        order, *blocks, *first_w, kv_w, *out_w, router, hidden, routes, gates, bounds_row, place_col, cosine,
        sine_table, query, keys, values, wide,
    )


def split_kernel(block, gate, up):
    half = block.shape[1] // 2
    gate[...] = block[:, :half].T.reshape(gate.shape)
    up[...] = block[:, half:].T.reshape(up.shape)


def split_columns(weight, shards):
    depth, both = weight.shape
    inner = both // (2 * shards)
    tile = 128
    out = jax.ShapeDtypeStruct((shards, inner, depth), BF16)
    spec = pl.BlockSpec((shards, inner, tile), lambda i: (0, 0, i))
    return pl.pallas_call(
        split_kernel,
        grid=(depth // tile,),
        in_specs=[tiles((tile, both))],
        out_specs=[spec, spec],
        out_shape=[out, out],
        compiler_params=pltpu.CompilerParams(vmem_limit_bytes=VMEM_LIMIT),
        cost_estimate=cost(5),
        name="split_columns",
    )(weight)


def join_kernel(gate, up, out):
    shards, inner, tile = gate.shape
    half = shards * inner
    out[:, :half] = gate[...].reshape(half, tile).T.astype(F32)
    out[:, half:] = up[...].reshape(half, tile).T.astype(F32)


def join_columns(gate, up):
    shards, inner, depth = gate.shape
    tile = 128
    spec = pl.BlockSpec((shards, inner, tile), lambda i: (0, 0, i))
    return pl.pallas_call(
        join_kernel,
        grid=(depth // tile,),
        in_specs=[spec, spec],
        out_specs=tiles((tile, 2 * shards * inner)),
        out_shape=jax.ShapeDtypeStruct((depth, 2 * shards * inner), F32),
        compiler_params=pltpu.CompilerParams(vmem_limit_bytes=VMEM_LIMIT),
        cost_estimate=cost(7),
        name="join_columns",
    )(gate, up)


def dispatch_kernel(capacity, count, gated, rank, *refs):
    blocks, refs = refs[:count], refs[count:]
    if gated:
        router, out, gates_out, hidden = refs
    else:
        out, hidden = refs
    step = pl.program_id(0)
    _, experts, rows = rank.shape

    @pl.when(step == 0)
    def _():
        lay(blocks, hidden)

    rows_in = hidden[pl.ds(pl.multiple_of(step * rows, rows), rows), :]
    ranks = rank[0]
    slot = lax.broadcasted_iota(jnp.int32, (capacity, rows), 0)
    pick = jnp.concatenate([(slot == ranks[k : k + 1, :]).astype(BF16) for k in range(experts)], axis=0)
    picked = dot(pick, rows_in).astype(BF16)
    for k in range(experts):
        out[k] = picked[k * capacity : (k + 1) * capacity, :]
    if gated:
        logits = dot(router[...], rows_in, ((1,), (1,)))[:experts, :]
        logits = jnp.where(ranks >= 0, logits, NEG)
        raised = jnp.where(ranks >= 0, jnp.exp(logits - jnp.max(logits, axis=0, keepdims=True)), 0.0)
        gates_out[0] = raised / jnp.sum(raised, axis=0, keepdims=True)


def dispatch(blocks, rank, capacity, router=None):
    shards, experts, rows = rank.shape
    width = blocks[0].shape[1]
    out_specs = [pl.BlockSpec((experts, capacity, width), lambda i: (0, i, 0))]
    out_shape = [jax.ShapeDtypeStruct((experts, shards * capacity, width), BF16)]
    extra = []
    if router is not None:
        extra = [router]
        out_specs += [tiles((1, experts, rows)), whole((shards * rows, width))]
        out_shape += [
            jax.ShapeDtypeStruct((shards, experts, rows), F32),
            jax.ShapeDtypeStruct((shards * rows, width), BF16),
        ]
    return pl.pallas_call(
        functools.partial(dispatch_kernel, capacity, len(blocks), router is not None),
        grid=(shards,),
        in_specs=[tiles((1, experts, rows))] + [whole(item.shape) for item in [*blocks, *extra]],
        out_specs=out_specs,
        out_shape=out_shape,
        scratch_shapes=[] if router is not None else [pltpu.VMEM((shards * rows, width), BF16)],
        compiler_params=pltpu.CompilerParams(vmem_limit_bytes=VMEM_LIMIT),
        cost_estimate=cost(10),
        name="dispatch",
    )(rank, *blocks, *extra)


def fetch(step, count, weights, store, sems):
    def copies(index):
        made = []
        for i, pieces in enumerate(weights[index]):
            at = 0
            for piece in pieces:
                parts = [piece] if len(piece.shape) == 2 else [piece.at[s] for s in range(piece.shape[0])]
                for part in parts:
                    span = part.shape[1]
                    target = store.at[index % 2, i, :, at : at + span]
                    made.append(pltpu.make_async_copy(part, target, sems.at[index % 2, len(made)]))
                    at += span
        return made

    for index in range(count):

        @pl.when(step == index)
        def _():
            if index == 0:
                for copy in copies(0):
                    copy.start()
            if index + 1 < count:
                for copy in copies(index + 1):
                    copy.start()
            for copy in copies(index):
                copy.wait()


def regroup(refs, layout):
    groups, at = [], 0
    for expert in layout:
        groups.append([])
        for pieces in expert:
            groups[-1].append(refs[at : at + pieces])
            at += pieces
    return groups, refs[at:]


def row_scale(capacity, rank, gates):
    blocks, rows = rank.shape
    slot = lax.broadcasted_iota(jnp.int32, (capacity, rows), 0)
    return jnp.concatenate(
        [
            jnp.sum(jnp.where(slot == rank[b : b + 1, :], gates[b : b + 1, :], 0.0), axis=1, keepdims=True)
            for b in range(blocks)
        ],
        axis=0,
    )


def forward_kernel(capacity, layout, rank, gates, rows_in, *refs):
    weights, refs = regroup(refs, layout)
    count = len(layout)
    gate_out, up_out, act_out, result, store, sems = refs
    step = pl.program_id(0)
    fetch(step, count, weights, store, sems)
    gate_w, up_w, down_w = [store.at[step % 2, i] for i in range(3)]
    scale = row_scale(capacity, rank[0], gates[0])
    slots = rows_in.shape[1]
    part = slots // 2
    for at in range(0, slots, part):
        here = slice(at, at + part)
        data = rows_in[0, here, :]
        gate = dot(data, gate_w[...], ((1,), (1,)))
        up = dot(data, up_w[...], ((1,), (1,)))
        act = (gate * jax.nn.sigmoid(gate) * up * scale[here, :]).astype(BF16)
        gate_out[0, here, :] = gate.astype(BF16)
        up_out[0, here, :] = up.astype(BF16)
        act_out[0, here, :] = act
        result[0, here, :] = dot(act, down_w[...]).astype(BF16)


def backward_kernel(capacity, layout, rank, gates, cot, gate_ref, up_ref, act, *refs):
    weights, refs = regroup(refs, layout)
    count = len(layout)
    grad_gate_out, grad_up_out, grad_rows, gate_sums, store, sems = refs
    step = pl.program_id(0)
    fetch(step, count, weights, store, sems)
    gate_w, up_w, down_w = [store.at[step % 2, i] for i in range(3)]
    scale = row_scale(capacity, rank[0], gates[0])
    slots = cot.shape[1]
    part = slots // 2
    blocks, rows = rank.shape[1:]
    slot = lax.broadcasted_iota(jnp.int32, (capacity, rows), 0)
    for at in range(0, slots, part):
        here = slice(at, at + part)
        back = dot(cot[0, here, :], down_w[...], ((1,), (1,)))
        sums = jnp.sum(act[0, here, :].astype(F32) * back, axis=1, keepdims=True)
        for b in range(at // capacity, (at + part) // capacity):
            hit = slot == rank[0, b : b + 1, :]
            piece = sums[b * capacity - at : (b + 1) * capacity - at, :]
            gate_sums[0, b : b + 1, :] = jnp.sum(jnp.where(hit, piece, 0.0), axis=0, keepdims=True)
        gate = gate_ref[0, here, :].astype(F32)
        sigmoid_gate = jax.nn.sigmoid(gate)
        grad_act = back * scale[here, :]
        grad_up = (grad_act * gate * sigmoid_gate).astype(BF16)
        grad_gate = (
            grad_act * up_ref[0, here, :].astype(F32) * sigmoid_gate * (1.0 + gate * (1.0 - sigmoid_gate))
        ).astype(BF16)
        grad_up_out[0, here, :] = grad_up
        grad_gate_out[0, here, :] = grad_gate
        grad_rows[0, here, :] = (dot(grad_gate, gate_w[...]) + dot(grad_up, up_w[...])).astype(BF16)


def expert_call(
    kernel, name, first, rows_in, parts, weights, out_cols, sums, rank, gates, capacity, skip=0
):
    _, shards, rows = rank.shape
    width, inner = rows_in.shape[2], weights[0][0][0].shape[-2]
    count = len(weights)
    slots = shards * capacity
    layout = [[len(pieces) for pieces in group] for group in weights]
    flat = [piece for group in weights for pieces in group for piece in pieces]
    copies = 2 * shards + PARTS

    def of_all(shape):
        return pl.BlockSpec((1,) + shape, lambda i: (first + i, 0, 0))

    def of_these(shape):
        return pl.BlockSpec((1,) + shape, lambda i: (i, 0, 0))

    def of_parts(shape):
        return pl.BlockSpec((1,) + shape, lambda i: (skip + i, 0, 0))

    return pl.pallas_call(
        functools.partial(kernel, capacity, layout),
        grid=(count,),
        in_specs=[of_all((shards, rows)), of_all((shards, rows)), of_all((slots, width))]
        + [of_parts((slots, inner)) for _ in parts]
        + [pl.BlockSpec(memory_space=pl.ANY)] * len(flat),
        out_specs=[of_these((slots, cols)) for cols in out_cols] + [of_these((shards, rows))] * sums,
        out_shape=[jax.ShapeDtypeStruct((count, slots, cols), BF16) for cols in out_cols]
        + [jax.ShapeDtypeStruct((count, shards, rows), F32)] * sums,
        scratch_shapes=[pltpu.VMEM((2, 3, inner, width), BF16), pltpu.SemaphoreType.DMA((2, copies))],
        compiler_params=pltpu.CompilerParams(vmem_limit_bytes=VMEM_LIMIT),
        cost_estimate=cost(10 * count),
        name=name,
    )(rank, gates, rows_in, *parts, *flat)


def combine_kernel(capacity, extra, rank, *refs):
    rows, experts = rank.shape
    if extra:
        sums, gates, router, hidden, refs = refs[0], refs[1], refs[2], refs[3], refs[4:]
        *parts, out, small = refs
    else:
        *parts, out = refs
    slot = lax.broadcasted_iota(jnp.int32, (rows, experts * capacity), 1)
    pick = jnp.zeros(slot.shape, F32)
    for k in range(experts):
        at = jnp.where(rank[:, k : k + 1] >= 0, rank[:, k : k + 1] + k * capacity, -1)
        pick = pick + (slot == at).astype(F32)
    data = jnp.concatenate([part[i] for part in parts for i in range(part.shape[0])], axis=0)
    total = dot(pick.astype(BF16), data)
    if extra:
        grads = sums[0] - gates[0] * jnp.sum(sums[0], axis=0, keepdims=True)
        pad = router.shape[0] - experts
        grads = jnp.concatenate([grads, jnp.zeros((pad, rows), F32)], axis=0).astype(BF16)
        total = total + dot(grads, router[...], ((0,), (0,)))

        @pl.when(pl.program_id(0) == 0)
        def _():
            small[...] = jnp.zeros_like(small)

        small[...] += dot(grads, hidden[...])
    out[...] = total.astype(BF16)


def combine(rank_cols, parts, rows, capacity, extra=()):
    total_rows, experts = rank_cols.shape
    width = parts[0].shape[2]
    out_specs = [tiles((rows, width))]
    out_shape = [jax.ShapeDtypeStruct((total_rows, width), BF16)]
    in_specs = [tiles((rows, experts))]
    if extra:
        router = extra[2]
        in_specs += [
            tiles((1, experts, rows)), tiles((1, experts, rows)), whole(router.shape), tiles((rows, width)),
        ]
        out_specs.append(whole(router.shape))
        out_shape.append(jax.ShapeDtypeStruct(router.shape, F32))
    return pl.pallas_call(
        functools.partial(combine_kernel, capacity, bool(extra)),
        grid=(total_rows // rows,),
        in_specs=in_specs
        + [pl.BlockSpec((part.shape[0], capacity, width), lambda i: (0, i, 0)) for part in parts],
        out_specs=out_specs,
        out_shape=out_shape,
        compiler_params=pltpu.CompilerParams(vmem_limit_bytes=VMEM_LIMIT),
        cost_estimate=cost(10),
        name="combine",
    )(rank_cols, *extra, *parts)


def body(
    tokens_in,
    cotangent,
    norm1_gain,
    kv_weight,
    query_weight,
    attn_out_weight,
    attn_router,
    norm2_gain,
    in_weight,
    out_weight,
    mlp_router,
    attn_routes,
    mlp_routes,
    place_order,
    seq_lengths,
):
    experts = lax.axis_size("expert")
    shards = lax.axis_size("shard")
    rows, width = tokens_in.shape
    total_rows = rows * shards
    chips = experts // 2
    capacity = -(-5 * rows // (2 * experts) // 16) * 16
    span = query_weight.shape[2] // shards
    inner = out_weight.shape[1]
    depth = in_weight.shape[1]
    order = jnp.stack(expert_order())
    own_expert = order[0]

    chunk = depth // experts
    kv_chunk = lax.dynamic_slice_in_dim(kv_weight, own_expert * chunk, chunk, axis=0)
    kv_chunk = kv_chunk.reshape(chunk, 2, shards, span).transpose(2, 1, 0, 3)
    query_blocks = query_weight[0].reshape(depth, shards, span).transpose(1, 0, 2)
    first_blocks = jnp.concatenate([query_blocks, kv_chunk.reshape(shards, 2 * chunk, span)], axis=1)

    info = jnp.concatenate(
        [place_order, attn_routes.T, mlp_routes.T, jnp.zeros((3, rows), jnp.int32)], axis=0
    )
    info = Transfer(direct_gather, lambda info=info: info)
    inverse = jnp.argsort(order)

    stream = tokens_in.astype(F32)
    normed1, row_scale1 = norm_rows(stream, norm1_gain)
    hidden1_own = normed1.astype(BF16)
    first = Transfer(shard_exchange, lambda: first_blocks)
    out_far = fetch_far(lambda: attn_out_weight[0])
    first_far = [fetch_far(lambda: first.value, i, 2) for i in range(2)]
    (hidden1_own,) = begin([hidden1_own], [first])
    gate_blocks, up_blocks = split_columns(in_weight[0], shards)
    down_far = [fetch_far(lambda: out_weight[0], i, PARTS) for i in range(PARTS)]
    ring = RingGather(hidden1_own)
    ring.tie([], out_far + [info])
    ring.step()
    ring.tie([], (), [first, gate_blocks, info] + out_far)
    ring.tie([], first_far[0])
    ring.step()
    ring.tie([], (), first_far[0])
    ring.tie([], first_far[1])
    ring.step()
    info = info.value
    lengths = seq_lengths[0]
    places = info[:, 0].reshape(total_rows)
    cosine, sine_table, seq_ids = rope_tables(places, lengths)
    starts = jnp.sum(
        jnp.where(jnp.arange(lengths.shape[0])[None, :] < seq_ids[:, None], lengths[None, :], 0), axis=1
    )
    cosine = jnp.concatenate([cosine, cosine], axis=1)
    sine_table = jnp.concatenate([-sine_table, sine_table], axis=1)
    bounds = jnp.stack([starts, places])

    def routes_of(first):
        return info[:, first : first + 2].transpose(0, 2, 1).reshape(total_rows, 2)

    routes_attn = routes_of(1)
    named = jnp.any(info[:, 3:5, None, :] == order[None, None, :, None], axis=1)
    earlier = (jnp.arange(rows)[:, None] < jnp.arange(rows)[None, :]).astype(BF16)
    rank = jnp.einsum("bku,ut->bkt", named.astype(BF16), earlier, preferred_element_type=F32)
    rank = jnp.where(named, rank, -1.0).astype(jnp.int32)
    rank_cols = rank.transpose(0, 2, 1).reshape(total_rows, experts)
    rank_rows = rank.transpose(1, 0, 2)
    attn_router_rel = jnp.take(attn_router, order, axis=1)
    mlp_router_rel = jnp.take(mlp_router, order, axis=1)

    router_wide = jnp.pad(attn_router_rel, ((0, 0), (0, 128 - experts)))
    tables = [cosine, sine_table, bounds, routes_attn, rank, router_wide]
    ring.tie([], (), tables + first_far[1])
    ring.step()
    ring.tie([])
    hidden1_blocks = ring.blocks()
    gate_own = Transfer(shard_exchange, lambda: gate_blocks)
    hidden1_blocks = begin(hidden1_blocks, [gate_own])
    hidden1_blocks = begin(hidden1_blocks, down_far[1] + down_far[2])
    first_all = []
    for pieces in [[first.value]] + [[a.value, b.value] for a, b in zip(*first_far)]:
        first_all += [pieces, [core_swap(piece) for piece in pieces]]
    attn_out_w = with_swaps([attn_out_weight[0]] + [item.value for item in out_far])
    up_own = Transfer(shard_exchange, lambda: up_blocks)
    gate_far = [fetch_far(lambda: gate_own.value, i, PARTS) for i in range(PARTS)]
    up_far = [fetch_far(lambda: up_own.value, i, PARTS) for i in range(PARTS)]

    def first_parts(grad):
        key_grad, value_grad = [
            grad[:, (experts + i) * span : (experts + i + 1) * span].reshape(shards, experts, chunk, span)
            for i in range(2)
        ]
        parts = []
        for k in range(experts):
            query_grad = grad[:, k * span : (k + 1) * span].reshape(shards, depth, span)
            own = [
                lax.dynamic_index_in_dim(item, order[k], axis=1, keepdims=False)
                for item in (key_grad, value_grad)
            ]
            parts.append(jnp.concatenate([query_grad, *own], axis=1))
        return expert_sums(parts, range(0, experts, 2))

    mixed, query, keys, values, vec_wide, gates_attn, hidden1, kv_w = attend(
        hidden1_blocks, first_all, attn_out_w, router_wide, routes_attn, order[None], bounds.T,
        places[None], cosine, sine_table, chunk,
    )
    (mixed,) = tie([mixed], [gate_own] + down_far[1] + down_far[2])
    middle = stream + ring_scatter(
        mixed,
        {
            0: ([up_own] + down_far[3] + gate_far[0] + gate_far[1], down_far[3] + gate_far[0] + gate_far[1]),
            1: (gate_far[2] + gate_far[3], gate_far[2] + gate_far[3]),
            2: (down_far[0], [up_own] + down_far[0]),
            3: (up_far[0], up_far[0]),
        },
    )

    normed2, row_scale2 = norm_rows(middle, norm2_gain)
    hidden2_own = normed2.astype(BF16)
    cot_steps = RingGather(cotangent)
    ring = RingGather(hidden2_own)
    for part in up_far[1:]:
        ring.tie([], part)
        ring.step()
        ring.tie([], (), part)
    ring.step()
    cot_steps.ahead[0], *ring.last = tie([cotangent, *ring.last], [])
    cot_steps.behind[0] = cot_steps.ahead[0]
    hidden2_blocks = ring.blocks()
    cot_steps.step()
    router_rows = jnp.pad(mlp_router_rel.T, ((0, 16 - experts), (0, 0)))
    rows_in, gates_mlp, hidden2 = dispatch(hidden2_blocks, rank, capacity, router_rows)
    gate_rows = gates_mlp.transpose(1, 0, 2)
    down_own = Transfer(None, None, out_weight[0])
    halves = []
    forwards = []
    rows_now = rows_in
    for first in range(0, experts, 2):
        (rows_now,) = cot_steps.tie([rows_now])
        cot_steps.step()
        at = first // 2 - 1
        these = [
            [[own.value]] if first == 0 else [[part[at].value for part in far]]
            for own, far in ((gate_own, gate_far), (up_own, up_far), (down_own, down_far))
        ]
        these = [(near[0], [core_swap(piece) for piece in near[0]]) for near in these]
        these = list(zip(*these))
        halves.append((first, these))
        forwards.append(
            list(
                expert_call(
                forward_kernel, "expert_forward", first, rows_now, [], these,
                [inner, inner, inner, width], 0, rank_rows, gate_rows, capacity,
                )
            )
        )
        (forwards[-1][3],) = cot_steps.tie([forwards[-1][3]])
        rows_now = after(rows_now, forwards[-1][3])
    gates_low, ups_low, acts, results = zip(*forwards)
    cot_steps.step()
    combined = combine(rank_cols, results, rows, capacity)[0]
    (combined,) = cot_steps.tie([combined])
    cot_blocks = cot_steps.blocks()
    cot_blocks[0] = after(cot_blocks[0], combined)
    result_steps = RingScatter(combined)
    result_steps.step()
    rows_cot = dispatch(cot_blocks, rank, capacity)[0]
    rows_cot = dispatch(cot_blocks, rank, capacity)[0]
    backs, gate_w_grads = {}, {}
    cot_now = rows_cot
    calls = halves[:0:-1] + [(1, halves[0][1][1:]), (0, halves[0][1][:1])]
    for first, these in calls:
        at = first // 2
        (cot_now,) = result_steps.tie([cot_now], gate_hand[1 - first] if first < 2 else ())
        result_steps.step()
        back = [*expert_call(
            backward_kernel, "expert_backward", first, cot_now, [gates_low[at], ups_low[at], acts[at]],
            these, [inner, inner, width], 1, rank_rows, gate_rows, capacity, first % 2,
        )]
        (back[2],) = result_steps.tie([back[2]], (), gate_hand[1 - first] if first < 2 else ())
        cot_now = after(cot_now, back[2])
        for k in range(len(these)):
            backs[first + k] = [back[0][k], back[1][k], back[2], back[3]]
        if first >= 2:
            for k in (first + 1, first):
                gate_w_grads[k] = dot(backs[k][0], rows_in[k], ((0,), (0,))).astype(BF16)
                cot_now = after(cot_now, gate_w_grads[k])
            gate_sums_far = expert_sums(gate_w_grads, range(2, experts, 2)) if first == 2 else None
            gate_hand = [hand_far(lambda: gate_sums_far, i, PARTS) for i in range(PARTS)]
    grad_gates, grad_ups = [[backs[k][i] for k in range(experts)] for i in range(2)]
    groups = [0, 1] + list(range(2, experts, 2))
    grads, gate_sums = [[backs[k][i] for k in groups] for i in (2, 3)]
    acts = [item[i] for item in acts for i in range(2)]
    gate_sums = jnp.concatenate(gate_sums, axis=0).transpose(1, 0, 2)
    grads = begin(grads[:1], gate_hand[2]) + grads[1:]
    combined, mlp_part = combine(
        rank_cols, grads, rows, capacity, (gate_sums, gates_mlp, router_rows, hidden2)
    )
    result_rows = result_steps.total()
    output = (middle + result_rows).astype(BF16)
    up_w_grads, down_w_grads = {}, {}

    def weight_grad(into, left, right, k, late):
        into[k] = dot(after(left[k], late), right[k], ((0,), (0,))).astype(BF16)
        return into[k]

    gate_back = Transfer(
        lambda v: shard_exchange(v.reshape(inner, shards, depth).transpose(1, 0, 2)),
        lambda: gate_total,
    )
    up_back = Transfer(shard_exchange, lambda: up_total)
    ring = RingScatter(combined)
    (late,) = ring.tie([after(rank, result_rows)], (), gate_hand[2])
    (late,) = ring.tie([late], gate_hand[3])
    for k in range(experts - 1, 3, -1):
        weight_grad(up_w_grads, grad_ups, rows_in, k, late)
    ring.step()
    weight_grad(up_w_grads, grad_ups, rows_in, 3, late)
    (late,) = ring.tie([late], (), [up_w_grads[3]] + gate_hand[3])
    ring.step()
    weight_grad(up_w_grads, grad_ups, rows_in, 2, late)
    (late,) = ring.tie([late], (), [up_w_grads[2]])
    ring.step()
    up_sums_far = expert_sums(up_w_grads, range(2, experts, 2))
    up_hand = [hand_far(lambda: up_sums_far, i, PARTS) for i in range(PARTS)]
    weight_grad(gate_w_grads, grad_gates, rows_in, 1, late)
    (late,) = ring.tie([late], (), [gate_w_grads[1], *up_sums_far])
    ring.step()
    weight_grad(gate_w_grads, grad_gates, rows_in, 0, late)
    gate_near = expert_sums(gate_w_grads, [0])[0].astype(F32)
    (late,) = ring.tie([late], (), [gate_w_grads[0]])
    back_rows = ring.total()
    grad_hidden2 = back_rows
    grad_middle, grad_gain2 = norm_back(grad_hidden2, middle, row_scale2, norm2_gain)
    grad_middle = grad_middle + cotangent.astype(F32)

    gate_total = total_of(gate_near, gate_hand).astype(BF16)
    gate_total = total_of(gate_near, gate_hand).astype(BF16)
    ring = RingGather(grad_middle.astype(BF16))
    (late,) = ring.tie([late], [gate_back] + up_hand[0] + up_hand[1])
    ring.step()
    weight_grad(up_w_grads, grad_ups, rows_in, 1, late)
    (late,) = ring.tie([late], (), [up_w_grads[1]] + up_hand[0] + up_hand[1])
    (late,) = ring.tie([late], up_hand[2] + up_hand[3])
    ring.step()
    weight_grad(up_w_grads, grad_ups, rows_in, 0, late)
    up_near = expert_sums(up_w_grads, [0])[0].astype(F32)
    for k in range(experts - 1, 1, -1):
        weight_grad(down_w_grads, acts, rows_cot, k, late)
    down_sums_far = expert_sums(down_w_grads, range(2, experts, 2))
    down_hand = [hand_far(lambda: down_sums_far, i, PARTS) for i in range(PARTS)]
    (late,) = ring.tie([late], (), [up_w_grads[0], *down_sums_far, gate_back] + up_hand[2] + up_hand[3])
    (late,) = ring.tie([late], down_hand[0])
    ring.step()
    up_total = total_of(up_near, up_hand).astype(BF16)
    up_total = up_total.reshape(inner, shards, depth).transpose(1, 0, 2)
    for k in (1, 0):
        weight_grad(down_w_grads, acts, rows_cot, k, late)
    (late,) = ring.tie([late], (), [up_total] + down_hand[0])
    ring.step()
    (late,) = ring.tie([late], (), [down_w_grads[0], down_w_grads[1]])
    mid_blocks = ring.blocks()
    mid_blocks = begin(mid_blocks, [up_back] + down_hand[1] + down_hand[2] + down_hand[3])
    grad_rows1, grad_first, attn_part, grad_mid = attend_back(
        mid_blocks, first_all, kv_w, attn_out_w, router_wide, hidden1, routes_attn, order[None], gates_attn, bounds,
        places[:, None], cosine, sine_table, query, keys, values, vec_wide,
    )
    grad_rows1, grad_first, attn_part, late = tie(
        [grad_rows1, grad_first, attn_part, late], down_hand[1] + down_hand[2] + down_hand[3]
    )
    grad_first_w = dot(hidden1, grad_first, ((0,), (0,))).astype(BF16)
    sums = jnp.concatenate(
        [
            jnp.sum(attn_part[-8:], axis=0, keepdims=True) / norm1_gain,
            grad_gain2[None],
            jnp.take(attn_part, inverse, axis=0),
            jnp.take(mlp_part, inverse, axis=0),
        ],
        axis=0,
    )
    rounds = [("expert", step) for step in powers(experts)] + [("shard", step) for step in powers(shards)]
    small = []
    for i, (axis, step) in enumerate(rounds):
        source = (lambda: sums) if i == 0 else (lambda i=i: small[i - 1].value)
        small.append(Transfer(lambda v, axis=axis, step=step: sum_pairs(v, axis, step), source))
    (late,) = begin([late], small[:1])
    grad_rows1, late = tie([grad_rows1, late], [up_back, grad_first_w] + small[:1])
    first_sums = first_parts(grad_first_w)
    first_hand = [hand_far(lambda: first_sums[1:], i, 2) for i in range(2)]
    ring = RingScatter(grad_rows1)
    (late,) = ring.tie([late], small[1:2])
    ring.step()
    (late,) = ring.tie([late], (), first_sums + small[1:2])
    (late,) = ring.tie([late], first_hand[0] + small[2:3])
    ring.step()
    (late,) = ring.tie([late], (), first_hand[0] + small[2:3])
    (late,) = ring.tie([late], first_hand[1] + small[3:4])
    ring.step()
    grad_second_w = dot(after(vec_wide, late), grad_mid, ((0,), (0,))).astype(BF16)
    (late,) = ring.tie([late], (), first_hand[1] + small[3:4] + [grad_second_w])
    came = [jnp.concatenate([a.value, b.value], axis=0) for a, b in zip(*first_hand)]
    first_grad = sum_f32(first_sums[:1] + came).astype(BF16)
    first_back = Transfer(shard_exchange, lambda: first_grad)
    second_sums = expert_sums(jnp.split(grad_second_w, experts, axis=0), range(0, experts, 2))
    second_hand = hand_far(lambda: second_sums[1:])
    (late,) = ring.tie([late], [first_back])
    ring.step()
    (late,) = begin([late], second_hand)
    for item in small[4:]:
        (late,) = tie(begin([late], [item]), [item])
    back_rows1 = ring.total()
    late = after(late, back_rows1)
    in_grad = join_columns(after(gate_back.value, late), up_back.value)[None]
    attn_grad = sum_f32(second_sums[:1] + [item.value for item in second_hand])[None]
    out_grad = total_of(after(expert_sums(down_w_grads, [0])[0], late).astype(F32), down_hand)[None]
    first_grad = first_back.value
    sums = small[-1].value
    grad_hidden1 = back_rows1
    grad_stream, _ = norm_back(grad_hidden1, stream, row_scale1, norm1_gain)
    grad_input = grad_stream + grad_middle

    query_grad = first_grad[:, :depth].transpose(1, 0, 2).reshape(1, depth, shards * span).astype(F32)
    kv_grad = first_grad[:, depth:].reshape(shards, 2, chunk, span)
    kv_grad = kv_grad.transpose(2, 1, 0, 3).reshape(chunk, 2 * shards * span)
    pieces = expert_gather(kv_grad.astype(BF16))
    kv_grad = jnp.zeros((depth, 2 * shards * span), F32)
    for k, piece in enumerate(pieces):
        kv_grad = lax.dynamic_update_slice_in_dim(kv_grad, piece.astype(F32), order[k] * chunk, axis=0)

    return (
        output,
        grad_input,
        sums[0],
        kv_grad,
        query_grad,
        attn_grad,
        sums[2 : 2 + experts].T,
        sums[1],
        in_grad,
        out_grad,
        sums[2 + experts :].T,
    )


def solution(mesh):
    return jax.shard_map(
        body,
        mesh=mesh,
        in_specs=(
            P(("expert", "shard"), None),
            P(("expert", "shard"), None),
            P(),
            P("shard", None),
            P("expert", "shard", None),
            P("expert", "shard", None),
            P(),
            P(),
            P("expert", "shard", None),
            P("expert", "shard", None),
            P(),
            P(("expert", "shard"), None),
            P(("expert", "shard"), None),
            P("expert", "shard"),
            P("expert", None),
        ),
        out_specs=(
            P(("expert", "shard"), None),
            P(("expert", "shard"), None),
            P(),
            P("shard", None),
            P("expert", "shard", None),
            P("expert", "shard", None),
            P(),
            P(),
            P("expert", "shard", None),
            P("expert", "shard", None),
            P(),
        ),
        check_vma=False,
    )
```

```python
import functools

import jax
import jax.numpy as jnp
from jax import lax
from jax.experimental import pallas as pl
from jax.experimental.pallas import tpu as pltpu
from jax.sharding import PartitionSpec as P

HD = 128


EPS = 1e-05
THETA = 10000.0
NEG = -1e30
F32 = jnp.float32
BF16 = jnp.bfloat16
VMEM_LIMIT = 60 * 1024 * 1024


def dot(left, right, contract=((1,), (0,))):
    return lax.dot_general(left, right, (contract, ((), ())), preferred_element_type=F32)


def norm_rows(values, norm_gain):
    row_scale = lax.rsqrt(jnp.mean(values * values, axis=-1, keepdims=True) + EPS)
    return (values * row_scale * norm_gain, row_scale)


def norm_back(grad_rows, values, row_scale, norm_gain):
    gain_grad = jnp.sum(grad_rows * values * row_scale, axis=0)
    scaled_grad = grad_rows * norm_gain
    mean_term = jnp.mean(scaled_grad * values, axis=-1, keepdims=True)
    return (
        row_scale * scaled_grad - values * row_scale * row_scale * row_scale * mean_term,
        gain_grad,
    )


def seq_of(places, lengths):
    seq_ends = jnp.cumsum(lengths)
    passed = seq_ends[None, :] <= places[:, None]
    return (passed, jnp.sum(passed.astype(jnp.int32), axis=1))


def rope_tables(places, lengths):
    passed, seq_ids = seq_of(places, lengths)
    starts = jnp.sum(jnp.where(passed, lengths[None, :], 0), axis=1)
    where_in = (places - starts).astype(F32)
    frequency = THETA ** (-jnp.arange(0, HD // 2, dtype=F32) * (2.0 / HD))
    angles = where_in[:, None] * frequency[None, :]
    return (jnp.cos(angles), jnp.sin(angles), seq_ids)


def rotate(values, cosine, sine_table):
    half_width = values.shape[-1] // 2
    leading = values[..., :half_width]
    trailing = values[..., half_width:]
    return jnp.concatenate(
        [leading * cosine - trailing * sine_table, trailing * cosine + leading * sine_table],
        axis=-1,
    )


def ring_cycle(count):
    if count == 8:
        return [0, 2, 4, 6, 7, 5, 3, 1]
    if count == 16:
        return [0, 1, 2, 3, 7, 6, 5, 9, 10, 11, 15, 14, 13, 12, 8, 4]
    return list(range(count))


def ring_move(value, hops):
    cycle = ring_cycle(lax.axis_size("shard"))
    count = len(cycle)
    return lax.ppermute(
        value, "shard", [(cycle[i], cycle[(i + hops) % count]) for i in range(count)]
    )


def after(value, *others):
    return lax.optimization_barrier((value,) + others)[0] if others else value


class Transfer:
    def __init__(self, move, source, value=None):
        self.move, self.source, self.value = move, source, value

    def begin(self):
        self.value = self.move(self.value)


def tie(values, others):
    if len(values) + len(others) < 2:
        return list(values)
    held = [item.value if isinstance(item, Transfer) else item for item in others]
    tied = lax.optimization_barrier((*values, *held))
    for item, value in zip(others, tied[len(values) :]):
        if isinstance(item, Transfer):
            item.value = value
    return list(tied[: len(values)])


def begin(values, transfers):
    for item in transfers:
        item.value = item.source()
    values = tie(values, transfers)
    for item in transfers:
        item.begin()
    return values


class RingGather:
    def __init__(self, block):
        self.ahead, self.behind = [block], [block]
        self.last = []

    def tie(self, values, begins=(), ends=()):
        heads = self.last or [self.ahead[-1], self.behind[-1]]
        for item in begins:
            item.value = item.source()
        tied = tie([*heads, *values], [*begins, *ends])
        if self.last:
            self.last = tied[:2]
        else:
            self.ahead[-1], self.behind[-1] = tied[:2]
        for item in begins:
            item.begin()
        return tied[2:]

    def step(self):
        far = lax.axis_size("shard") // 2
        if len(self.ahead) < far:
            self.ahead.append(ring_move(self.ahead[-1], 1))
            self.behind.append(ring_move(self.behind[-1], -1))
        elif not self.last:
            cut = self.ahead[0].shape[0] // 2
            self.last = [ring_move(self.ahead[-1][:cut], 1), ring_move(self.behind[-1][cut:], -1)]

    def blocks(self):
        while not self.last:
            self.step()
        return self.ahead + self.last + self.behind[:0:-1]


class RingScatter:
    def __init__(self, partial):
        count = lax.axis_size("shard")
        rows = partial.shape[0] // count
        self.far, self.done = count // 2, 0
        self.part = [partial[r * rows : (r + 1) * rows] for r in range(count)]
        cut = rows // 2
        self.back, self.fore = self.part[self.far][:cut], self.part[self.far][cut:]

    def tie(self, values, begins=(), ends=()):
        for item in begins:
            item.value = item.source()
        tied = tie([self.back, self.fore, *values], [*begins, *ends])
        self.back, self.fore = tied[:2]
        for item in begins:
            item.begin()
        return tied[2:]

    def step(self):
        if self.done == self.far:
            return
        self.back, self.fore = ring_move(self.back, -1), ring_move(self.fore, 1)
        if self.done == 0:
            empty = jnp.zeros_like(self.back)
            self.back = jnp.concatenate([self.back, empty], axis=0)
            self.fore = jnp.concatenate([empty, self.fore], axis=0)
        if self.done < self.far - 1:
            self.back = self.part[self.far - 1 - self.done] + self.back
            self.fore = self.part[self.far + 1 + self.done] + self.fore
        self.done += 1

    def total(self):
        while self.done < self.far:
            self.step()
        return self.part[0].astype(F32) + self.back.astype(F32) + self.fore.astype(F32)


def ring_gather(block, plan={}):
    ring = RingGather(block)
    for step in range(lax.axis_size("shard") // 2):
        begins, ends = plan.get(step, ((), ()))
        ring.tie([], begins)
        ring.step()
        ring.tie([], (), ends)
    return ring.blocks()


def ring_scatter(partial, plan={}):
    ring = RingScatter(partial)
    for step in range(lax.axis_size("shard") // 2):
        begins, ends = plan.get(step, ((), ()))
        ring.tie([], begins)
        ring.step()
        ring.tie([], (), ends)
    return ring.total()


def doubled(value, step):
    count = lax.axis_size("shard")
    return jnp.concatenate([value, lax.ppermute(value, "shard", [(i, i ^ step) for i in range(count)])])


def ring_sorted(blocks):
    cycle = ring_cycle(lax.axis_size("shard"))
    own = lax.axis_index("shard")
    spot = jnp.array([cycle.index(s) for s in range(len(cycle))])[own]
    return jnp.take(blocks, own ^ jnp.array(cycle)[(spot - jnp.arange(len(cycle))) % len(cycle)], axis=0)


def core_swap(value):
    return lax.ppermute(value, "expert", [(i, i ^ 1) for i in range(lax.axis_size("expert"))])


def chip_shift(value, hops):
    count = lax.axis_size("expert")
    chips = count // 2
    return lax.ppermute(
        value, "expert", [(i, (i // 2 + hops) % chips * 2 + i % 2) for i in range(count)]
    )


def expert_order():
    index = lax.axis_index("expert")
    chips = lax.axis_size("expert") // 2
    return [
        (index // 2 + dx) % chips * 2 + (index % 2 + dc) % 2
        for dx in range(chips)
        for dc in range(2)
    ]


def expert_gather(value):
    chips = lax.axis_size("expert") // 2
    own = [value] + [chip_shift(value, -dx) for dx in range(1, chips)]
    return [piece for item in own for piece in (item, core_swap(item))]


def after_all(values, *others):
    return [after(item, *others) for item in values]


PARTS = 4


def part_of(value, which, parts=PARTS):
    size = value.shape[1 if value.ndim == 2 else 0] // parts
    here = slice(which * size, (which + 1) * size)
    return value[:, here] if value.ndim == 2 else value[here]


def fetch_far(source, which=0, parts=1):
    chips = lax.axis_size("expert") // 2
    take = lambda: part_of(source(), which, parts)
    return [Transfer(lambda v, dx=dx: chip_shift(v, -dx), take) for dx in range(1, chips)]


def hand_far(source, which=0, parts=1):
    chips = lax.axis_size("expert") // 2
    return [
        Transfer(
            lambda v, dx=dx: chip_shift(v, dx), lambda dx=dx: part_of(source()[dx - 1], which, parts)
        )
        for dx in range(1, chips)
    ]


def total_of(near, parts):
    came = [sum_f32([item.value for item in part]) for part in parts]
    return near + jnp.concatenate(came, axis=1)


def with_swaps(items):
    return [piece for item in items for piece in (item, core_swap(item))]


def expert_sums(pieces, firsts):
    return [
        (pieces[k].astype(F32) + core_swap(pieces[k + 1]).astype(F32)).astype(BF16) for k in firsts
    ]


def far_exchange(sums):
    return [chip_shift(item, dx + 1) for dx, item in enumerate(sums)]


def sum_f32(parts):
    return sum(item.astype(F32) for item in parts)


def expert_reduce(pieces):
    sums = expert_sums(pieces, range(0, len(pieces), 2))
    return sum_f32(sums[:1] + far_exchange(sums[1:]))


def shard_exchange(pieces):
    return lax.all_to_all(pieces, "shard", split_axis=0, concat_axis=0, tiled=True)


def sum_pairs(value, axis, step):
    count = lax.axis_size(axis)
    return value + lax.ppermute(value, axis, [(i, i ^ step) for i in range(count)])


def powers(count):
    return [1 << i for i in range(count.bit_length() - 1)]


def turn(values, cosine, sine_table):
    return values * cosine + pltpu.roll(values, HD // 2, 1) * sine_table


def whole(shape):
    zeros = (0,) * len(shape)
    return pl.BlockSpec(shape, lambda *_: zeros, pipeline_mode=pl.Buffered(1))


def tiles(shape):
    return pl.BlockSpec(shape, lambda i: (i,) + (0,) * (len(shape) - 1))


def named_by(routes, order, slot, k):
    return (routes[:, slot : slot + 1] == order[0, k]).astype(F32)


def columns(parts):
    lane = lax.broadcasted_iota(jnp.int32, (parts[0].shape[0], len(parts)), 1)
    total = jnp.zeros(lane.shape, F32)
    for k, part in enumerate(parts):
        total = jnp.where(lane == k, part, total)
    return total


def lay(blocks, target):
    start = 0
    for block in blocks:
        target[start : start + block.shape[0], :] = block[...]
        start += block.shape[0]


def cost(microseconds):
    return pl.CostEstimate(flops=microseconds * 115 * 10**6, bytes_accessed=1 << 16, transcendentals=0)


def attend_kernel(layout, count, chunk, order, *refs):
    blocks, refs = refs[:count], refs[count:]
    (first_w,), refs = regroup(refs, [layout])
    experts = len(layout)
    out_w, refs = refs[:experts], refs[experts:]
    router, routes_ref, bounds, place_row, cosine, sine_table = refs[:6]
    mixed, query_out, keys, values, wide, gates_out, hidden, kv_w = refs[6:]
    step = pl.program_id(0)
    tile = mixed.shape[0]
    total_rows, span = keys.shape
    width = hidden.shape[1]
    shards = sum(piece.shape[0] for piece in first_w[0])
    depth = width // shards

    @pl.when(step == 0)
    def _():
        lay(blocks, hidden)
        for k in range(experts):
            for s, block in enumerate([piece.at[i] for piece in first_w[k] for i in range(piece.shape[0])]):
                to = pl.ds(pl.multiple_of(s * depth + order[0, k] * chunk, chunk), chunk)
                for half in range(2):
                    kv_w[half, to, :] = block[depth + half * chunk : depth + (half + 1) * chunk, :]

        @pl.loop(0, total_rows // tile)
        def _(i):
            here = pl.ds(pl.multiple_of(i * tile, tile), tile)
            raw = dot(hidden[here, :], kv_w[0])
            for h in range(span // HD):
                cols = slice(h * HD, (h + 1) * HD)
                keys[here, cols] = turn(raw[:, cols], cosine[here, :], sine_table[here, :]).astype(BF16)
            values[here, :] = dot(hidden[here, :], kv_w[1]).astype(BF16)

    here = pl.ds(pl.multiple_of(step * tile, tile), tile)
    rows_in = hidden[here, :]
    routes = routes_ref[...]
    hot = [[named_by(routes, order, j, k) for k in range(experts)] for j in range(2)]
    logits = dot(rows_in, router[...])
    picked = [sum(hot[j][k] * logits[:, k : k + 1] for k in range(experts)) for j in range(2)]
    top = jnp.maximum(picked[0], picked[1])
    raised = [jnp.exp(value - top) for value in picked]
    gates = [value / (raised[0] + raised[1]) for value in raised]
    gates_out[...] = columns([hot[0][k] * gates[0] + hot[1][k] * gates[1] for k in range(experts)])
    query_all = []
    for pieces in first_w:
        at, total = 0, 0.0
        for piece in pieces:
            size = piece.shape[0] * depth
            total = total + dot(rows_in[:, at : at + size], piece[:, :depth, :].reshape(size, span))
            at += size
        query_all.append(total)
    allowed = (place_row[...] >= bounds[:, 0:1]) & (place_row[...] <= bounds[:, 1:2])
    cos_here, sin_here = cosine[here, :], sine_table[here, :]
    vectors = []
    for j in range(2):
        raw = sum(hot[j][k] * query_all[k] for k in range(experts))
        heads = []
        for h in range(span // HD):
            cols = slice(h * HD, (h + 1) * HD)
            query = turn(raw[:, cols], cos_here, sin_here).astype(BF16)
            query_out[:, j * span + h * HD : j * span + (h + 1) * HD] = query
            scores = dot(query, keys[:, cols], ((1,), (1,))) * HD**-0.5
            scores = jnp.where(allowed, scores, NEG)
            row_top = jnp.max(scores, axis=1, keepdims=True)
            exp_scores = jnp.exp(scores - row_top)
            row_total = jnp.sum(exp_scores, axis=1, keepdims=True)
            heads.append(dot(exp_scores.astype(BF16), values[:, cols]) / row_total)
        vectors.append((jnp.concatenate(heads, axis=1) if len(heads) > 1 else heads[0]) * gates[j])
    total = 0.0
    for k in range(experts):
        part = (hot[0][k] * vectors[0] + hot[1][k] * vectors[1]).astype(BF16)
        wide[:, k * span : (k + 1) * span] = part
        total = total + dot(part, out_w[k][...])
    mixed[...] = total.astype(BF16)


def attend(blocks, first_w, out_w, router, routes, order, bounds, place_row, cosine, sine_table, chunk):
    total_rows, width = routes.shape[0], blocks[0].shape[1]
    experts = len(first_w)
    span = first_w[0][0].shape[2]
    layout = [len(pieces) for pieces in first_w]
    first_w = [piece for pieces in first_w for piece in pieces]
    tile = 256

    def struct(*shape):
        return jax.ShapeDtypeStruct(shape, BF16)

    return pl.pallas_call(
        functools.partial(attend_kernel, layout, len(blocks), chunk),
        grid=(total_rows // tile,),
        in_specs=[pl.BlockSpec(memory_space=pltpu.SMEM)]
        + [whole(w.shape) for w in [*blocks, *first_w, *out_w, router]]
        + [
            tiles((tile, 2)),
            tiles((tile, 2)),
            whole(place_row.shape),
            whole(cosine.shape),
            whole(sine_table.shape),
        ],
        out_specs=[
            tiles((tile, width)),
            tiles((tile, 2 * span)),
            whole((total_rows, span)),
            whole((total_rows, span)),
            tiles((tile, experts * span)),
            tiles((tile, experts)),
            whole((total_rows, width)),
            whole((2, width, span)),
        ],
        out_shape=[
            struct(total_rows, width),
            struct(total_rows, 2 * span),
            struct(total_rows, span),
            struct(total_rows, span),
            struct(total_rows, experts * span),
            jax.ShapeDtypeStruct((total_rows, experts), F32),
            struct(total_rows, width),
            struct(2, width, span),
        ],
        compiler_params=pltpu.CompilerParams(vmem_limit_bytes=VMEM_LIMIT),
        cost_estimate=cost(35),
        name="attend",
    )(order, *blocks, *first_w, *out_w, router, routes, bounds, place_row, cosine, sine_table)


def attend_back_kernel(layout, steps, count, order, *refs):
    blocks, refs = refs[:count], refs[count:]
    (first_w,), refs = regroup(refs, [layout])
    experts = len(layout)
    kv_w, refs = refs[0], refs[1:]
    out_w, refs = refs[:experts], refs[experts:]
    router, hidden, refs = refs[0], refs[1], refs[2:]
    routes_ref, gates_ref, bounds_row, place_col, cosine, sine_table, query_ref, keys, values, wide = refs[:10]
    grad_rows, grad_first, small, grad_mid, key_sum, value_sum, logit_grads = refs[10:]
    step = pl.program_id(0)
    tile = grad_rows.shape[0]
    total_rows, span = keys.shape

    @pl.when(step == 0)
    def _():
        lay(blocks, grad_mid)
        small[...] = jnp.zeros_like(small)
        key_sum[...] = jnp.zeros_like(key_sum)
        value_sum[...] = jnp.zeros_like(value_sum)

    @pl.when(step < steps)
    def _():
        here = pl.ds(pl.multiple_of(step * tile, tile), tile)
        routes = routes_ref[here, :]
        gates = gates_ref[here, :]
        hot = [[named_by(routes, order, j, k) for k in range(experts)] for j in range(2)]
        allowed = (place_col[...] >= bounds_row[0:1, here]) & (place_col[...] <= bounds_row[1:2, here])
        rows_in = grad_mid[here, :]
        slot_grads = [0.0, 0.0]
        sums = []
        for k in range(experts):
            grad = dot(rows_in, out_w[k][...], ((1,), (1,)))
            part = wide[:, k * span : (k + 1) * span].astype(F32)
            sums.append(jnp.sum(part * grad, axis=1, keepdims=True))
            for j in range(2):
                slot_grads[j] = slot_grads[j] + (hot[j][k] * gates[:, k : k + 1]) * grad
        sums = columns(sums)
        wide_grads = sums - gates * jnp.sum(sums, axis=1, keepdims=True)
        wide_grads = jnp.concatenate([wide_grads, jnp.zeros((tile, HD - experts), F32)], axis=1)
        logit_grads[here, :] = wide_grads.astype(BF16)
        cos_here, sin_here = cosine[here, :], sine_table[here, :]
        slot_queries = []
        for j in range(2):
            heads = []
            for h in range(span // HD):
                cols = slice(h * HD, (h + 1) * HD)
                query = query_ref[:, j * span + h * HD : j * span + (h + 1) * HD]
                grad = slot_grads[j][:, cols].astype(BF16)
                scores = dot(keys[:, cols], query, ((1,), (1,))) * HD**-0.5
                scores = jnp.where(allowed, scores, NEG)
                exp_scores = jnp.exp(scores - jnp.max(scores, axis=0, keepdims=True))
                probs = exp_scores * (1.0 / jnp.sum(exp_scores, axis=0, keepdims=True))
                value_sum[:, cols] += dot(probs.astype(BF16), grad)
                grad_probs = dot(values[:, cols], grad, ((1,), (1,)))
                mean = jnp.sum(probs * grad_probs, axis=0, keepdims=True)
                grad_scores = (probs * (grad_probs - mean)).astype(BF16)
                key_sum[:, cols] += dot(grad_scores, query)
                grad_query = dot(grad_scores, keys[:, cols], ((0,), (0,))) * HD**-0.5
                heads.append(turn(grad_query, cos_here, -sin_here))
            slot_queries.append(jnp.concatenate(heads, axis=1) if len(heads) > 1 else heads[0])
        for k in range(experts):
            grad_first[here, k * span : (k + 1) * span] = (
                hot[0][k] * slot_queries[0] + hot[1][k] * slot_queries[1]
            ).astype(BF16)

    @pl.when(step == steps - 1)
    def _():
        for h in range(span // HD):
            cols = slice(h * HD, (h + 1) * HD)
            grad_first[:, experts * span + h * HD : experts * span + (h + 1) * HD] = turn(
                key_sum[:, cols] * HD**-0.5, cosine[...], -sine_table[...]
            ).astype(BF16)
        grad_first[:, (experts + 1) * span :] = value_sum[...].astype(BF16)

    @pl.when(step >= steps)
    def _():
        here = pl.ds(pl.multiple_of((step - steps) * tile, tile), tile)
        total = dot(grad_first[here, experts * span : (experts + 1) * span], kv_w[0], ((1,), (1,)))
        total = total + dot(grad_first[here, (experts + 1) * span :], kv_w[1], ((1,), (1,)))
        total = total + dot(logit_grads[here, :], router[...], ((1,), (1,)))
        width = total.shape[1]
        depth = width // sum(piece.shape[0] for piece in first_w[0])
        for k, pieces in enumerate(first_w):
            grad = grad_first[here, k * span : (k + 1) * span]
            back = [
                dot(grad, piece[:, :depth, :].reshape(piece.shape[0] * depth, span), ((1,), (1,)))
                for piece in pieces
            ]
            total = total + (jnp.concatenate(back, axis=1) if len(back) > 1 else back[0])
        grad_rows[...] = total.astype(BF16)
        rows_in = hidden[...]
        small[:-8, :] += dot(logit_grads[here, :], rows_in, ((0,), (0,)))[: small.shape[0] - 8, :]
        small[-8:, :] += jnp.sum((total * rows_in.astype(F32)).reshape(-1, 8, total.shape[1]), axis=0)


def attend_back(
    blocks, first_w, kv_w, out_w, router, hidden, routes, order, gates, bounds_row, place_col, cosine,
    sine_table, query, keys, values, wide,
):
    small_rows = -(-len(first_w) // 8) * 8 + 8
    total_rows, width = routes.shape[0], blocks[0].shape[1]
    experts = len(first_w)
    span = first_w[0][0].shape[2]
    layout = [len(pieces) for pieces in first_w]
    first_w = [piece for pieces in first_w for piece in pieces]
    tile = 256 if total_rows <= 1024 else 128
    steps = total_rows // tile

    def early(shape):
        return pl.BlockSpec(shape, lambda i: (jnp.minimum(i, steps - 1), 0))

    return pl.pallas_call(
        functools.partial(attend_back_kernel, layout, steps, len(blocks)),
        grid=(2 * steps,),
        in_specs=[pl.BlockSpec(memory_space=pltpu.SMEM)]
        + [whole(w.shape) for w in [*blocks, *first_w, kv_w, *out_w, router]]
        + [pl.BlockSpec((tile, width), lambda i: (jnp.maximum(i - steps, 0), 0))]
        + [
            whole(routes.shape),
            whole(gates.shape),
            whole(bounds_row.shape),
            whole(place_col.shape),
            whole(cosine.shape),
            whole(sine_table.shape),
            early((tile, 2 * span)),
            whole(keys.shape),
            whole(values.shape),
            early((tile, experts * span)),
        ],
        out_specs=[
            pl.BlockSpec((tile, width), lambda i: (jnp.maximum(i - steps, 0), 0)),
            whole((total_rows, (experts + 2) * span)),
            whole((small_rows, width)),
            whole((total_rows, width)),
        ],
        out_shape=[
            jax.ShapeDtypeStruct((total_rows, width), BF16),
            jax.ShapeDtypeStruct((total_rows, (experts + 2) * span), BF16),
            jax.ShapeDtypeStruct((small_rows, width), F32),
            jax.ShapeDtypeStruct((total_rows, width), BF16),
        ],
        scratch_shapes=[
            pltpu.VMEM((total_rows, span), F32),
            pltpu.VMEM((total_rows, span), F32),
            pltpu.VMEM((total_rows, HD), BF16),
        ],
        compiler_params=pltpu.CompilerParams(vmem_limit_bytes=VMEM_LIMIT),
        cost_estimate=cost(45),
        name="attend_back",
    )(
        order, *blocks, *first_w, kv_w, *out_w, router, hidden, routes, gates, bounds_row, place_col, cosine,
        sine_table, query, keys, values, wide,
    )


def split_kernel(block, gate, up):
    half = block.shape[1] // 2
    gate[...] = block[:, :half].T.reshape(gate.shape)
    up[...] = block[:, half:].T.reshape(up.shape)


def split_columns(weight, shards):
    depth, both = weight.shape
    inner = both // (2 * shards)
    tile = 128
    out = jax.ShapeDtypeStruct((shards, inner, depth), BF16)
    spec = pl.BlockSpec((shards, inner, tile), lambda i: (0, 0, i))
    return pl.pallas_call(
        split_kernel,
        grid=(depth // tile,),
        in_specs=[tiles((tile, both))],
        out_specs=[spec, spec],
        out_shape=[out, out],
        compiler_params=pltpu.CompilerParams(vmem_limit_bytes=VMEM_LIMIT),
        cost_estimate=cost(5),
        name="split_columns",
    )(weight)


def join_kernel(gate, up, out):
    shards, inner, tile = gate.shape
    half = shards * inner
    out[:, :half] = gate[...].reshape(half, tile).T.astype(F32)
    out[:, half:] = up[...].reshape(half, tile).T.astype(F32)


def join_columns(gate, up):
    shards, inner, depth = gate.shape
    tile = 128
    spec = pl.BlockSpec((shards, inner, tile), lambda i: (0, 0, i))
    return pl.pallas_call(
        join_kernel,
        grid=(depth // tile,),
        in_specs=[spec, spec],
        out_specs=tiles((tile, 2 * shards * inner)),
        out_shape=jax.ShapeDtypeStruct((depth, 2 * shards * inner), F32),
        compiler_params=pltpu.CompilerParams(vmem_limit_bytes=VMEM_LIMIT),
        cost_estimate=cost(7),
        name="join_columns",
    )(gate, up)


def dispatch_kernel(capacity, count, gated, rank, *refs):
    blocks, refs = refs[:count], refs[count:]
    if gated:
        router, out, gates_out, hidden = refs
    else:
        out, hidden = refs
    step = pl.program_id(0)
    _, experts, rows = rank.shape

    @pl.when(step == 0)
    def _():
        lay(blocks, hidden)

    rows_in = hidden[pl.ds(pl.multiple_of(step * rows, rows), rows), :]
    ranks = rank[0]
    slot = lax.broadcasted_iota(jnp.int32, (capacity, rows), 0)
    pick = jnp.concatenate([(slot == ranks[k : k + 1, :]).astype(BF16) for k in range(experts)], axis=0)
    picked = dot(pick, rows_in).astype(BF16)
    for k in range(experts):
        out[k] = picked[k * capacity : (k + 1) * capacity, :]
    if gated:
        logits = dot(router[...], rows_in, ((1,), (1,)))[:experts, :]
        logits = jnp.where(ranks >= 0, logits, NEG)
        raised = jnp.where(ranks >= 0, jnp.exp(logits - jnp.max(logits, axis=0, keepdims=True)), 0.0)
        gates_out[0] = raised / jnp.sum(raised, axis=0, keepdims=True)


def dispatch(blocks, rank, capacity, router=None):
    shards, experts, rows = rank.shape
    width = blocks[0].shape[1]
    out_specs = [pl.BlockSpec((experts, capacity, width), lambda i: (0, i, 0))]
    out_shape = [jax.ShapeDtypeStruct((experts, shards * capacity, width), BF16)]
    extra = []
    if router is not None:
        extra = [router]
        out_specs += [tiles((1, experts, rows)), whole((shards * rows, width))]
        out_shape += [
            jax.ShapeDtypeStruct((shards, experts, rows), F32),
            jax.ShapeDtypeStruct((shards * rows, width), BF16),
        ]
    return pl.pallas_call(
        functools.partial(dispatch_kernel, capacity, len(blocks), router is not None),
        grid=(shards,),
        in_specs=[tiles((1, experts, rows))] + [whole(item.shape) for item in [*blocks, *extra]],
        out_specs=out_specs,
        out_shape=out_shape,
        scratch_shapes=[] if router is not None else [pltpu.VMEM((shards * rows, width), BF16)],
        compiler_params=pltpu.CompilerParams(vmem_limit_bytes=VMEM_LIMIT),
        cost_estimate=cost(10),
        name="dispatch",
    )(rank, *blocks, *extra)


class Fetch:
    def __init__(self, step, weights, store, sems):
        self.step, self.weights, self.store, self.sems = step, weights, store, sems

    def copies(self, index, which):
        made, slot = [], 0
        for i, pieces in enumerate(self.weights[index]):
            at = 0
            for piece in pieces:
                parts = [piece] if len(piece.shape) == 2 else [piece.at[s] for s in range(piece.shape[0])]
                for part in parts:
                    span = part.shape[1]
                    if i == which:
                        target = self.store.at[index % 2, i, :, at : at + span]
                        made.append(pltpu.make_async_copy(part, target, self.sems.at[index % 2, slot]))
                    at += span
                    slot += 1
        return made

    def start(self, sequence):
        count = len(self.weights)
        for index in range(count):

            @pl.when(self.step == index)
            def _():
                for ahead in [0, 1] if index == 0 else [index + 1]:
                    if ahead < count:
                        for i in sequence:
                            for copy in self.copies(ahead, i):
                                copy.start()

    def wait(self, i):
        for index in range(len(self.weights)):

            @pl.when(self.step == index)
            def _():
                for copy in self.copies(index, i):
                    copy.wait()


def regroup(refs, layout):
    groups, at = [], 0
    for expert in layout:
        groups.append([])
        for pieces in expert:
            groups[-1].append(refs[at : at + pieces])
            at += pieces
    return groups, refs[at:]


def row_scale(capacity, rank, gates):
    blocks, rows = rank.shape
    slot = lax.broadcasted_iota(jnp.int32, (capacity, rows), 0)
    return jnp.concatenate(
        [
            jnp.sum(jnp.where(slot == rank[b : b + 1, :], gates[b : b + 1, :], 0.0), axis=1, keepdims=True)
            for b in range(blocks)
        ],
        axis=0,
    )


def forward_kernel(capacity, layout, rank, gates, rows_in, *refs):
    weights, refs = regroup(refs, layout)
    count = len(layout)
    gate_out, up_out, act_out, result, store, sems = refs
    step = pl.program_id(0)
    fetch = Fetch(step, weights, store, sems)
    fetch.start((0, 1, 2))
    gate_w, up_w, down_w = [store.at[step % 2, i] for i in range(3)]
    scale = row_scale(capacity, rank[0], gates[0])
    slots = rows_in.shape[1]
    part = slots // 2
    for at in range(0, slots, part):
        here = slice(at, at + part)
        data = rows_in[0, here, :]
        if at == 0:
            fetch.wait(0)
        gate = dot(data, gate_w[...], ((1,), (1,)))
        if at == 0:
            fetch.wait(1)
        up = dot(data, up_w[...], ((1,), (1,)))
        act = (gate * jax.nn.sigmoid(gate) * up * scale[here, :]).astype(BF16)
        gate_out[0, here, :] = gate.astype(BF16)
        up_out[0, here, :] = up.astype(BF16)
        act_out[0, here, :] = act
        if at == 0:
            fetch.wait(2)
        result[0, here, :] = dot(act, down_w[...]).astype(BF16)


def backward_kernel(capacity, layout, rank, gates, cot, gate_ref, up_ref, act, *refs):
    weights, refs = regroup(refs, layout)
    count = len(layout)
    grad_gate_out, grad_up_out, grad_rows, gate_sums, store, sems = refs
    step = pl.program_id(0)
    fetch = Fetch(step, weights, store, sems)
    fetch.start((2, 0, 1))
    gate_w, up_w, down_w = [store.at[step % 2, i] for i in range(3)]
    scale = row_scale(capacity, rank[0], gates[0])
    slots = cot.shape[1]
    part = slots // 2
    blocks, rows = rank.shape[1:]
    slot = lax.broadcasted_iota(jnp.int32, (capacity, rows), 0)
    for at in range(0, slots, part):
        here = slice(at, at + part)
        if at == 0:
            fetch.wait(2)
        back = dot(cot[0, here, :], down_w[...], ((1,), (1,)))
        sums = jnp.sum(act[0, here, :].astype(F32) * back, axis=1, keepdims=True)
        for b in range(at // capacity, (at + part) // capacity):
            hit = slot == rank[0, b : b + 1, :]
            piece = sums[b * capacity - at : (b + 1) * capacity - at, :]
            gate_sums[0, b : b + 1, :] = jnp.sum(jnp.where(hit, piece, 0.0), axis=0, keepdims=True)
        gate = gate_ref[0, here, :].astype(F32)
        sigmoid_gate = jax.nn.sigmoid(gate)
        grad_act = back * scale[here, :]
        grad_up = (grad_act * gate * sigmoid_gate).astype(BF16)
        grad_gate = (
            grad_act * up_ref[0, here, :].astype(F32) * sigmoid_gate * (1.0 + gate * (1.0 - sigmoid_gate))
        ).astype(BF16)
        grad_up_out[0, here, :] = grad_up
        grad_gate_out[0, here, :] = grad_gate
        if at == 0:
            fetch.wait(0)
            fetch.wait(1)
        grad_rows[0, here, :] = (dot(grad_gate, gate_w[...]) + dot(grad_up, up_w[...])).astype(BF16)


def expert_call(
    kernel, name, first, rows_in, parts, weights, out_cols, sums, rank, gates, capacity, skip=0
):
    _, shards, rows = rank.shape
    width, inner = rows_in.shape[2], weights[0][0][0].shape[-2]
    count = len(weights)
    slots = shards * capacity
    layout = [[len(pieces) for pieces in group] for group in weights]
    flat = [piece for group in weights for pieces in group for piece in pieces]
    copies = 2 * shards + PARTS

    def of_all(shape):
        return pl.BlockSpec((1,) + shape, lambda i: (first + i, 0, 0))

    def of_these(shape):
        return pl.BlockSpec((1,) + shape, lambda i: (i, 0, 0))

    def of_parts(shape):
        return pl.BlockSpec((1,) + shape, lambda i: (skip + i, 0, 0))

    return pl.pallas_call(
        functools.partial(kernel, capacity, layout),
        grid=(count,),
        in_specs=[of_all((shards, rows)), of_all((shards, rows)), of_all((slots, width))]
        + [of_parts((slots, inner)) for _ in parts]
        + [pl.BlockSpec(memory_space=pl.ANY)] * len(flat),
        out_specs=[of_these((slots, cols)) for cols in out_cols] + [of_these((shards, rows))] * sums,
        out_shape=[jax.ShapeDtypeStruct((count, slots, cols), BF16) for cols in out_cols]
        + [jax.ShapeDtypeStruct((count, shards, rows), F32)] * sums,
        scratch_shapes=[pltpu.VMEM((2, 3, inner, width), BF16), pltpu.SemaphoreType.DMA((2, copies))],
        compiler_params=pltpu.CompilerParams(vmem_limit_bytes=VMEM_LIMIT),
        cost_estimate=cost(10 * count),
        name=name,
    )(rank, gates, rows_in, *parts, *flat)


def combine_kernel(capacity, extra, rank, *refs):
    rows, experts = rank.shape
    if extra:
        sums, gates, router, hidden, refs = refs[0], refs[1], refs[2], refs[3], refs[4:]
        *parts, out, small = refs
    else:
        *parts, out = refs
    slot = lax.broadcasted_iota(jnp.int32, (rows, experts * capacity), 1)
    pick = jnp.zeros(slot.shape, F32)
    for k in range(experts):
        at = jnp.where(rank[:, k : k + 1] >= 0, rank[:, k : k + 1] + k * capacity, -1)
        pick = pick + (slot == at).astype(F32)
    data = jnp.concatenate([part[i] for part in parts for i in range(part.shape[0])], axis=0)
    total = dot(pick.astype(BF16), data)
    if extra:
        grads = sums[0] - gates[0] * jnp.sum(sums[0], axis=0, keepdims=True)
        pad = router.shape[0] - experts
        grads = jnp.concatenate([grads, jnp.zeros((pad, rows), F32)], axis=0).astype(BF16)
        total = total + dot(grads, router[...], ((0,), (0,)))

        @pl.when(pl.program_id(0) == 0)
        def _():
            small[...] = jnp.zeros_like(small)

        small[...] += dot(grads, hidden[...])
    out[...] = total.astype(BF16)


def combine(rank_cols, parts, rows, capacity, extra=()):
    total_rows, experts = rank_cols.shape
    width = parts[0].shape[2]
    out_specs = [tiles((rows, width))]
    out_shape = [jax.ShapeDtypeStruct((total_rows, width), BF16)]
    in_specs = [tiles((rows, experts))]
    if extra:
        router = extra[2]
        in_specs += [
            tiles((1, experts, rows)), tiles((1, experts, rows)), whole(router.shape), tiles((rows, width)),
        ]
        out_specs.append(whole(router.shape))
        out_shape.append(jax.ShapeDtypeStruct(router.shape, F32))
    return pl.pallas_call(
        functools.partial(combine_kernel, capacity, bool(extra)),
        grid=(total_rows // rows,),
        in_specs=in_specs
        + [pl.BlockSpec((part.shape[0], capacity, width), lambda i: (0, i, 0)) for part in parts],
        out_specs=out_specs,
        out_shape=out_shape,
        compiler_params=pltpu.CompilerParams(vmem_limit_bytes=VMEM_LIMIT),
        cost_estimate=cost(10),
        name="combine",
    )(rank_cols, *extra, *parts)


def body(
    tokens_in,
    cotangent,
    norm1_gain,
    kv_weight,
    query_weight,
    attn_out_weight,
    attn_router,
    norm2_gain,
    in_weight,
    out_weight,
    mlp_router,
    attn_routes,
    mlp_routes,
    place_order,
    seq_lengths,
):
    experts = lax.axis_size("expert")
    shards = lax.axis_size("shard")
    rows, width = tokens_in.shape
    total_rows = rows * shards
    chips = experts // 2
    capacity = -(-5 * rows // (2 * experts) // 16) * 16
    span = query_weight.shape[2] // shards
    inner = out_weight.shape[1]
    depth = in_weight.shape[1]
    order = jnp.stack(expert_order())
    own_expert = order[0]

    chunk = depth // experts
    kv_chunk = lax.dynamic_slice_in_dim(kv_weight, own_expert * chunk, chunk, axis=0)
    kv_chunk = kv_chunk.reshape(chunk, 2, shards, span).transpose(2, 1, 0, 3)
    query_blocks = query_weight[0].reshape(depth, shards, span).transpose(1, 0, 2)
    first_blocks = jnp.concatenate([query_blocks, kv_chunk.reshape(shards, 2 * chunk, span)], axis=1)

    info = jnp.concatenate(
        [place_order, attn_routes.T, mlp_routes.T, jnp.zeros((3, rows), jnp.int32)], axis=0
    )
    rounds = []
    for i, step in enumerate(powers(shards)):
        source = (lambda info=info: info[None]) if i == 0 else (lambda i=i: rounds[i - 1].value)
        rounds.append(Transfer(lambda v, step=step: doubled(v, step), source))
    inverse = jnp.argsort(order)

    stream = tokens_in.astype(F32)
    normed1, row_scale1 = norm_rows(stream, norm1_gain)
    hidden1_own = normed1.astype(BF16)
    first = Transfer(shard_exchange, lambda: first_blocks)
    out_far = fetch_far(lambda: attn_out_weight[0])
    first_far = [fetch_far(lambda: first.value, i, 2) for i in range(2)]
    (hidden1_own,) = begin([hidden1_own], [first])
    gate_blocks, up_blocks = split_columns(in_weight[0], shards)
    down_parts = [part_of(out_weight[0], i) for i in range(PARTS)]
    down_far = [fetch_far(lambda i=i: down_parts[i]) for i in range(PARTS)]
    ring = RingGather(hidden1_own)
    ring.tie([], out_far + rounds[:1])
    ring.step()
    ring.tie([], (), [first, gate_blocks, *down_parts] + out_far + rounds[:1])
    ring.tie([], first_far[0] + rounds[1:2])
    ring.step()
    ring.tie([], (), first_far[0] + rounds[1:2])
    ring.tie([], first_far[1] + rounds[2:3])
    ring.step()
    ring.tie([], (), rounds[2:3])
    for item in rounds[3:]:
        item.value = item.source()
        item.begin()
    info = ring_sorted(rounds[-1].value)
    lengths = seq_lengths[0]
    places = info[:, 0].reshape(total_rows)
    cosine, sine_table, seq_ids = rope_tables(places, lengths)
    starts = jnp.sum(
        jnp.where(jnp.arange(lengths.shape[0])[None, :] < seq_ids[:, None], lengths[None, :], 0), axis=1
    )
    cosine = jnp.concatenate([cosine, cosine], axis=1)
    sine_table = jnp.concatenate([-sine_table, sine_table], axis=1)
    bounds = jnp.stack([starts, places])

    def routes_of(first):
        return info[:, first : first + 2].transpose(0, 2, 1).reshape(total_rows, 2)

    routes_attn = routes_of(1)
    named = jnp.any(info[:, 3:5, None, :] == order[None, None, :, None], axis=1)
    earlier = (jnp.arange(rows)[:, None] < jnp.arange(rows)[None, :]).astype(BF16)
    rank = jnp.einsum("bku,ut->bkt", named.astype(BF16), earlier, preferred_element_type=F32)
    rank = jnp.where(named, rank, -1.0).astype(jnp.int32)
    rank_cols = rank.transpose(0, 2, 1).reshape(total_rows, experts)
    rank_rows = rank.transpose(1, 0, 2)
    attn_router_rel = jnp.take(attn_router, order, axis=1)
    mlp_router_rel = jnp.take(mlp_router, order, axis=1)

    router_wide = jnp.pad(attn_router_rel, ((0, 0), (0, 128 - experts)))
    tables = [cosine, sine_table, bounds, routes_attn, rank, router_wide]
    ring.step()
    ring.tie([], (), tables + first_far[1])
    hidden1_blocks = ring.blocks()
    gate_own = Transfer(shard_exchange, lambda: gate_blocks)
    hidden1_blocks = begin(hidden1_blocks, [gate_own])
    first_all = []
    for pieces in [[first.value]] + [[a.value, b.value] for a, b in zip(*first_far)]:
        first_all += [pieces, [core_swap(piece) for piece in pieces]]
    attn_out_w = with_swaps([attn_out_weight[0]] + [item.value for item in out_far])
    hidden1_blocks = begin(hidden1_blocks, down_far[1] + down_far[2])
    up_own = Transfer(shard_exchange, lambda: up_blocks)
    gate_far = [fetch_far(lambda: gate_own.value, i, PARTS) for i in range(PARTS)]
    up_far = [fetch_far(lambda: up_own.value, i, PARTS) for i in range(PARTS)]

    def first_parts(grad):
        key_grad, value_grad = [
            grad[:, (experts + i) * span : (experts + i + 1) * span].reshape(shards, experts, chunk, span)
            for i in range(2)
        ]
        parts = []
        for k in range(experts):
            query_grad = grad[:, k * span : (k + 1) * span].reshape(shards, depth, span)
            own = [
                lax.dynamic_index_in_dim(item, order[k], axis=1, keepdims=False)
                for item in (key_grad, value_grad)
            ]
            parts.append(jnp.concatenate([query_grad, *own], axis=1))
        return expert_sums(parts, range(0, experts, 2))

    mixed, query, keys, values, vec_wide, gates_attn, hidden1, kv_w = attend(
        hidden1_blocks, first_all, attn_out_w, router_wide, routes_attn, order[None], bounds.T,
        places[None], cosine, sine_table, chunk,
    )
    (mixed,) = tie([mixed], [gate_own] + down_far[1] + down_far[2])
    middle = stream + ring_scatter(
        mixed,
        {
            0: ([up_own] + gate_far[0] + gate_far[1] + gate_far[2], gate_far[0] + gate_far[1] + gate_far[2]),
            1: (gate_far[3], [up_own] + gate_far[3]),
            2: (up_far[0], up_far[0]),
            3: (up_far[1], up_far[1]),
        },
    )

    normed2, row_scale2 = norm_rows(middle, norm2_gain)
    hidden2_own = normed2.astype(BF16)
    cot_steps = RingGather(cotangent)
    ring = RingGather(hidden2_own)
    for part in (up_far[2], up_far[3], down_far[3]):
        ring.tie([], part)
        ring.step()
        ring.tie([], (), part)
    ring.step()
    cot_steps.ahead[0], *ring.last = tie([cotangent, *ring.last], [])
    cot_steps.behind[0] = cot_steps.ahead[0]
    hidden2_blocks = ring.blocks()
    cot_steps.step()
    router_rows = jnp.pad(mlp_router_rel.T, ((0, 16 - experts), (0, 0)))
    rows_in, gates_mlp, hidden2 = dispatch(hidden2_blocks, rank, capacity, router_rows)
    gate_rows = gates_mlp.transpose(1, 0, 2)
    down_own = Transfer(None, None, out_weight[0])
    halves = []
    forwards = []
    rows_now = rows_in
    for first in range(0, experts, 2):
        (rows_now,) = cot_steps.tie([rows_now], () if first else down_far[0])
        cot_steps.step()
        at = first // 2 - 1
        these = [
            [[own.value]] if first == 0 else [[part[at].value for part in far]]
            for own, far in ((gate_own, gate_far), (up_own, up_far), (down_own, down_far))
        ]
        these = [(near[0], [core_swap(piece) for piece in near[0]]) for near in these]
        these = list(zip(*these))
        halves.append((first, these))
        forwards.append(
            list(
                expert_call(
                forward_kernel, "expert_forward", first, rows_now, [], these,
                [inner, inner, inner, width], 0, rank_rows, gate_rows, capacity,
                )
            )
        )
        (forwards[-1][3],) = cot_steps.tie([forwards[-1][3]], (), () if first else down_far[0])
        rows_now = after(rows_now, forwards[-1][3])
    gates_low, ups_low, acts, results = zip(*forwards)
    cot_steps.step()
    combined = combine(rank_cols, results, rows, capacity)[0]
    (combined,) = cot_steps.tie([combined])
    cot_blocks = cot_steps.blocks()
    cot_blocks[0] = after(cot_blocks[0], combined)
    result_steps = RingScatter(combined)
    result_steps.step()
    rows_cot = dispatch(cot_blocks, rank, capacity)[0]
    rows_cot = dispatch(cot_blocks, rank, capacity)[0]
    backs, gate_w_grads = {}, {}
    cot_now = rows_cot
    calls = halves[:0:-1] + [(1, halves[0][1][1:]), (0, halves[0][1][:1])]
    for first, these in calls:
        at = first // 2
        (cot_now,) = result_steps.tie([cot_now], gate_hand[1 - first] if first < 2 else ())
        result_steps.step()
        back = [*expert_call(
            backward_kernel, "expert_backward", first, cot_now, [gates_low[at], ups_low[at], acts[at]],
            these, [inner, inner, width], 1, rank_rows, gate_rows, capacity, first % 2,
        )]
        (back[2],) = result_steps.tie([back[2]], (), gate_hand[1 - first] if first < 2 else ())
        cot_now = after(cot_now, back[2])
        for k in range(len(these)):
            backs[first + k] = [back[0][k], back[1][k], back[2], back[3]]
        if first >= 2:
            for k in (first + 1, first):
                gate_w_grads[k] = dot(backs[k][0], rows_in[k], ((0,), (0,))).astype(BF16)
                cot_now = after(cot_now, gate_w_grads[k])
            gate_sums_far = expert_sums(gate_w_grads, range(2, experts, 2)) if first == 2 else None
            gate_hand = [hand_far(lambda: gate_sums_far, i, PARTS) for i in range(PARTS)]
    grad_gates, grad_ups = [[backs[k][i] for k in range(experts)] for i in range(2)]
    groups = [0, 1] + list(range(2, experts, 2))
    grads, gate_sums = [[backs[k][i] for k in groups] for i in (2, 3)]
    acts = [item[i] for item in acts for i in range(2)]
    gate_sums = jnp.concatenate(gate_sums, axis=0).transpose(1, 0, 2)
    grads = begin(grads[:1], gate_hand[2]) + grads[1:]
    combined, mlp_part = combine(
        rank_cols, grads, rows, capacity, (gate_sums, gates_mlp, router_rows, hidden2)
    )
    result_rows = result_steps.total()
    output = (middle + result_rows).astype(BF16)
    up_w_grads, down_w_grads = {}, {}

    def weight_grad(into, left, right, k, late):
        into[k] = dot(after(left[k], late), right[k], ((0,), (0,))).astype(BF16)
        return into[k]

    gate_back = Transfer(
        lambda v: shard_exchange(v.reshape(inner, shards, depth).transpose(1, 0, 2)),
        lambda: gate_total,
    )
    up_back = Transfer(shard_exchange, lambda: up_total)
    ring = RingScatter(combined)
    (late,) = ring.tie([after(rank, result_rows)], (), gate_hand[2])
    (late,) = ring.tie([late], gate_hand[3])
    for k in range(experts - 1, 3, -1):
        weight_grad(up_w_grads, grad_ups, rows_in, k, late)
    ring.step()
    weight_grad(up_w_grads, grad_ups, rows_in, 3, late)
    (late,) = ring.tie([late], (), [up_w_grads[3]])
    ring.step()
    weight_grad(up_w_grads, grad_ups, rows_in, 2, late)
    (late,) = ring.tie([late], (), [up_w_grads[2]] + gate_hand[3])
    ring.step()
    up_sums_far = expert_sums(up_w_grads, range(2, experts, 2))
    up_hand = [hand_far(lambda: up_sums_far, i, PARTS) for i in range(PARTS)]
    weight_grad(gate_w_grads, grad_gates, rows_in, 1, late)
    (late,) = ring.tie([late], (), [gate_w_grads[1], *up_sums_far])
    ring.step()
    weight_grad(gate_w_grads, grad_gates, rows_in, 0, late)
    gate_near = expert_sums(gate_w_grads, [0])[0].astype(F32)
    (late,) = ring.tie([late], (), [gate_w_grads[0]])
    back_rows = ring.total()
    grad_hidden2 = back_rows
    grad_middle, grad_gain2 = norm_back(grad_hidden2, middle, row_scale2, norm2_gain)
    grad_middle = grad_middle + cotangent.astype(F32)

    gate_total = total_of(gate_near, gate_hand).astype(BF16)
    gate_total = total_of(gate_near, gate_hand).astype(BF16)
    ring = RingGather(grad_middle.astype(BF16))
    (late,) = ring.tie([late], [gate_back] + up_hand[0] + up_hand[1])
    ring.step()
    weight_grad(up_w_grads, grad_ups, rows_in, 1, late)
    weight_grad(down_w_grads, acts, rows_cot, 1, late)
    (late,) = ring.tie([late], (), [up_w_grads[1], down_w_grads[1]] + up_hand[0] + up_hand[1])
    (late,) = ring.tie([late], up_hand[2] + up_hand[3])
    ring.step()
    weight_grad(up_w_grads, grad_ups, rows_in, 0, late)
    up_near = expert_sums(up_w_grads, [0])[0].astype(F32)
    for k in [*range(experts - 1, 1, -1), 0]:
        weight_grad(down_w_grads, acts, rows_cot, k, late)
    down_sums_far = expert_sums(down_w_grads, range(2, experts, 2))
    down_hand = [hand_far(lambda: down_sums_far, i, PARTS) for i in range(PARTS)]
    (late,) = ring.tie([late], (), [up_w_grads[0], down_w_grads[0], *down_sums_far, gate_back] + up_hand[2] + up_hand[3])
    (late,) = ring.tie([late], down_hand[0])
    ring.step()
    up_total = total_of(up_near, up_hand).astype(BF16)
    up_total = up_total.reshape(inner, shards, depth).transpose(1, 0, 2)
    (late,) = ring.tie([late], (), [up_total] + down_hand[0])
    ring.step()
    (late,) = ring.tie([late])
    mid_blocks = ring.blocks()
    mid_blocks = begin(mid_blocks, [up_back] + down_hand[1] + down_hand[2] + down_hand[3])
    grad_rows1, grad_first, attn_part, grad_mid = attend_back(
        mid_blocks, first_all, kv_w, attn_out_w, router_wide, hidden1, routes_attn, order[None], gates_attn, bounds,
        places[:, None], cosine, sine_table, query, keys, values, vec_wide,
    )
    grad_rows1, grad_first, attn_part, late = tie(
        [grad_rows1, grad_first, attn_part, late], down_hand[1] + down_hand[2] + down_hand[3]
    )
    sums = jnp.concatenate(
        [
            jnp.sum(attn_part[-8:], axis=0, keepdims=True) / norm1_gain,
            grad_gain2[None],
            jnp.take(attn_part, inverse, axis=0),
            jnp.take(mlp_part, inverse, axis=0),
        ],
        axis=0,
    )
    rounds = [("expert", step) for step in powers(experts)] + [("shard", step) for step in powers(shards)]
    small = []
    for i, (axis, step) in enumerate(rounds):
        source = (lambda: sums) if i == 0 else (lambda i=i: small[i - 1].value)
        small.append(Transfer(lambda v, axis=axis, step=step: sum_pairs(v, axis, step), source))
    ring = RingScatter(grad_rows1)
    late, grad_first = ring.tie([late, grad_first], small[:1])
    ring.step()
    grad_first_w = dot(hidden1, grad_first, ((0,), (0,))).astype(BF16)
    first_sums = first_parts(grad_first_w)
    first_hand = [hand_far(lambda: first_sums[1:], i, 2) for i in range(2)]
    (late,) = tie([late], [grad_first_w] + small[:1])
    (late,) = begin([late], small[1:2])
    (late,) = ring.tie([late], (), [up_back] + first_sums + small[1:2])
    (late,) = ring.tie([late], first_hand[0] + small[2:3])
    ring.step()
    (late,) = ring.tie([late], (), first_hand[0] + small[2:3])
    (late,) = ring.tie([late], first_hand[1] + small[3:4])
    ring.step()
    grad_second_w = dot(after(vec_wide, late), grad_mid, ((0,), (0,))).astype(BF16)
    (late,) = ring.tie([late], (), first_hand[1] + small[3:4] + [grad_second_w])
    came = [jnp.concatenate([a.value, b.value], axis=0) for a, b in zip(*first_hand)]
    first_grad = sum_f32(first_sums[:1] + came).astype(BF16)
    first_back = Transfer(shard_exchange, lambda: first_grad)
    second_sums = expert_sums(jnp.split(grad_second_w, experts, axis=0), range(0, experts, 2))
    second_hand = hand_far(lambda: second_sums[1:])
    (late,) = ring.tie([late], [first_back])
    ring.step()
    (late,) = begin([late], second_hand)
    for item in small[4:]:
        (late,) = tie(begin([late], [item]), [item])
    back_rows1 = ring.total()
    late = after(late, back_rows1)
    in_grad = join_columns(after(gate_back.value, late), up_back.value)[None]
    attn_grad = sum_f32(second_sums[:1] + [item.value for item in second_hand])[None]
    out_grad = total_of(expert_sums(down_w_grads, [0])[0].astype(F32), down_hand)[None]
    sums = small[-1].value
    grad_hidden1 = back_rows1
    grad_stream, _ = norm_back(grad_hidden1, stream, row_scale1, norm1_gain)
    grad_input = grad_stream + grad_middle

    first_grad = first_back.value
    query_grad = first_grad[:, :depth].transpose(1, 0, 2).reshape(1, depth, shards * span).astype(F32)
    kv_grad = first_grad[:, depth:].reshape(shards, 2, chunk, span)
    kv_grad = kv_grad.transpose(2, 1, 0, 3).reshape(chunk, 2 * shards * span)
    pieces = expert_gather(kv_grad.astype(BF16))
    kv_grad = jnp.zeros((depth, 2 * shards * span), F32)
    for k, piece in enumerate(pieces):
        kv_grad = lax.dynamic_update_slice_in_dim(kv_grad, piece.astype(F32), order[k] * chunk, axis=0)

    return (
        output,
        grad_input,
        sums[0],
        kv_grad,
        query_grad,
        attn_grad,
        sums[2 : 2 + experts].T,
        sums[1],
        in_grad,
        out_grad,
        sums[2 + experts :].T,
    )


def solution(mesh):
    return jax.shard_map(
        body,
        mesh=mesh,
        in_specs=(
            P(("expert", "shard"), None),
            P(("expert", "shard"), None),
            P(),
            P("shard", None),
            P("expert", "shard", None),
            P("expert", "shard", None),
            P(),
            P(),
            P("expert", "shard", None),
            P("expert", "shard", None),
            P(),
            P(("expert", "shard"), None),
            P(("expert", "shard"), None),
            P("expert", "shard"),
            P("expert", None),
        ),
        out_specs=(
            P(("expert", "shard"), None),
            P(("expert", "shard"), None),
            P(),
            P("shard", None),
            P("expert", "shard", None),
            P("expert", "shard", None),
            P(),
            P(),
            P("expert", "shard", None),
            P("expert", "shard", None),
            P(),
        ),
        check_vma=False,
    )
```

```python
import functools

import jax
import jax.numpy as jnp
from jax import lax
from jax.experimental import pallas as pl
from jax.experimental.pallas import tpu as pltpu
from jax.sharding import PartitionSpec as P

HD = 128


EPS = 1e-05
THETA = 10000.0
NEG = -1e30
F32 = jnp.float32
BF16 = jnp.bfloat16
VMEM_LIMIT = 60 * 1024 * 1024


def dot(left, right, contract=((1,), (0,))):
    return lax.dot_general(left, right, (contract, ((), ())), preferred_element_type=F32)


def norm_rows(values, norm_gain):
    row_scale = lax.rsqrt(jnp.mean(values * values, axis=-1, keepdims=True) + EPS)
    return (values * row_scale * norm_gain, row_scale)


def norm_back(grad_rows, values, row_scale, norm_gain):
    gain_grad = jnp.sum(grad_rows * values * row_scale, axis=0)
    scaled_grad = grad_rows * norm_gain
    mean_term = jnp.mean(scaled_grad * values, axis=-1, keepdims=True)
    return (
        row_scale * scaled_grad - values * row_scale * row_scale * row_scale * mean_term,
        gain_grad,
    )


def seq_of(places, lengths):
    seq_ends = jnp.cumsum(lengths)
    passed = seq_ends[None, :] <= places[:, None]
    return (passed, jnp.sum(passed.astype(jnp.int32), axis=1))


def rope_tables(places, lengths):
    passed, seq_ids = seq_of(places, lengths)
    starts = jnp.sum(jnp.where(passed, lengths[None, :], 0), axis=1)
    where_in = (places - starts).astype(F32)
    frequency = THETA ** (-jnp.arange(0, HD // 2, dtype=F32) * (2.0 / HD))
    angles = where_in[:, None] * frequency[None, :]
    return (jnp.cos(angles), jnp.sin(angles), seq_ids)


def rotate(values, cosine, sine_table):
    half_width = values.shape[-1] // 2
    leading = values[..., :half_width]
    trailing = values[..., half_width:]
    return jnp.concatenate(
        [leading * cosine - trailing * sine_table, trailing * cosine + leading * sine_table],
        axis=-1,
    )


def ring_cycle(count):
    if count == 8:
        return [0, 2, 4, 6, 7, 5, 3, 1]
    if count == 16:
        return [0, 1, 2, 3, 7, 6, 5, 9, 10, 11, 15, 14, 13, 12, 8, 4]
    return list(range(count))


def ring_move(value, hops):
    cycle = ring_cycle(lax.axis_size("shard"))
    count = len(cycle)
    return lax.ppermute(
        value, "shard", [(cycle[i], cycle[(i + hops) % count]) for i in range(count)]
    )


def after(value, *others):
    return lax.optimization_barrier((value,) + others)[0] if others else value


class Transfer:
    def __init__(self, move, source, value=None):
        self.move, self.source, self.value = move, source, value

    def begin(self):
        self.value = self.move(self.value)


def tie(values, others):
    if len(values) + len(others) < 2:
        return list(values)
    held = [item.value if isinstance(item, Transfer) else item for item in others]
    tied = lax.optimization_barrier((*values, *held))
    for item, value in zip(others, tied[len(values) :]):
        if isinstance(item, Transfer):
            item.value = value
    return list(tied[: len(values)])


def begin(values, transfers):
    for item in transfers:
        item.value = item.source()
    values = tie(values, transfers)
    for item in transfers:
        item.begin()
    return values


class RingGather:
    def __init__(self, block):
        self.ahead, self.behind = [block], [block]
        self.last = []

    def tie(self, values, begins=(), ends=()):
        heads = self.last or [self.ahead[-1], self.behind[-1]]
        for item in begins:
            item.value = item.source()
        tied = tie([*heads, *values], [*begins, *ends])
        if self.last:
            self.last = tied[:2]
        else:
            self.ahead[-1], self.behind[-1] = tied[:2]
        for item in begins:
            item.begin()
        return tied[2:]

    def step(self):
        far = lax.axis_size("shard") // 2
        if len(self.ahead) < far:
            self.ahead.append(ring_move(self.ahead[-1], 1))
            self.behind.append(ring_move(self.behind[-1], -1))
        elif not self.last:
            cut = self.ahead[0].shape[0] // 2
            self.last = [ring_move(self.ahead[-1][:cut], 1), ring_move(self.behind[-1][cut:], -1)]

    def blocks(self):
        while not self.last:
            self.step()
        return self.ahead + self.last + self.behind[:0:-1]


class RingScatter:
    def __init__(self, partial):
        count = lax.axis_size("shard")
        rows = partial.shape[0] // count
        self.far, self.done = count // 2, 0
        self.part = [partial[r * rows : (r + 1) * rows] for r in range(count)]
        cut = rows // 2
        self.back, self.fore = self.part[self.far][:cut], self.part[self.far][cut:]

    def tie(self, values, begins=(), ends=()):
        for item in begins:
            item.value = item.source()
        tied = tie([self.back, self.fore, *values], [*begins, *ends])
        self.back, self.fore = tied[:2]
        for item in begins:
            item.begin()
        return tied[2:]

    def step(self):
        if self.done == self.far:
            return
        self.back, self.fore = ring_move(self.back, -1), ring_move(self.fore, 1)
        if self.done == 0:
            empty = jnp.zeros_like(self.back)
            self.back = jnp.concatenate([self.back, empty], axis=0)
            self.fore = jnp.concatenate([empty, self.fore], axis=0)
        if self.done < self.far - 1:
            self.back = self.part[self.far - 1 - self.done] + self.back
            self.fore = self.part[self.far + 1 + self.done] + self.fore
        self.done += 1

    def total(self):
        while self.done < self.far:
            self.step()
        return self.part[0].astype(F32) + self.back.astype(F32) + self.fore.astype(F32)


def ring_gather(block, plan={}):
    ring = RingGather(block)
    for step in range(lax.axis_size("shard") // 2):
        begins, ends = plan.get(step, ((), ()))
        ring.tie([], begins)
        ring.step()
        ring.tie([], (), ends)
    return ring.blocks()


def ring_scatter(partial, plan={}):
    ring = RingScatter(partial)
    for step in range(lax.axis_size("shard") // 2):
        begins, ends = plan.get(step, ((), ()))
        ring.tie([], begins)
        ring.step()
        ring.tie([], (), ends)
    return ring.total()


def doubled(value, step):
    count = lax.axis_size("shard")
    return jnp.concatenate([value, lax.ppermute(value, "shard", [(i, i ^ step) for i in range(count)])])


def ring_sorted(blocks):
    cycle = ring_cycle(lax.axis_size("shard"))
    own = lax.axis_index("shard")
    spot = jnp.array([cycle.index(s) for s in range(len(cycle))])[own]
    return jnp.take(blocks, own ^ jnp.array(cycle)[(spot - jnp.arange(len(cycle))) % len(cycle)], axis=0)


def core_swap(value):
    return lax.ppermute(value, "expert", [(i, i ^ 1) for i in range(lax.axis_size("expert"))])


def chip_shift(value, hops):
    count = lax.axis_size("expert")
    chips = count // 2
    return lax.ppermute(
        value, "expert", [(i, (i // 2 + hops) % chips * 2 + i % 2) for i in range(count)]
    )


def expert_order():
    index = lax.axis_index("expert")
    chips = lax.axis_size("expert") // 2
    return [
        (index // 2 + dx) % chips * 2 + (index % 2 + dc) % 2
        for dx in range(chips)
        for dc in range(2)
    ]


def expert_gather(value):
    chips = lax.axis_size("expert") // 2
    own = [value] + [chip_shift(value, -dx) for dx in range(1, chips)]
    return [piece for item in own for piece in (item, core_swap(item))]


def after_all(values, *others):
    return [after(item, *others) for item in values]


PARTS = 4


def part_of(value, which, parts=PARTS):
    size = value.shape[1 if value.ndim == 2 else 0] // parts
    here = slice(which * size, (which + 1) * size)
    return value[:, here] if value.ndim == 2 else value[here]


def fetch_far(source, which=0, parts=1):
    chips = lax.axis_size("expert") // 2
    take = lambda: part_of(source(), which, parts)
    return [Transfer(lambda v, dx=dx: chip_shift(v, -dx), take) for dx in range(1, chips)]


def hand_far(source, which=0, parts=1):
    chips = lax.axis_size("expert") // 2
    return [
        Transfer(
            lambda v, dx=dx: chip_shift(v, dx), lambda dx=dx: part_of(source()[dx - 1], which, parts)
        )
        for dx in range(1, chips)
    ]


def total_of(near, parts):
    came = [sum_f32([item.value for item in part]) for part in parts]
    return near + jnp.concatenate(came, axis=1)


def with_swaps(items):
    return [piece for item in items for piece in (item, core_swap(item))]


def expert_sums(pieces, firsts):
    return [
        (pieces[k].astype(F32) + core_swap(pieces[k + 1]).astype(F32)).astype(BF16) for k in firsts
    ]


def far_exchange(sums):
    return [chip_shift(item, dx + 1) for dx, item in enumerate(sums)]


def sum_f32(parts):
    return sum(item.astype(F32) for item in parts)


def expert_reduce(pieces):
    sums = expert_sums(pieces, range(0, len(pieces), 2))
    return sum_f32(sums[:1] + far_exchange(sums[1:]))


def shard_exchange(pieces):
    return lax.all_to_all(pieces, "shard", split_axis=0, concat_axis=0, tiled=True)


def sum_pairs(value, axis, step):
    count = lax.axis_size(axis)
    return value + lax.ppermute(value, axis, [(i, i ^ step) for i in range(count)])


def powers(count):
    return [1 << i for i in range(count.bit_length() - 1)]


def turn(values, cosine, sine_table):
    return values * cosine + pltpu.roll(values, HD // 2, 1) * sine_table


def whole(shape):
    zeros = (0,) * len(shape)
    return pl.BlockSpec(shape, lambda *_: zeros, pipeline_mode=pl.Buffered(1))


def tiles(shape):
    return pl.BlockSpec(shape, lambda i: (i,) + (0,) * (len(shape) - 1))


def named_by(routes, order, slot, k):
    return (routes[:, slot : slot + 1] == order[0, k]).astype(F32)


def columns(parts):
    lane = lax.broadcasted_iota(jnp.int32, (parts[0].shape[0], len(parts)), 1)
    total = jnp.zeros(lane.shape, F32)
    for k, part in enumerate(parts):
        total = jnp.where(lane == k, part, total)
    return total


def lay(blocks, target):
    start = 0
    for block in blocks:
        target[start : start + block.shape[0], :] = block[...]
        start += block.shape[0]


def cost(microseconds):
    return pl.CostEstimate(flops=microseconds * 115 * 10**6, bytes_accessed=1 << 16, transcendentals=0)


def attend_kernel(layout, count, chunk, order, *refs):
    blocks, refs = refs[:count], refs[count:]
    (first_w,), refs = regroup(refs, [layout])
    experts = len(layout)
    out_w, refs = refs[:experts], refs[experts:]
    router, routes_ref, bounds, place_row, cosine, sine_table = refs[:6]
    mixed, query_out, keys, values, wide, gates_out, hidden, kv_w = refs[6:]
    step = pl.program_id(0)
    tile = mixed.shape[0]
    total_rows, span = keys.shape
    width = hidden.shape[1]
    shards = sum(piece.shape[0] for piece in first_w[0])
    depth = width // shards

    @pl.when(step == 0)
    def _():
        lay(blocks, hidden)
        for k in range(experts):
            for s, block in enumerate([piece.at[i] for piece in first_w[k] for i in range(piece.shape[0])]):
                to = pl.ds(pl.multiple_of(s * depth + order[0, k] * chunk, chunk), chunk)
                for half in range(2):
                    kv_w[half, to, :] = block[depth + half * chunk : depth + (half + 1) * chunk, :]

        @pl.loop(0, total_rows // tile)
        def _(i):
            here = pl.ds(pl.multiple_of(i * tile, tile), tile)
            raw = dot(hidden[here, :], kv_w[0])
            for h in range(span // HD):
                cols = slice(h * HD, (h + 1) * HD)
                keys[here, cols] = turn(raw[:, cols], cosine[here, :], sine_table[here, :]).astype(BF16)
            values[here, :] = dot(hidden[here, :], kv_w[1]).astype(BF16)

    here = pl.ds(pl.multiple_of(step * tile, tile), tile)
    rows_in = hidden[here, :]
    routes = routes_ref[...]
    hot = [[named_by(routes, order, j, k) for k in range(experts)] for j in range(2)]
    logits = dot(rows_in, router[...])
    picked = [sum(hot[j][k] * logits[:, k : k + 1] for k in range(experts)) for j in range(2)]
    top = jnp.maximum(picked[0], picked[1])
    raised = [jnp.exp(value - top) for value in picked]
    gates = [value / (raised[0] + raised[1]) for value in raised]
    gates_out[...] = columns([hot[0][k] * gates[0] + hot[1][k] * gates[1] for k in range(experts)])
    query_all = []
    for pieces in first_w:
        at, total = 0, 0.0
        for piece in pieces:
            size = piece.shape[0] * depth
            total = total + dot(rows_in[:, at : at + size], piece[:, :depth, :].reshape(size, span))
            at += size
        query_all.append(total)
    allowed = (place_row[...] >= bounds[:, 0:1]) & (place_row[...] <= bounds[:, 1:2])
    cos_here, sin_here = cosine[here, :], sine_table[here, :]
    vectors = []
    for j in range(2):
        raw = sum(hot[j][k] * query_all[k] for k in range(experts))
        heads = []
        for h in range(span // HD):
            cols = slice(h * HD, (h + 1) * HD)
            query = turn(raw[:, cols], cos_here, sin_here).astype(BF16)
            query_out[:, j * span + h * HD : j * span + (h + 1) * HD] = query
            scores = dot(query, keys[:, cols], ((1,), (1,))) * HD**-0.5
            scores = jnp.where(allowed, scores, NEG)
            row_top = jnp.max(scores, axis=1, keepdims=True)
            exp_scores = jnp.exp(scores - row_top)
            row_total = jnp.sum(exp_scores, axis=1, keepdims=True)
            heads.append(dot(exp_scores.astype(BF16), values[:, cols]) / row_total)
        vectors.append((jnp.concatenate(heads, axis=1) if len(heads) > 1 else heads[0]) * gates[j])
    total = 0.0
    for k in range(experts):
        part = (hot[0][k] * vectors[0] + hot[1][k] * vectors[1]).astype(BF16)
        wide[:, k * span : (k + 1) * span] = part
        total = total + dot(part, out_w[k][...])
    mixed[...] = total.astype(BF16)


def attend(blocks, first_w, out_w, router, routes, order, bounds, place_row, cosine, sine_table, chunk):
    total_rows, width = routes.shape[0], blocks[0].shape[1]
    experts = len(first_w)
    span = first_w[0][0].shape[2]
    layout = [len(pieces) for pieces in first_w]
    first_w = [piece for pieces in first_w for piece in pieces]
    tile = 256

    def struct(*shape):
        return jax.ShapeDtypeStruct(shape, BF16)

    return pl.pallas_call(
        functools.partial(attend_kernel, layout, len(blocks), chunk),
        grid=(total_rows // tile,),
        in_specs=[pl.BlockSpec(memory_space=pltpu.SMEM)]
        + [whole(w.shape) for w in [*blocks, *first_w, *out_w, router]]
        + [
            tiles((tile, 2)),
            tiles((tile, 2)),
            whole(place_row.shape),
            whole(cosine.shape),
            whole(sine_table.shape),
        ],
        out_specs=[
            tiles((tile, width)),
            tiles((tile, 2 * span)),
            whole((total_rows, span)),
            whole((total_rows, span)),
            tiles((tile, experts * span)),
            tiles((tile, experts)),
            whole((total_rows, width)),
            whole((2, width, span)),
        ],
        out_shape=[
            struct(total_rows, width),
            struct(total_rows, 2 * span),
            struct(total_rows, span),
            struct(total_rows, span),
            struct(total_rows, experts * span),
            jax.ShapeDtypeStruct((total_rows, experts), F32),
            struct(total_rows, width),
            struct(2, width, span),
        ],
        compiler_params=pltpu.CompilerParams(vmem_limit_bytes=VMEM_LIMIT),
        cost_estimate=cost(35),
        name="attend",
    )(order, *blocks, *first_w, *out_w, router, routes, bounds, place_row, cosine, sine_table)


def attend_back_kernel(layout, steps, count, order, *refs):
    blocks, refs = refs[:count], refs[count:]
    (first_w,), refs = regroup(refs, [layout])
    experts = len(layout)
    kv_w, refs = refs[0], refs[1:]
    out_w, refs = refs[:experts], refs[experts:]
    router, hidden, refs = refs[0], refs[1], refs[2:]
    routes_ref, gates_ref, bounds_row, place_col, cosine, sine_table, query_ref, keys, values, wide = refs[:10]
    grad_rows, grad_first, small, grad_mid, key_sum, value_sum, logit_grads = refs[10:]
    step = pl.program_id(0)
    tile = grad_rows.shape[0]
    total_rows, span = keys.shape

    @pl.when(step == 0)
    def _():
        lay(blocks, grad_mid)
        small[...] = jnp.zeros_like(small)
        key_sum[...] = jnp.zeros_like(key_sum)
        value_sum[...] = jnp.zeros_like(value_sum)

    @pl.when(step < steps)
    def _():
        here = pl.ds(pl.multiple_of(step * tile, tile), tile)
        routes = routes_ref[here, :]
        gates = gates_ref[here, :]
        hot = [[named_by(routes, order, j, k) for k in range(experts)] for j in range(2)]
        allowed = (place_col[...] >= bounds_row[0:1, here]) & (place_col[...] <= bounds_row[1:2, here])
        rows_in = grad_mid[here, :]
        slot_grads = [0.0, 0.0]
        sums = []
        for k in range(experts):
            grad = dot(rows_in, out_w[k][...], ((1,), (1,)))
            part = wide[:, k * span : (k + 1) * span].astype(F32)
            sums.append(jnp.sum(part * grad, axis=1, keepdims=True))
            for j in range(2):
                slot_grads[j] = slot_grads[j] + (hot[j][k] * gates[:, k : k + 1]) * grad
        sums = columns(sums)
        wide_grads = sums - gates * jnp.sum(sums, axis=1, keepdims=True)
        wide_grads = jnp.concatenate([wide_grads, jnp.zeros((tile, HD - experts), F32)], axis=1)
        logit_grads[here, :] = wide_grads.astype(BF16)
        cos_here, sin_here = cosine[here, :], sine_table[here, :]
        slot_queries = []
        for j in range(2):
            heads = []
            for h in range(span // HD):
                cols = slice(h * HD, (h + 1) * HD)
                query = query_ref[:, j * span + h * HD : j * span + (h + 1) * HD]
                grad = slot_grads[j][:, cols].astype(BF16)
                scores = dot(keys[:, cols], query, ((1,), (1,))) * HD**-0.5
                scores = jnp.where(allowed, scores, NEG)
                exp_scores = jnp.exp(scores - jnp.max(scores, axis=0, keepdims=True))
                probs = exp_scores * (1.0 / jnp.sum(exp_scores, axis=0, keepdims=True))
                value_sum[:, cols] += dot(probs.astype(BF16), grad)
                grad_probs = dot(values[:, cols], grad, ((1,), (1,)))
                mean = jnp.sum(probs * grad_probs, axis=0, keepdims=True)
                grad_scores = (probs * (grad_probs - mean)).astype(BF16)
                key_sum[:, cols] += dot(grad_scores, query)
                grad_query = dot(grad_scores, keys[:, cols], ((0,), (0,))) * HD**-0.5
                heads.append(turn(grad_query, cos_here, -sin_here))
            slot_queries.append(jnp.concatenate(heads, axis=1) if len(heads) > 1 else heads[0])
        for k in range(experts):
            grad_first[here, k * span : (k + 1) * span] = (
                hot[0][k] * slot_queries[0] + hot[1][k] * slot_queries[1]
            ).astype(BF16)

    @pl.when(step == steps - 1)
    def _():
        for h in range(span // HD):
            cols = slice(h * HD, (h + 1) * HD)
            grad_first[:, experts * span + h * HD : experts * span + (h + 1) * HD] = turn(
                key_sum[:, cols] * HD**-0.5, cosine[...], -sine_table[...]
            ).astype(BF16)
        grad_first[:, (experts + 1) * span :] = value_sum[...].astype(BF16)

    @pl.when(step >= steps)
    def _():
        here = pl.ds(pl.multiple_of((step - steps) * tile, tile), tile)
        total = dot(grad_first[here, experts * span : (experts + 1) * span], kv_w[0], ((1,), (1,)))
        total = total + dot(grad_first[here, (experts + 1) * span :], kv_w[1], ((1,), (1,)))
        total = total + dot(logit_grads[here, :], router[...], ((1,), (1,)))
        width = total.shape[1]
        depth = width // sum(piece.shape[0] for piece in first_w[0])
        for k, pieces in enumerate(first_w):
            grad = grad_first[here, k * span : (k + 1) * span]
            back = [
                dot(grad, piece[:, :depth, :].reshape(piece.shape[0] * depth, span), ((1,), (1,)))
                for piece in pieces
            ]
            total = total + (jnp.concatenate(back, axis=1) if len(back) > 1 else back[0])
        grad_rows[...] = total.astype(BF16)
        rows_in = hidden[...]
        small[:-8, :] += dot(logit_grads[here, :], rows_in, ((0,), (0,)))[: small.shape[0] - 8, :]
        small[-8:, :] += jnp.sum((total * rows_in.astype(F32)).reshape(-1, 8, total.shape[1]), axis=0)


def attend_back(
    blocks, first_w, kv_w, out_w, router, hidden, routes, order, gates, bounds_row, place_col, cosine,
    sine_table, query, keys, values, wide,
):
    small_rows = -(-len(first_w) // 8) * 8 + 8
    total_rows, width = routes.shape[0], blocks[0].shape[1]
    experts = len(first_w)
    span = first_w[0][0].shape[2]
    layout = [len(pieces) for pieces in first_w]
    first_w = [piece for pieces in first_w for piece in pieces]
    tile = 256 if total_rows <= 1024 else 128
    steps = total_rows // tile

    def early(shape):
        return pl.BlockSpec(shape, lambda i: (jnp.minimum(i, steps - 1), 0))

    return pl.pallas_call(
        functools.partial(attend_back_kernel, layout, steps, len(blocks)),
        grid=(2 * steps,),
        in_specs=[pl.BlockSpec(memory_space=pltpu.SMEM)]
        + [whole(w.shape) for w in [*blocks, *first_w, kv_w, *out_w, router]]
        + [pl.BlockSpec((tile, width), lambda i: (jnp.maximum(i - steps, 0), 0))]
        + [
            whole(routes.shape),
            whole(gates.shape),
            whole(bounds_row.shape),
            whole(place_col.shape),
            whole(cosine.shape),
            whole(sine_table.shape),
            early((tile, 2 * span)),
            whole(keys.shape),
            whole(values.shape),
            early((tile, experts * span)),
        ],
        out_specs=[
            pl.BlockSpec((tile, width), lambda i: (jnp.maximum(i - steps, 0), 0)),
            whole((total_rows, (experts + 2) * span)),
            whole((small_rows, width)),
            whole((total_rows, width)),
        ],
        out_shape=[
            jax.ShapeDtypeStruct((total_rows, width), BF16),
            jax.ShapeDtypeStruct((total_rows, (experts + 2) * span), BF16),
            jax.ShapeDtypeStruct((small_rows, width), F32),
            jax.ShapeDtypeStruct((total_rows, width), BF16),
        ],
        scratch_shapes=[
            pltpu.VMEM((total_rows, span), F32),
            pltpu.VMEM((total_rows, span), F32),
            pltpu.VMEM((total_rows, HD), BF16),
        ],
        compiler_params=pltpu.CompilerParams(vmem_limit_bytes=VMEM_LIMIT),
        cost_estimate=cost(45),
        name="attend_back",
    )(
        order, *blocks, *first_w, kv_w, *out_w, router, hidden, routes, gates, bounds_row, place_col, cosine,
        sine_table, query, keys, values, wide,
    )


def split_kernel(block, gate, up):
    half = block.shape[1] // 2
    gate[...] = block[:, :half].T.reshape(gate.shape)
    up[...] = block[:, half:].T.reshape(up.shape)


def split_columns(weight, shards):
    depth, both = weight.shape
    inner = both // (2 * shards)
    tile = 128
    out = jax.ShapeDtypeStruct((shards, inner, depth), BF16)
    spec = pl.BlockSpec((shards, inner, tile), lambda i: (0, 0, i))
    return pl.pallas_call(
        split_kernel,
        grid=(depth // tile,),
        in_specs=[tiles((tile, both))],
        out_specs=[spec, spec],
        out_shape=[out, out],
        compiler_params=pltpu.CompilerParams(vmem_limit_bytes=VMEM_LIMIT),
        cost_estimate=cost(5),
        name="split_columns",
    )(weight)


def join_kernel(gate, up, out):
    shards, inner, tile = gate.shape
    half = shards * inner
    out[:, :half] = gate[...].reshape(half, tile).T.astype(F32)
    out[:, half:] = up[...].reshape(half, tile).T.astype(F32)


def join_columns(gate, up):
    shards, inner, depth = gate.shape
    tile = 128
    spec = pl.BlockSpec((shards, inner, tile), lambda i: (0, 0, i))
    return pl.pallas_call(
        join_kernel,
        grid=(depth // tile,),
        in_specs=[spec, spec],
        out_specs=tiles((tile, 2 * shards * inner)),
        out_shape=jax.ShapeDtypeStruct((depth, 2 * shards * inner), F32),
        compiler_params=pltpu.CompilerParams(vmem_limit_bytes=VMEM_LIMIT),
        cost_estimate=cost(7),
        name="join_columns",
    )(gate, up)


def dispatch_kernel(capacity, count, gated, rank, *refs):
    blocks, refs = refs[:count], refs[count:]
    if gated:
        router, out, gates_out, hidden = refs
    else:
        out, hidden = refs
    step = pl.program_id(0)
    _, experts, rows = rank.shape

    @pl.when(step == 0)
    def _():
        lay(blocks, hidden)

    rows_in = hidden[pl.ds(pl.multiple_of(step * rows, rows), rows), :]
    ranks = rank[0]
    slot = lax.broadcasted_iota(jnp.int32, (capacity, rows), 0)
    pick = jnp.concatenate([(slot == ranks[k : k + 1, :]).astype(BF16) for k in range(experts)], axis=0)
    picked = dot(pick, rows_in).astype(BF16)
    for k in range(experts):
        out[k] = picked[k * capacity : (k + 1) * capacity, :]
    if gated:
        logits = dot(router[...], rows_in, ((1,), (1,)))[:experts, :]
        logits = jnp.where(ranks >= 0, logits, NEG)
        raised = jnp.where(ranks >= 0, jnp.exp(logits - jnp.max(logits, axis=0, keepdims=True)), 0.0)
        gates_out[0] = raised / jnp.sum(raised, axis=0, keepdims=True)


def dispatch(blocks, rank, capacity, router=None):
    shards, experts, rows = rank.shape
    width = blocks[0].shape[1]
    out_specs = [pl.BlockSpec((experts, capacity, width), lambda i: (0, i, 0))]
    out_shape = [jax.ShapeDtypeStruct((experts, shards * capacity, width), BF16)]
    extra = []
    if router is not None:
        extra = [router]
        out_specs += [tiles((1, experts, rows)), whole((shards * rows, width))]
        out_shape += [
            jax.ShapeDtypeStruct((shards, experts, rows), F32),
            jax.ShapeDtypeStruct((shards * rows, width), BF16),
        ]
    return pl.pallas_call(
        functools.partial(dispatch_kernel, capacity, len(blocks), router is not None),
        grid=(shards,),
        in_specs=[tiles((1, experts, rows))] + [whole(item.shape) for item in [*blocks, *extra]],
        out_specs=out_specs,
        out_shape=out_shape,
        scratch_shapes=[] if router is not None else [pltpu.VMEM((shards * rows, width), BF16)],
        compiler_params=pltpu.CompilerParams(vmem_limit_bytes=VMEM_LIMIT),
        cost_estimate=cost(10),
        name="dispatch",
    )(rank, *blocks, *extra)


class Fetch:
    def __init__(self, step, weights, store, sems):
        self.step, self.weights, self.store, self.sems = step, weights, store, sems

    def copies(self, index, which):
        made, slot = [], 0
        for i, pieces in enumerate(self.weights[index]):
            at = 0
            for piece in pieces:
                parts = [piece] if len(piece.shape) == 2 else [piece.at[s] for s in range(piece.shape[0])]
                for part in parts:
                    span = part.shape[1]
                    if i == which:
                        target = self.store.at[index % 2, i, :, at : at + span]
                        made.append(pltpu.make_async_copy(part, target, self.sems.at[index % 2, slot]))
                    at += span
                    slot += 1
        return made

    def start(self, sequence):
        count = len(self.weights)
        for index in range(count):

            @pl.when(self.step == index)
            def _():
                for ahead in [0, 1] if index == 0 else [index + 1]:
                    if ahead < count:
                        for i in sequence:
                            for copy in self.copies(ahead, i):
                                copy.start()

    def wait(self, i):
        for index in range(len(self.weights)):

            @pl.when(self.step == index)
            def _():
                for copy in self.copies(index, i):
                    copy.wait()


def regroup(refs, layout):
    groups, at = [], 0
    for expert in layout:
        groups.append([])
        for pieces in expert:
            groups[-1].append(refs[at : at + pieces])
            at += pieces
    return groups, refs[at:]


def row_scale(capacity, rank, gates):
    blocks, rows = rank.shape
    slot = lax.broadcasted_iota(jnp.int32, (capacity, rows), 0)
    return jnp.concatenate(
        [
            jnp.sum(jnp.where(slot == rank[b : b + 1, :], gates[b : b + 1, :], 0.0), axis=1, keepdims=True)
            for b in range(blocks)
        ],
        axis=0,
    )


def forward_kernel(capacity, layout, rank, gates, rows_in, *refs):
    weights, refs = regroup(refs, layout)
    count = len(layout)
    gate_out, up_out, act_out, result, store, sems = refs
    step = pl.program_id(0)
    fetch = Fetch(step, weights, store, sems)
    fetch.start((0, 1, 2))
    gate_w, up_w, down_w = [store.at[step % 2, i] for i in range(3)]
    scale = row_scale(capacity, rank[0], gates[0])
    slots = rows_in.shape[1]
    part = slots // 2
    for at in range(0, slots, part):
        here = slice(at, at + part)
        data = rows_in[0, here, :]
        if at == 0:
            fetch.wait(0)
        gate = dot(data, gate_w[...], ((1,), (1,)))
        if at == 0:
            fetch.wait(1)
        up = dot(data, up_w[...], ((1,), (1,)))
        act = (gate * jax.nn.sigmoid(gate) * up * scale[here, :]).astype(BF16)
        gate_out[0, here, :] = gate.astype(BF16)
        up_out[0, here, :] = up.astype(BF16)
        act_out[0, here, :] = act
        if at == 0:
            fetch.wait(2)
        result[0, here, :] = dot(act, down_w[...]).astype(BF16)


def backward_kernel(capacity, layout, rank, gates, cot, gate_ref, up_ref, act, *refs):
    weights, refs = regroup(refs, layout)
    count = len(layout)
    grad_gate_out, grad_up_out, grad_rows, gate_sums, store, sems = refs
    step = pl.program_id(0)
    fetch = Fetch(step, weights, store, sems)
    fetch.start((2, 0, 1))
    gate_w, up_w, down_w = [store.at[step % 2, i] for i in range(3)]
    scale = row_scale(capacity, rank[0], gates[0])
    slots = cot.shape[1]
    part = slots // 2
    blocks, rows = rank.shape[1:]
    slot = lax.broadcasted_iota(jnp.int32, (capacity, rows), 0)
    for at in range(0, slots, part):
        here = slice(at, at + part)
        if at == 0:
            fetch.wait(2)
        back = dot(cot[0, here, :], down_w[...], ((1,), (1,)))
        sums = jnp.sum(act[0, here, :].astype(F32) * back, axis=1, keepdims=True)
        for b in range(at // capacity, (at + part) // capacity):
            hit = slot == rank[0, b : b + 1, :]
            piece = sums[b * capacity - at : (b + 1) * capacity - at, :]
            gate_sums[0, b : b + 1, :] = jnp.sum(jnp.where(hit, piece, 0.0), axis=0, keepdims=True)
        gate = gate_ref[0, here, :].astype(F32)
        sigmoid_gate = jax.nn.sigmoid(gate)
        grad_act = back * scale[here, :]
        grad_up = (grad_act * gate * sigmoid_gate).astype(BF16)
        grad_gate = (
            grad_act * up_ref[0, here, :].astype(F32) * sigmoid_gate * (1.0 + gate * (1.0 - sigmoid_gate))
        ).astype(BF16)
        grad_up_out[0, here, :] = grad_up
        grad_gate_out[0, here, :] = grad_gate
        if at == 0:
            fetch.wait(0)
            fetch.wait(1)
        grad_rows[0, here, :] = (dot(grad_gate, gate_w[...]) + dot(grad_up, up_w[...])).astype(BF16)


def expert_call(
    kernel, name, first, rows_in, parts, weights, out_cols, sums, rank, gates, capacity, skip=0
):
    _, shards, rows = rank.shape
    width, inner = rows_in.shape[2], weights[0][0][0].shape[-2]
    count = len(weights)
    slots = shards * capacity
    layout = [[len(pieces) for pieces in group] for group in weights]
    flat = [piece for group in weights for pieces in group for piece in pieces]
    copies = 2 * shards + PARTS

    def of_all(shape):
        return pl.BlockSpec((1,) + shape, lambda i: (first + i, 0, 0))

    def of_these(shape):
        return pl.BlockSpec((1,) + shape, lambda i: (i, 0, 0))

    def of_parts(shape):
        return pl.BlockSpec((1,) + shape, lambda i: (skip + i, 0, 0))

    return pl.pallas_call(
        functools.partial(kernel, capacity, layout),
        grid=(count,),
        in_specs=[of_all((shards, rows)), of_all((shards, rows)), of_all((slots, width))]
        + [of_parts((slots, inner)) for _ in parts]
        + [pl.BlockSpec(memory_space=pl.ANY)] * len(flat),
        out_specs=[of_these((slots, cols)) for cols in out_cols] + [of_these((shards, rows))] * sums,
        out_shape=[jax.ShapeDtypeStruct((count, slots, cols), BF16) for cols in out_cols]
        + [jax.ShapeDtypeStruct((count, shards, rows), F32)] * sums,
        scratch_shapes=[pltpu.VMEM((2, 3, inner, width), BF16), pltpu.SemaphoreType.DMA((2, copies))],
        compiler_params=pltpu.CompilerParams(vmem_limit_bytes=VMEM_LIMIT),
        cost_estimate=cost(10 * count),
        name=name,
    )(rank, gates, rows_in, *parts, *flat)


def combine_kernel(capacity, extra, rank, *refs):
    rows, experts = rank.shape
    if extra:
        sums, gates, router, hidden, refs = refs[0], refs[1], refs[2], refs[3], refs[4:]
        *parts, out, small = refs
    else:
        *parts, out = refs
    slot = lax.broadcasted_iota(jnp.int32, (rows, experts * capacity), 1)
    pick = jnp.zeros(slot.shape, F32)
    for k in range(experts):
        at = jnp.where(rank[:, k : k + 1] >= 0, rank[:, k : k + 1] + k * capacity, -1)
        pick = pick + (slot == at).astype(F32)
    data = jnp.concatenate([part[i] for part in parts for i in range(part.shape[0])], axis=0)
    total = dot(pick.astype(BF16), data)
    if extra:
        grads = sums[0] - gates[0] * jnp.sum(sums[0], axis=0, keepdims=True)
        pad = router.shape[0] - experts
        grads = jnp.concatenate([grads, jnp.zeros((pad, rows), F32)], axis=0).astype(BF16)
        total = total + dot(grads, router[...], ((0,), (0,)))

        @pl.when(pl.program_id(0) == 0)
        def _():
            small[...] = jnp.zeros_like(small)

        small[...] += dot(grads, hidden[...])
    out[...] = total.astype(BF16)


def combine(rank_cols, parts, rows, capacity, extra=()):
    total_rows, experts = rank_cols.shape
    width = parts[0].shape[2]
    out_specs = [tiles((rows, width))]
    out_shape = [jax.ShapeDtypeStruct((total_rows, width), BF16)]
    in_specs = [tiles((rows, experts))]
    if extra:
        router = extra[2]
        in_specs += [
            tiles((1, experts, rows)), tiles((1, experts, rows)), whole(router.shape), tiles((rows, width)),
        ]
        out_specs.append(whole(router.shape))
        out_shape.append(jax.ShapeDtypeStruct(router.shape, F32))
    return pl.pallas_call(
        functools.partial(combine_kernel, capacity, bool(extra)),
        grid=(total_rows // rows,),
        in_specs=in_specs
        + [pl.BlockSpec((part.shape[0], capacity, width), lambda i: (0, i, 0)) for part in parts],
        out_specs=out_specs,
        out_shape=out_shape,
        compiler_params=pltpu.CompilerParams(vmem_limit_bytes=VMEM_LIMIT),
        cost_estimate=cost(10),
        name="combine",
    )(rank_cols, *extra, *parts)


def body(
    tokens_in,
    cotangent,
    norm1_gain,
    kv_weight,
    query_weight,
    attn_out_weight,
    attn_router,
    norm2_gain,
    in_weight,
    out_weight,
    mlp_router,
    attn_routes,
    mlp_routes,
    place_order,
    seq_lengths,
):
    experts = lax.axis_size("expert")
    shards = lax.axis_size("shard")
    rows, width = tokens_in.shape
    total_rows = rows * shards
    chips = experts // 2
    capacity = -(-5 * rows // (2 * experts) // 16) * 16
    span = query_weight.shape[2] // shards
    inner = out_weight.shape[1]
    depth = in_weight.shape[1]
    order = jnp.stack(expert_order())
    own_expert = order[0]

    chunk = depth // experts
    kv_chunk = lax.dynamic_slice_in_dim(kv_weight, own_expert * chunk, chunk, axis=0)
    kv_chunk = kv_chunk.reshape(chunk, 2, shards, span).transpose(2, 1, 0, 3)
    query_blocks = query_weight[0].reshape(depth, shards, span).transpose(1, 0, 2)
    first_blocks = jnp.concatenate([query_blocks, kv_chunk.reshape(shards, 2 * chunk, span)], axis=1)

    info = jnp.concatenate(
        [place_order, attn_routes.T, mlp_routes.T, jnp.zeros((3, rows), jnp.int32)], axis=0
    )
    rounds = []
    for i, step in enumerate(powers(shards)):
        source = (lambda info=info: info[None]) if i == 0 else (lambda i=i: rounds[i - 1].value)
        rounds.append(Transfer(lambda v, step=step: doubled(v, step), source))
    inverse = jnp.argsort(order)

    stream = tokens_in.astype(F32)
    normed1, row_scale1 = norm_rows(stream, norm1_gain)
    hidden1_own = normed1.astype(BF16)
    first = Transfer(shard_exchange, lambda: first_blocks)
    out_far = fetch_far(lambda: attn_out_weight[0])
    first_far = [fetch_far(lambda: first.value, i, 2) for i in range(2)]
    (hidden1_own,) = begin([hidden1_own], [first])
    gate_blocks, up_blocks = split_columns(in_weight[0], shards)
    down_parts = [part_of(out_weight[0], i) for i in range(PARTS)]
    down_far = [fetch_far(lambda i=i: down_parts[i]) for i in range(PARTS)]
    ring = RingGather(hidden1_own)
    ring.tie([], out_far + rounds[:1])
    ring.step()
    ring.tie([], (), [first, gate_blocks, *down_parts] + out_far + rounds[:1])
    ring.tie([], first_far[0] + rounds[1:2])
    ring.step()
    ring.tie([], (), first_far[0] + rounds[1:2])
    ring.tie([], first_far[1] + rounds[2:3])
    ring.step()
    ring.tie([], (), rounds[2:3])
    for item in rounds[3:]:
        item.value = item.source()
        item.begin()
    info = ring_sorted(rounds[-1].value)
    lengths = seq_lengths[0]
    places = info[:, 0].reshape(total_rows)
    cosine, sine_table, seq_ids = rope_tables(places, lengths)
    starts = jnp.sum(
        jnp.where(jnp.arange(lengths.shape[0])[None, :] < seq_ids[:, None], lengths[None, :], 0), axis=1
    )
    cosine = jnp.concatenate([cosine, cosine], axis=1)
    sine_table = jnp.concatenate([-sine_table, sine_table], axis=1)
    bounds = jnp.stack([starts, places])

    def routes_of(first):
        return info[:, first : first + 2].transpose(0, 2, 1).reshape(total_rows, 2)

    routes_attn = routes_of(1)
    named = jnp.any(info[:, 3:5, None, :] == order[None, None, :, None], axis=1)
    earlier = (jnp.arange(rows)[:, None] < jnp.arange(rows)[None, :]).astype(BF16)
    rank = jnp.einsum("bku,ut->bkt", named.astype(BF16), earlier, preferred_element_type=F32)
    rank = jnp.where(named, rank, -1.0).astype(jnp.int32)
    rank_cols = rank.transpose(0, 2, 1).reshape(total_rows, experts)
    rank_rows = rank.transpose(1, 0, 2)
    attn_router_rel = jnp.take(attn_router, order, axis=1)
    mlp_router_rel = jnp.take(mlp_router, order, axis=1)

    router_wide = jnp.pad(attn_router_rel, ((0, 0), (0, 128 - experts)))
    tables = [cosine, sine_table, bounds, routes_attn, rank, router_wide]
    ring.step()
    ring.tie([], (), tables + first_far[1])
    hidden1_blocks = ring.blocks()
    gate_own = Transfer(shard_exchange, lambda: gate_blocks)
    hidden1_blocks = begin(hidden1_blocks, [gate_own])
    first_all = []
    for pieces in [[first.value]] + [[a.value, b.value] for a, b in zip(*first_far)]:
        first_all += [pieces, [core_swap(piece) for piece in pieces]]
    attn_out_w = with_swaps([attn_out_weight[0]] + [item.value for item in out_far])
    hidden1_blocks = begin(hidden1_blocks, down_far[1] + down_far[2])
    up_own = Transfer(shard_exchange, lambda: up_blocks)
    gate_far = [fetch_far(lambda: gate_own.value, i, PARTS) for i in range(PARTS)]
    up_far = [fetch_far(lambda: up_own.value, i, PARTS) for i in range(PARTS)]

    def first_parts(grad):
        key_grad, value_grad = [
            grad[:, (experts + i) * span : (experts + i + 1) * span].reshape(shards, experts, chunk, span)
            for i in range(2)
        ]
        parts = []
        for k in range(experts):
            query_grad = grad[:, k * span : (k + 1) * span].reshape(shards, depth, span)
            own = [
                lax.dynamic_index_in_dim(item, order[k], axis=1, keepdims=False)
                for item in (key_grad, value_grad)
            ]
            parts.append(jnp.concatenate([query_grad, *own], axis=1))
        return expert_sums(parts, range(0, experts, 2))

    mixed, query, keys, values, vec_wide, gates_attn, hidden1, kv_w = attend(
        hidden1_blocks, first_all, attn_out_w, router_wide, routes_attn, order[None], bounds.T,
        places[None], cosine, sine_table, chunk,
    )
    (mixed,) = tie([mixed], [gate_own] + down_far[1] + down_far[2])
    middle = stream + ring_scatter(
        mixed,
        {
            0: ([up_own] + gate_far[0] + gate_far[1] + gate_far[2], gate_far[0] + gate_far[1] + gate_far[2]),
            1: (gate_far[3], [up_own] + gate_far[3]),
            2: (up_far[0], up_far[0]),
            3: (up_far[1], up_far[1]),
        },
    )

    normed2, row_scale2 = norm_rows(middle, norm2_gain)
    hidden2_own = normed2.astype(BF16)
    cot_steps = RingGather(cotangent)
    ring = RingGather(hidden2_own)
    for part in (up_far[2], up_far[3], down_far[3]):
        ring.tie([], part)
        ring.step()
        ring.tie([], (), part)
    ring.step()
    cot_steps.ahead[0], *ring.last = tie([cotangent, *ring.last], [])
    cot_steps.behind[0] = cot_steps.ahead[0]
    hidden2_blocks = ring.blocks()
    cot_steps.step()
    router_rows = jnp.pad(mlp_router_rel.T, ((0, 16 - experts), (0, 0)))
    rows_in, gates_mlp, hidden2 = dispatch(hidden2_blocks, rank, capacity, router_rows)
    gate_rows = gates_mlp.transpose(1, 0, 2)
    down_own = Transfer(None, None, out_weight[0])
    halves = []
    forwards = []
    rows_now = rows_in
    for first in range(0, experts, 2):
        (rows_now,) = cot_steps.tie([rows_now], () if first else down_far[0])
        cot_steps.step()
        at = first // 2 - 1
        these = [
            [[own.value]] if first == 0 else [[part[at].value for part in far]]
            for own, far in ((gate_own, gate_far), (up_own, up_far), (down_own, down_far))
        ]
        these = [(near[0], [core_swap(piece) for piece in near[0]]) for near in these]
        these = list(zip(*these))
        halves.append((first, these))
        forwards.append(
            list(
                expert_call(
                forward_kernel, "expert_forward", first, rows_now, [], these,
                [inner, inner, inner, width], 0, rank_rows, gate_rows, capacity,
                )
            )
        )
        (forwards[-1][3],) = cot_steps.tie([forwards[-1][3]], (), () if first else down_far[0])
        rows_now = after(rows_now, forwards[-1][3])
    gates_low, ups_low, acts, results = zip(*forwards)
    cot_steps.step()
    combined = combine(rank_cols, results, rows, capacity)[0]
    (combined,) = cot_steps.tie([combined])
    cot_blocks = cot_steps.blocks()
    cot_blocks[0] = after(cot_blocks[0], combined)
    result_steps = RingScatter(combined)
    result_steps.step()
    rows_cot = dispatch(cot_blocks, rank, capacity)[0]
    rows_cot = dispatch(cot_blocks, rank, capacity)[0]
    backs, gate_w_grads = {}, {}
    cot_now = rows_cot
    calls = halves[:0:-1] + [(1, halves[0][1][1:]), (0, halves[0][1][:1])]
    for first, these in calls:
        at = first // 2
        (cot_now,) = result_steps.tie([cot_now], gate_hand[1 - first] if first < 2 else ())
        result_steps.step()
        back = [*expert_call(
            backward_kernel, "expert_backward", first, cot_now, [gates_low[at], ups_low[at], acts[at]],
            these, [inner, inner, width], 1, rank_rows, gate_rows, capacity, first % 2,
        )]
        (back[2],) = result_steps.tie([back[2]], (), gate_hand[1 - first] if first < 2 else ())
        cot_now = after(cot_now, back[2])
        for k in range(len(these)):
            backs[first + k] = [back[0][k], back[1][k], back[2], back[3]]
        if first >= 2:
            for k in (first + 1, first):
                gate_w_grads[k] = dot(backs[k][0], rows_in[k], ((0,), (0,))).astype(BF16)
                cot_now = after(cot_now, gate_w_grads[k])
            gate_sums_far = expert_sums(gate_w_grads, range(2, experts, 2)) if first == 2 else None
            gate_hand = [hand_far(lambda: gate_sums_far, i, PARTS) for i in range(PARTS)]
    grad_gates, grad_ups = [[backs[k][i] for k in range(experts)] for i in range(2)]
    groups = [0, 1] + list(range(2, experts, 2))
    grads, gate_sums = [[backs[k][i] for k in groups] for i in (2, 3)]
    acts = [item[i] for item in acts for i in range(2)]
    gate_sums = jnp.concatenate(gate_sums, axis=0).transpose(1, 0, 2)
    grads = begin(grads[:1], gate_hand[2]) + grads[1:]
    combined, mlp_part = combine(
        rank_cols, grads, rows, capacity, (gate_sums, gates_mlp, router_rows, hidden2)
    )
    result_rows = result_steps.total()
    output = (middle + result_rows).astype(BF16)
    up_w_grads, down_w_grads = {}, {}

    def weight_grad(into, left, right, k, late):
        into[k] = dot(after(left[k], late), right[k], ((0,), (0,))).astype(BF16)
        return into[k]

    gate_back = Transfer(
        lambda v: shard_exchange(v.reshape(inner, shards, depth).transpose(1, 0, 2)),
        lambda: gate_total,
    )
    up_back = Transfer(shard_exchange, lambda: up_total)
    ring = RingScatter(combined)
    (late,) = ring.tie([after(rank, result_rows)], (), gate_hand[2])
    (late,) = ring.tie([late], gate_hand[3])
    for k in range(experts - 1, 3, -1):
        weight_grad(up_w_grads, grad_ups, rows_in, k, late)
    ring.step()
    weight_grad(up_w_grads, grad_ups, rows_in, 3, late)
    (late,) = ring.tie([late], (), [up_w_grads[3]])
    ring.step()
    weight_grad(up_w_grads, grad_ups, rows_in, 2, late)
    (late,) = ring.tie([late], (), [up_w_grads[2]] + gate_hand[3])
    ring.step()
    up_sums_far = expert_sums(up_w_grads, range(2, experts, 2))
    up_hand = [hand_far(lambda: up_sums_far, i, PARTS) for i in range(PARTS)]
    weight_grad(gate_w_grads, grad_gates, rows_in, 1, late)
    (late,) = ring.tie([late], (), [gate_w_grads[1], *up_sums_far])
    ring.step()
    weight_grad(gate_w_grads, grad_gates, rows_in, 0, late)
    gate_near = expert_sums(gate_w_grads, [0])[0].astype(F32)
    (late,) = ring.tie([late], (), [gate_w_grads[0]])
    back_rows = ring.total()
    grad_hidden2 = back_rows
    grad_middle, grad_gain2 = norm_back(grad_hidden2, middle, row_scale2, norm2_gain)
    grad_middle = grad_middle + cotangent.astype(F32)

    gate_total = total_of(gate_near, gate_hand).astype(BF16)
    gate_total = total_of(gate_near, gate_hand).astype(BF16)
    ring = RingGather(grad_middle.astype(BF16))
    (late,) = ring.tie([late], [gate_back] + up_hand[0] + up_hand[1])
    ring.step()
    weight_grad(up_w_grads, grad_ups, rows_in, 1, late)
    weight_grad(down_w_grads, acts, rows_cot, 1, late)
    (late,) = ring.tie([late], (), [up_w_grads[1], down_w_grads[1]] + up_hand[0] + up_hand[1])
    (late,) = ring.tie([late], up_hand[2] + up_hand[3])
    ring.step()
    weight_grad(up_w_grads, grad_ups, rows_in, 0, late)
    up_near = expert_sums(up_w_grads, [0])[0].astype(F32)
    for k in [*range(experts - 1, 1, -1), 0]:
        weight_grad(down_w_grads, acts, rows_cot, k, late)
    down_sums_far = expert_sums(down_w_grads, range(2, experts, 2))
    down_hand = [hand_far(lambda: down_sums_far, i, PARTS) for i in range(PARTS)]
    (late,) = ring.tie([late], (), [up_w_grads[0], down_w_grads[0], *down_sums_far, gate_back] + up_hand[2] + up_hand[3])
    (late,) = ring.tie([late], down_hand[0])
    ring.step()
    up_total = total_of(up_near, up_hand).astype(BF16)
    up_total = up_total.reshape(inner, shards, depth).transpose(1, 0, 2)
    (late,) = ring.tie([late], (), [up_total] + down_hand[0])
    ring.step()
    (late,) = ring.tie([late])
    mid_blocks = ring.blocks()
    mid_blocks = begin(mid_blocks, [up_back] + down_hand[1] + down_hand[2] + down_hand[3])
    grad_rows1, grad_first, attn_part, grad_mid = attend_back(
        mid_blocks, first_all, kv_w, attn_out_w, router_wide, hidden1, routes_attn, order[None], gates_attn, bounds,
        places[:, None], cosine, sine_table, query, keys, values, vec_wide,
    )
    grad_rows1, grad_first, attn_part, late = tie(
        [grad_rows1, grad_first, attn_part, late], down_hand[1] + down_hand[2] + down_hand[3]
    )
    sums = jnp.concatenate(
        [
            jnp.sum(attn_part[-8:], axis=0, keepdims=True) / norm1_gain,
            grad_gain2[None],
            jnp.take(attn_part, inverse, axis=0),
            jnp.take(mlp_part, inverse, axis=0),
        ],
        axis=0,
    )
    rounds = [("expert", step) for step in powers(experts)] + [("shard", step) for step in powers(shards)]
    small = []
    for i, (axis, step) in enumerate(rounds):
        source = (lambda: sums) if i == 0 else (lambda i=i: small[i - 1].value)
        small.append(Transfer(lambda v, axis=axis, step=step: sum_pairs(v, axis, step), source))
    ring = RingScatter(grad_rows1)
    late, grad_first = ring.tie([late, grad_first], small[:1])
    ring.step()
    grad_first_w = dot(hidden1, grad_first, ((0,), (0,))).astype(BF16)
    first_sums = first_parts(grad_first_w)
    first_hand = [hand_far(lambda: first_sums[1:], i, 2) for i in range(2)]
    (late,) = tie([late], [grad_first_w] + small[:1])
    (late,) = begin([late], small[1:2])
    (late,) = ring.tie([late], (), [up_back] + first_sums + small[1:2])
    (late,) = ring.tie([late], first_hand[0] + small[2:3])
    ring.step()
    (late,) = ring.tie([late], (), first_hand[0] + small[2:3])
    (late,) = ring.tie([late], first_hand[1] + small[3:4])
    ring.step()
    ring.step()
    grad_second_w = dot(after(vec_wide, late), grad_mid, ((0,), (0,))).astype(BF16)
    (late,) = ring.tie([late], (), first_hand[1] + small[3:4] + [grad_second_w])
    came = [jnp.concatenate([a.value, b.value], axis=0) for a, b in zip(*first_hand)]
    first_grad = sum_f32(first_sums[:1] + came).astype(BF16)
    first_back = Transfer(shard_exchange, lambda: first_grad)
    second_sums = expert_sums(jnp.split(grad_second_w, experts, axis=0), range(0, experts, 2))
    second_hand = hand_far(lambda: second_sums[1:])
    ring.tie([], [first_back])
    came_back = [gate_back, up_back] + [item for part in down_hand for item in part]
    for item, value in zip(came_back, begin([item.value for item in came_back], second_hand)):
        item.value = value
    for item in small[4:]:
        (late,) = tie(begin([late], [item]), [item])
    back_rows1 = ring.total()
    in_grad = join_columns(gate_back.value, up_back.value)[None]
    attn_grad = sum_f32(second_sums[:1] + [item.value for item in second_hand])[None]
    out_grad = total_of(expert_sums(down_w_grads, [0])[0].astype(F32), down_hand)[None]
    sums = small[-1].value
    grad_hidden1 = back_rows1
    grad_stream, _ = norm_back(grad_hidden1, stream, row_scale1, norm1_gain)
    grad_input = grad_stream + grad_middle

    first_grad = first_back.value
    query_grad = first_grad[:, :depth].transpose(1, 0, 2).reshape(1, depth, shards * span).astype(F32)
    kv_grad = first_grad[:, depth:].reshape(shards, 2, chunk, span)
    kv_grad = kv_grad.transpose(2, 1, 0, 3).reshape(chunk, 2 * shards * span)
    pieces = expert_gather(kv_grad.astype(BF16))
    kv_grad = jnp.zeros((depth, 2 * shards * span), F32)
    for k, piece in enumerate(pieces):
        kv_grad = lax.dynamic_update_slice_in_dim(kv_grad, piece.astype(F32), order[k] * chunk, axis=0)

    return (
        output,
        grad_input,
        sums[0],
        kv_grad,
        query_grad,
        attn_grad,
        sums[2 : 2 + experts].T,
        sums[1],
        in_grad,
        out_grad,
        sums[2 + experts :].T,
    )


def solution(mesh):
    return jax.shard_map(
        body,
        mesh=mesh,
        in_specs=(
            P(("expert", "shard"), None),
            P(("expert", "shard"), None),
            P(),
            P("shard", None),
            P("expert", "shard", None),
            P("expert", "shard", None),
            P(),
            P(),
            P("expert", "shard", None),
            P("expert", "shard", None),
            P(),
            P(("expert", "shard"), None),
            P(("expert", "shard"), None),
            P("expert", "shard"),
            P("expert", None),
        ),
        out_specs=(
            P(("expert", "shard"), None),
            P(("expert", "shard"), None),
            P(),
            P("shard", None),
            P("expert", "shard", None),
            P("expert", "shard", None),
            P(),
            P(),
            P("expert", "shard", None),
            P("expert", "shard", None),
            P(),
        ),
        check_vma=False,
    )
```

```python
import functools

import jax
import jax.numpy as jnp
from jax import lax
from jax.experimental import pallas as pl
from jax.experimental.pallas import tpu as pltpu
from jax.sharding import PartitionSpec as P

HD = 128


EPS = 1e-05
THETA = 10000.0
NEG = -1e30
F32 = jnp.float32
BF16 = jnp.bfloat16
VMEM_LIMIT = 60 * 1024 * 1024


def dot(left, right, contract=((1,), (0,))):
    return lax.dot_general(left, right, (contract, ((), ())), preferred_element_type=F32)


def norm_rows(values, norm_gain):
    row_scale = lax.rsqrt(jnp.mean(values * values, axis=-1, keepdims=True) + EPS)
    return (values * row_scale * norm_gain, row_scale)


def norm_back(grad_rows, values, row_scale, norm_gain):
    gain_grad = jnp.sum(grad_rows * values * row_scale, axis=0)
    scaled_grad = grad_rows * norm_gain
    mean_term = jnp.mean(scaled_grad * values, axis=-1, keepdims=True)
    return (
        row_scale * scaled_grad - values * row_scale * row_scale * row_scale * mean_term,
        gain_grad,
    )


def seq_of(places, lengths):
    seq_ends = jnp.cumsum(lengths)
    passed = seq_ends[None, :] <= places[:, None]
    return (passed, jnp.sum(passed.astype(jnp.int32), axis=1))


def rope_tables(places, lengths):
    passed, seq_ids = seq_of(places, lengths)
    starts = jnp.sum(jnp.where(passed, lengths[None, :], 0), axis=1)
    where_in = (places - starts).astype(F32)
    frequency = THETA ** (-jnp.arange(0, HD // 2, dtype=F32) * (2.0 / HD))
    angles = where_in[:, None] * frequency[None, :]
    return (jnp.cos(angles), jnp.sin(angles), seq_ids)


def rotate(values, cosine, sine_table):
    half_width = values.shape[-1] // 2
    leading = values[..., :half_width]
    trailing = values[..., half_width:]
    return jnp.concatenate(
        [leading * cosine - trailing * sine_table, trailing * cosine + leading * sine_table],
        axis=-1,
    )


def ring_cycle(count):
    if count == 8:
        return [0, 2, 4, 6, 7, 5, 3, 1]
    if count == 16:
        return [0, 1, 2, 3, 7, 6, 5, 9, 10, 11, 15, 14, 13, 12, 8, 4]
    return list(range(count))


def ring_move(value, hops):
    cycle = ring_cycle(lax.axis_size("shard"))
    count = len(cycle)
    return lax.ppermute(
        value, "shard", [(cycle[i], cycle[(i + hops) % count]) for i in range(count)]
    )


def after(value, *others):
    return lax.optimization_barrier((value,) + others)[0] if others else value


class Transfer:
    def __init__(self, move, source, value=None):
        self.move, self.source, self.value = move, source, value

    def begin(self):
        self.value = self.move(self.value)


def tie(values, others):
    if len(values) + len(others) < 2:
        return list(values)
    held = [item.value if isinstance(item, Transfer) else item for item in others]
    tied = lax.optimization_barrier((*values, *held))
    for item, value in zip(others, tied[len(values) :]):
        if isinstance(item, Transfer):
            item.value = value
    return list(tied[: len(values)])


def begin(values, transfers):
    for item in transfers:
        item.value = item.source()
    values = tie(values, transfers)
    for item in transfers:
        item.begin()
    return values


class RingGather:
    def __init__(self, block):
        self.ahead, self.behind = [block], [block]
        self.last = []

    def tie(self, values, begins=(), ends=()):
        heads = self.last or [self.ahead[-1], self.behind[-1]]
        for item in begins:
            item.value = item.source()
        tied = tie([*heads, *values], [*begins, *ends])
        if self.last:
            self.last = tied[:2]
        else:
            self.ahead[-1], self.behind[-1] = tied[:2]
        for item in begins:
            item.begin()
        return tied[2:]

    def step(self):
        far = lax.axis_size("shard") // 2
        if len(self.ahead) < far:
            self.ahead.append(ring_move(self.ahead[-1], 1))
            self.behind.append(ring_move(self.behind[-1], -1))
        elif not self.last:
            cut = self.ahead[0].shape[0] // 2
            self.last = [ring_move(self.ahead[-1][:cut], 1), ring_move(self.behind[-1][cut:], -1)]

    def blocks(self):
        while not self.last:
            self.step()
        return self.ahead + self.last + self.behind[:0:-1]


class RingScatter:
    def __init__(self, partial):
        count = lax.axis_size("shard")
        rows = partial.shape[0] // count
        self.far, self.done = count // 2, 0
        self.part = [partial[r * rows : (r + 1) * rows] for r in range(count)]
        cut = rows // 2
        self.back, self.fore = self.part[self.far][:cut], self.part[self.far][cut:]

    def tie(self, values, begins=(), ends=()):
        for item in begins:
            item.value = item.source()
        tied = tie([self.back, self.fore, *values], [*begins, *ends])
        self.back, self.fore = tied[:2]
        for item in begins:
            item.begin()
        return tied[2:]

    def step(self):
        if self.done == self.far:
            return
        self.back, self.fore = ring_move(self.back, -1), ring_move(self.fore, 1)
        if self.done == 0:
            empty = jnp.zeros_like(self.back)
            self.back = jnp.concatenate([self.back, empty], axis=0)
            self.fore = jnp.concatenate([empty, self.fore], axis=0)
        if self.done < self.far - 1:
            self.back = self.part[self.far - 1 - self.done] + self.back
            self.fore = self.part[self.far + 1 + self.done] + self.fore
        self.done += 1

    def total(self):
        while self.done < self.far:
            self.step()
        return self.part[0].astype(F32) + self.back.astype(F32) + self.fore.astype(F32)


def ring_gather(block, plan={}):
    ring = RingGather(block)
    for step in range(lax.axis_size("shard") // 2):
        begins, ends = plan.get(step, ((), ()))
        ring.tie([], begins)
        ring.step()
        ring.tie([], (), ends)
    return ring.blocks()


def ring_scatter(partial, plan={}):
    ring = RingScatter(partial)
    for step in range(lax.axis_size("shard") // 2):
        begins, ends = plan.get(step, ((), ()))
        ring.tie([], begins)
        ring.step()
        ring.tie([], (), ends)
    return ring.total()


def doubled(value, step):
    count = lax.axis_size("shard")
    return jnp.concatenate([value, lax.ppermute(value, "shard", [(i, i ^ step) for i in range(count)])])


def ring_sorted(blocks):
    cycle = ring_cycle(lax.axis_size("shard"))
    own = lax.axis_index("shard")
    spot = jnp.array([cycle.index(s) for s in range(len(cycle))])[own]
    return jnp.take(blocks, own ^ jnp.array(cycle)[(spot - jnp.arange(len(cycle))) % len(cycle)], axis=0)


def core_swap(value):
    return lax.ppermute(value, "expert", [(i, i ^ 1) for i in range(lax.axis_size("expert"))])


def chip_shift(value, hops):
    count = lax.axis_size("expert")
    chips = count // 2
    return lax.ppermute(
        value, "expert", [(i, (i // 2 + hops) % chips * 2 + i % 2) for i in range(count)]
    )


def expert_order():
    index = lax.axis_index("expert")
    chips = lax.axis_size("expert") // 2
    return [
        (index // 2 + dx) % chips * 2 + (index % 2 + dc) % 2
        for dx in range(chips)
        for dc in range(2)
    ]


def expert_gather(value):
    chips = lax.axis_size("expert") // 2
    own = [value] + [chip_shift(value, -dx) for dx in range(1, chips)]
    return [piece for item in own for piece in (item, core_swap(item))]


def after_all(values, *others):
    return [after(item, *others) for item in values]


PARTS = 4
PAIR = 2


def part_of(value, which, parts=PARTS):
    size = value.shape[1 if value.ndim == 2 else 0] // parts
    here = slice(which * size, (which + 1) * size)
    return value[:, here] if value.ndim == 2 else value[here]


def fetch_far(source, which=0, parts=1):
    chips = lax.axis_size("expert") // 2
    take = lambda: part_of(source(), which, parts)
    return [Transfer(lambda v, dx=dx: chip_shift(v, -dx), take) for dx in range(1, chips)]


def hand_far(source, which=0, parts=1):
    chips = lax.axis_size("expert") // 2
    return [
        Transfer(
            lambda v, dx=dx: chip_shift(v, dx), lambda dx=dx: part_of(source()[dx - 1], which, parts)
        )
        for dx in range(1, chips)
    ]


def total_of(near, parts):
    came = [sum_f32([item.value for item in part]) for part in parts]
    return near + jnp.concatenate(came, axis=1)


def with_swaps(items):
    return [piece for item in items for piece in (item, core_swap(item))]


def expert_sums(pieces, firsts):
    return [
        (pieces[k].astype(F32) + core_swap(pieces[k + 1]).astype(F32)).astype(BF16) for k in firsts
    ]


def far_exchange(sums):
    return [chip_shift(item, dx + 1) for dx, item in enumerate(sums)]


def sum_f32(parts):
    return sum(item.astype(F32) for item in parts)


def expert_reduce(pieces):
    sums = expert_sums(pieces, range(0, len(pieces), 2))
    return sum_f32(sums[:1] + far_exchange(sums[1:]))


def shard_exchange(pieces):
    return lax.all_to_all(pieces, "shard", split_axis=0, concat_axis=0, tiled=True)


def sum_pairs(value, axis, step):
    count = lax.axis_size(axis)
    return value + lax.ppermute(value, axis, [(i, i ^ step) for i in range(count)])


def powers(count):
    return [1 << i for i in range(count.bit_length() - 1)]


def turn(values, cosine, sine_table):
    return values * cosine + pltpu.roll(values, HD // 2, 1) * sine_table


def whole(shape):
    zeros = (0,) * len(shape)
    return pl.BlockSpec(shape, lambda *_: zeros, pipeline_mode=pl.Buffered(1))


def tiles(shape):
    return pl.BlockSpec(shape, lambda i: (i,) + (0,) * (len(shape) - 1))


def named_by(routes, order, slot, k):
    return (routes[:, slot : slot + 1] == order[0, k]).astype(F32)


def columns(parts):
    lane = lax.broadcasted_iota(jnp.int32, (parts[0].shape[0], len(parts)), 1)
    total = jnp.zeros(lane.shape, F32)
    for k, part in enumerate(parts):
        total = jnp.where(lane == k, part, total)
    return total


def lay(blocks, target):
    start = 0
    for block in blocks:
        target[start : start + block.shape[0], :] = block[...]
        start += block.shape[0]


def cost(microseconds):
    return pl.CostEstimate(flops=microseconds * 115 * 10**6, bytes_accessed=1 << 16, transcendentals=0)


def attend_kernel(layout, count, chunk, order, *refs):
    blocks, refs = refs[:count], refs[count:]
    (first_w,), refs = regroup(refs, [layout])
    experts = len(layout)
    out_w, refs = refs[:experts], refs[experts:]
    router, routes_ref, bounds, place_row, cosine, sine_table = refs[:6]
    mixed, query_out, keys, values, wide, gates_out, hidden, kv_w = refs[6:]
    step = pl.program_id(0)
    tile = mixed.shape[0]
    total_rows, span = keys.shape
    width = hidden.shape[1]
    shards = sum(piece.shape[0] for piece in first_w[0])
    depth = width // shards

    @pl.when(step == 0)
    def _():
        lay(blocks, hidden)
        for k in range(experts):
            for s, block in enumerate([piece.at[i] for piece in first_w[k] for i in range(piece.shape[0])]):
                to = pl.ds(pl.multiple_of(s * depth + order[0, k] * chunk, chunk), chunk)
                for half in range(2):
                    kv_w[half, to, :] = block[depth + half * chunk : depth + (half + 1) * chunk, :]

        @pl.loop(0, total_rows // tile)
        def _(i):
            here = pl.ds(pl.multiple_of(i * tile, tile), tile)
            raw = dot(hidden[here, :], kv_w[0])
            for h in range(span // HD):
                cols = slice(h * HD, (h + 1) * HD)
                keys[here, cols] = turn(raw[:, cols], cosine[here, :], sine_table[here, :]).astype(BF16)
            values[here, :] = dot(hidden[here, :], kv_w[1]).astype(BF16)

    here = pl.ds(pl.multiple_of(step * tile, tile), tile)
    rows_in = hidden[here, :]
    routes = routes_ref[...]
    hot = [[named_by(routes, order, j, k) for k in range(experts)] for j in range(2)]
    logits = dot(rows_in, router[...])
    picked = [sum(hot[j][k] * logits[:, k : k + 1] for k in range(experts)) for j in range(2)]
    top = jnp.maximum(picked[0], picked[1])
    raised = [jnp.exp(value - top) for value in picked]
    gates = [value / (raised[0] + raised[1]) for value in raised]
    gates_out[...] = columns([hot[0][k] * gates[0] + hot[1][k] * gates[1] for k in range(experts)])
    query_all = []
    for pieces in first_w:
        at, total = 0, 0.0
        for piece in pieces:
            size = piece.shape[0] * depth
            total = total + dot(rows_in[:, at : at + size], piece[:, :depth, :].reshape(size, span))
            at += size
        query_all.append(total)
    allowed = (place_row[...] >= bounds[:, 0:1]) & (place_row[...] <= bounds[:, 1:2])
    cos_here, sin_here = cosine[here, :], sine_table[here, :]
    vectors = []
    for j in range(2):
        raw = sum(hot[j][k] * query_all[k] for k in range(experts))
        heads = []
        for h in range(span // HD):
            cols = slice(h * HD, (h + 1) * HD)
            query = turn(raw[:, cols], cos_here, sin_here).astype(BF16)
            query_out[:, j * span + h * HD : j * span + (h + 1) * HD] = query
            scores = dot(query, keys[:, cols], ((1,), (1,))) * HD**-0.5
            scores = jnp.where(allowed, scores, NEG)
            row_top = jnp.max(scores, axis=1, keepdims=True)
            exp_scores = jnp.exp(scores - row_top)
            row_total = jnp.sum(exp_scores, axis=1, keepdims=True)
            heads.append(dot(exp_scores.astype(BF16), values[:, cols]) / row_total)
        vectors.append((jnp.concatenate(heads, axis=1) if len(heads) > 1 else heads[0]) * gates[j])
    total = 0.0
    for k in range(experts):
        part = (hot[0][k] * vectors[0] + hot[1][k] * vectors[1]).astype(BF16)
        wide[:, k * span : (k + 1) * span] = part
        total = total + dot(part, out_w[k][...])
    mixed[...] = total.astype(BF16)


def attend(blocks, first_w, out_w, router, routes, order, bounds, place_row, cosine, sine_table, chunk):
    total_rows, width = routes.shape[0], blocks[0].shape[1]
    experts = len(first_w)
    span = first_w[0][0].shape[2]
    layout = [len(pieces) for pieces in first_w]
    first_w = [piece for pieces in first_w for piece in pieces]
    tile = 256

    def struct(*shape):
        return jax.ShapeDtypeStruct(shape, BF16)

    return pl.pallas_call(
        functools.partial(attend_kernel, layout, len(blocks), chunk),
        grid=(total_rows // tile,),
        in_specs=[pl.BlockSpec(memory_space=pltpu.SMEM)]
        + [whole(w.shape) for w in [*blocks, *first_w, *out_w, router]]
        + [
            tiles((tile, 2)),
            tiles((tile, 2)),
            whole(place_row.shape),
            whole(cosine.shape),
            whole(sine_table.shape),
        ],
        out_specs=[
            tiles((tile, width)),
            tiles((tile, 2 * span)),
            whole((total_rows, span)),
            whole((total_rows, span)),
            tiles((tile, experts * span)),
            tiles((tile, experts)),
            whole((total_rows, width)),
            whole((2, width, span)),
        ],
        out_shape=[
            struct(total_rows, width),
            struct(total_rows, 2 * span),
            struct(total_rows, span),
            struct(total_rows, span),
            struct(total_rows, experts * span),
            jax.ShapeDtypeStruct((total_rows, experts), F32),
            struct(total_rows, width),
            struct(2, width, span),
        ],
        compiler_params=pltpu.CompilerParams(vmem_limit_bytes=VMEM_LIMIT),
        cost_estimate=cost(35),
        name="attend",
    )(order, *blocks, *first_w, *out_w, router, routes, bounds, place_row, cosine, sine_table)


def attend_back_kernel(layout, steps, count, order, *refs):
    blocks, refs = refs[:count], refs[count:]
    (first_w,), refs = regroup(refs, [layout])
    experts = len(layout)
    kv_w, refs = refs[0], refs[1:]
    out_w, refs = refs[:experts], refs[experts:]
    router, hidden, refs = refs[0], refs[1], refs[2:]
    routes_ref, gates_ref, bounds_row, place_col, cosine, sine_table, query_ref, keys, values, wide = refs[:10]
    grad_rows, grad_first, small, grad_mid, key_sum, value_sum, logit_grads = refs[10:]
    step = pl.program_id(0)
    tile = grad_rows.shape[0]
    total_rows, span = keys.shape

    @pl.when(step == 0)
    def _():
        lay(blocks, grad_mid)
        small[...] = jnp.zeros_like(small)
        key_sum[...] = jnp.zeros_like(key_sum)
        value_sum[...] = jnp.zeros_like(value_sum)

    @pl.when(step < steps)
    def _():
        here = pl.ds(pl.multiple_of(step * tile, tile), tile)
        routes = routes_ref[here, :]
        gates = gates_ref[here, :]
        hot = [[named_by(routes, order, j, k) for k in range(experts)] for j in range(2)]
        allowed = (place_col[...] >= bounds_row[0:1, here]) & (place_col[...] <= bounds_row[1:2, here])
        rows_in = grad_mid[here, :]
        slot_grads = [0.0, 0.0]
        sums = []
        for k in range(experts):
            grad = dot(rows_in, out_w[k][...], ((1,), (1,)))
            part = wide[:, k * span : (k + 1) * span].astype(F32)
            sums.append(jnp.sum(part * grad, axis=1, keepdims=True))
            for j in range(2):
                slot_grads[j] = slot_grads[j] + (hot[j][k] * gates[:, k : k + 1]) * grad
        sums = columns(sums)
        wide_grads = sums - gates * jnp.sum(sums, axis=1, keepdims=True)
        wide_grads = jnp.concatenate([wide_grads, jnp.zeros((tile, HD - experts), F32)], axis=1)
        logit_grads[here, :] = wide_grads.astype(BF16)
        cos_here, sin_here = cosine[here, :], sine_table[here, :]
        slot_queries = []
        for j in range(2):
            heads = []
            for h in range(span // HD):
                cols = slice(h * HD, (h + 1) * HD)
                query = query_ref[:, j * span + h * HD : j * span + (h + 1) * HD]
                grad = slot_grads[j][:, cols].astype(BF16)
                scores = dot(keys[:, cols], query, ((1,), (1,))) * HD**-0.5
                scores = jnp.where(allowed, scores, NEG)
                exp_scores = jnp.exp(scores - jnp.max(scores, axis=0, keepdims=True))
                probs = exp_scores * (1.0 / jnp.sum(exp_scores, axis=0, keepdims=True))
                value_sum[:, cols] += dot(probs.astype(BF16), grad)
                grad_probs = dot(values[:, cols], grad, ((1,), (1,)))
                mean = jnp.sum(probs * grad_probs, axis=0, keepdims=True)
                grad_scores = (probs * (grad_probs - mean)).astype(BF16)
                key_sum[:, cols] += dot(grad_scores, query)
                grad_query = dot(grad_scores, keys[:, cols], ((0,), (0,))) * HD**-0.5
                heads.append(turn(grad_query, cos_here, -sin_here))
            slot_queries.append(jnp.concatenate(heads, axis=1) if len(heads) > 1 else heads[0])
        for k in range(experts):
            grad_first[here, k * span : (k + 1) * span] = (
                hot[0][k] * slot_queries[0] + hot[1][k] * slot_queries[1]
            ).astype(BF16)

    @pl.when(step == steps - 1)
    def _():
        for h in range(span // HD):
            cols = slice(h * HD, (h + 1) * HD)
            grad_first[:, experts * span + h * HD : experts * span + (h + 1) * HD] = turn(
                key_sum[:, cols] * HD**-0.5, cosine[...], -sine_table[...]
            ).astype(BF16)
        grad_first[:, (experts + 1) * span :] = value_sum[...].astype(BF16)

    @pl.when(step >= steps)
    def _():
        here = pl.ds(pl.multiple_of((step - steps) * tile, tile), tile)
        total = dot(grad_first[here, experts * span : (experts + 1) * span], kv_w[0], ((1,), (1,)))
        total = total + dot(grad_first[here, (experts + 1) * span :], kv_w[1], ((1,), (1,)))
        total = total + dot(logit_grads[here, :], router[...], ((1,), (1,)))
        width = total.shape[1]
        depth = width // sum(piece.shape[0] for piece in first_w[0])
        for k, pieces in enumerate(first_w):
            grad = grad_first[here, k * span : (k + 1) * span]
            back = [
                dot(grad, piece[:, :depth, :].reshape(piece.shape[0] * depth, span), ((1,), (1,)))
                for piece in pieces
            ]
            total = total + (jnp.concatenate(back, axis=1) if len(back) > 1 else back[0])
        grad_rows[...] = total.astype(BF16)
        rows_in = hidden[...]
        small[:-8, :] += dot(logit_grads[here, :], rows_in, ((0,), (0,)))[: small.shape[0] - 8, :]
        small[-8:, :] += jnp.sum((total * rows_in.astype(F32)).reshape(-1, 8, total.shape[1]), axis=0)


def attend_back(
    blocks, first_w, kv_w, out_w, router, hidden, routes, order, gates, bounds_row, place_col, cosine,
    sine_table, query, keys, values, wide,
):
    small_rows = -(-len(first_w) // 8) * 8 + 8
    total_rows, width = routes.shape[0], blocks[0].shape[1]
    experts = len(first_w)
    span = first_w[0][0].shape[2]
    layout = [len(pieces) for pieces in first_w]
    first_w = [piece for pieces in first_w for piece in pieces]
    tile = 256 if total_rows <= 1024 else 128
    steps = total_rows // tile

    def early(shape):
        return pl.BlockSpec(shape, lambda i: (jnp.minimum(i, steps - 1), 0))

    return pl.pallas_call(
        functools.partial(attend_back_kernel, layout, steps, len(blocks)),
        grid=(2 * steps,),
        in_specs=[pl.BlockSpec(memory_space=pltpu.SMEM)]
        + [whole(w.shape) for w in [*blocks, *first_w, kv_w, *out_w, router]]
        + [pl.BlockSpec((tile, width), lambda i: (jnp.maximum(i - steps, 0), 0))]
        + [
            whole(routes.shape),
            whole(gates.shape),
            whole(bounds_row.shape),
            whole(place_col.shape),
            whole(cosine.shape),
            whole(sine_table.shape),
            early((tile, 2 * span)),
            whole(keys.shape),
            whole(values.shape),
            early((tile, experts * span)),
        ],
        out_specs=[
            pl.BlockSpec((tile, width), lambda i: (jnp.maximum(i - steps, 0), 0)),
            whole((total_rows, (experts + 2) * span)),
            whole((small_rows, width)),
            whole((total_rows, width)),
        ],
        out_shape=[
            jax.ShapeDtypeStruct((total_rows, width), BF16),
            jax.ShapeDtypeStruct((total_rows, (experts + 2) * span), BF16),
            jax.ShapeDtypeStruct((small_rows, width), F32),
            jax.ShapeDtypeStruct((total_rows, width), BF16),
        ],
        scratch_shapes=[
            pltpu.VMEM((total_rows, span), F32),
            pltpu.VMEM((total_rows, span), F32),
            pltpu.VMEM((total_rows, HD), BF16),
        ],
        compiler_params=pltpu.CompilerParams(vmem_limit_bytes=VMEM_LIMIT),
        cost_estimate=cost(45),
        name="attend_back",
    )(
        order, *blocks, *first_w, kv_w, *out_w, router, hidden, routes, gates, bounds_row, place_col, cosine,
        sine_table, query, keys, values, wide,
    )


def split_kernel(block, gate, up):
    half = block.shape[1] // 2
    gate[...] = block[:, :half].T.reshape(gate.shape)
    up[...] = block[:, half:].T.reshape(up.shape)


def split_columns(weight, shards):
    depth, both = weight.shape
    inner = both // (2 * shards)
    tile = 128
    out = jax.ShapeDtypeStruct((shards, inner, depth), BF16)
    spec = pl.BlockSpec((shards, inner, tile), lambda i: (0, 0, i))
    return pl.pallas_call(
        split_kernel,
        grid=(depth // tile,),
        in_specs=[tiles((tile, both))],
        out_specs=[spec, spec],
        out_shape=[out, out],
        compiler_params=pltpu.CompilerParams(vmem_limit_bytes=VMEM_LIMIT),
        cost_estimate=cost(5),
        name="split_columns",
    )(weight)


def join_kernel(gate, up, out):
    shards, inner, tile = gate.shape
    half = shards * inner
    out[:, :half] = gate[...].reshape(half, tile).T.astype(F32)
    out[:, half:] = up[...].reshape(half, tile).T.astype(F32)


def join_columns(gate, up):
    shards, inner, depth = gate.shape
    tile = 128
    spec = pl.BlockSpec((shards, inner, tile), lambda i: (0, 0, i))
    return pl.pallas_call(
        join_kernel,
        grid=(depth // tile,),
        in_specs=[spec, spec],
        out_specs=tiles((tile, 2 * shards * inner)),
        out_shape=jax.ShapeDtypeStruct((depth, 2 * shards * inner), F32),
        compiler_params=pltpu.CompilerParams(vmem_limit_bytes=VMEM_LIMIT),
        cost_estimate=cost(7),
        name="join_columns",
    )(gate, up)


def dispatch_kernel(capacity, count, gated, rank, *refs):
    blocks, refs = refs[:count], refs[count:]
    if gated:
        router, out, gates_out, hidden = refs
    else:
        out, hidden = refs
    step = pl.program_id(0)
    _, experts, rows = rank.shape

    @pl.when(step == 0)
    def _():
        lay(blocks, hidden)

    rows_in = hidden[pl.ds(pl.multiple_of(step * rows, rows), rows), :]
    ranks = rank[0]
    slot = lax.broadcasted_iota(jnp.int32, (capacity, rows), 0)
    pick = jnp.concatenate([(slot == ranks[k : k + 1, :]).astype(BF16) for k in range(experts)], axis=0)
    picked = dot(pick, rows_in).astype(BF16)
    for k in range(experts):
        out[k] = picked[k * capacity : (k + 1) * capacity, :]
    if gated:
        logits = dot(router[...], rows_in, ((1,), (1,)))[:experts, :]
        logits = jnp.where(ranks >= 0, logits, NEG)
        raised = jnp.where(ranks >= 0, jnp.exp(logits - jnp.max(logits, axis=0, keepdims=True)), 0.0)
        gates_out[0] = raised / jnp.sum(raised, axis=0, keepdims=True)


def dispatch(blocks, rank, capacity, router=None):
    shards, experts, rows = rank.shape
    width = blocks[0].shape[1]
    out_specs = [pl.BlockSpec((experts, capacity, width), lambda i: (0, i, 0))]
    out_shape = [jax.ShapeDtypeStruct((experts, shards * capacity, width), BF16)]
    extra = []
    if router is not None:
        extra = [router]
        out_specs += [tiles((1, experts, rows)), whole((shards * rows, width))]
        out_shape += [
            jax.ShapeDtypeStruct((shards, experts, rows), F32),
            jax.ShapeDtypeStruct((shards * rows, width), BF16),
        ]
    return pl.pallas_call(
        functools.partial(dispatch_kernel, capacity, len(blocks), router is not None),
        grid=(shards,),
        in_specs=[tiles((1, experts, rows))] + [whole(item.shape) for item in [*blocks, *extra]],
        out_specs=out_specs,
        out_shape=out_shape,
        scratch_shapes=[] if router is not None else [pltpu.VMEM((shards * rows, width), BF16)],
        compiler_params=pltpu.CompilerParams(vmem_limit_bytes=VMEM_LIMIT),
        cost_estimate=cost(10),
        name="dispatch",
    )(rank, *blocks, *extra)


class Fetch:
    def __init__(self, step, weights, store, sems):
        self.step, self.weights, self.store, self.sems = step, weights, store, sems

    def copies(self, index, which):
        made, slot = [], 0
        for i, pieces in enumerate(self.weights[index]):
            at = 0
            for piece in pieces:
                parts = [piece] if len(piece.shape) == 2 else [piece.at[s] for s in range(piece.shape[0])]
                for part in parts:
                    span = part.shape[1]
                    if i == which:
                        target = self.store.at[index % 2, i, :, at : at + span]
                        made.append(pltpu.make_async_copy(part, target, self.sems.at[index % 2, slot]))
                    at += span
                    slot += 1
        return made

    def start(self, sequence):
        count = len(self.weights)
        for index in range(count):

            @pl.when(self.step == index)
            def _():
                for ahead in [0, 1] if index == 0 else [index + 1]:
                    if ahead < count:
                        for i in sequence:
                            for copy in self.copies(ahead, i):
                                copy.start()

    def wait(self, i):
        for index in range(len(self.weights)):

            @pl.when(self.step == index)
            def _():
                for copy in self.copies(index, i):
                    copy.wait()


def regroup(refs, layout):
    groups, at = [], 0
    for expert in layout:
        groups.append([])
        for pieces in expert:
            groups[-1].append(refs[at : at + pieces])
            at += pieces
    return groups, refs[at:]


def row_scale(capacity, rank, gates):
    blocks, rows = rank.shape
    slot = lax.broadcasted_iota(jnp.int32, (capacity, rows), 0)
    return jnp.concatenate(
        [
            jnp.sum(jnp.where(slot == rank[b : b + 1, :], gates[b : b + 1, :], 0.0), axis=1, keepdims=True)
            for b in range(blocks)
        ],
        axis=0,
    )


def forward_kernel(capacity, layout, rank, gates, rows_in, *refs):
    weights, refs = regroup(refs, layout)
    count = len(layout)
    gate_out, up_out, act_out, result, store, sems = refs
    step = pl.program_id(0)
    fetch = Fetch(step, weights, store, sems)
    fetch.start((0, 1, 2))
    gate_w, up_w, down_w = [store.at[step % 2, i] for i in range(3)]
    scale = row_scale(capacity, rank[0], gates[0])
    slots = rows_in.shape[1]
    part = slots // 2
    for at in range(0, slots, part):
        here = slice(at, at + part)
        data = rows_in[0, here, :]
        if at == 0:
            fetch.wait(0)
        gate = dot(data, gate_w[...], ((1,), (1,)))
        if at == 0:
            fetch.wait(1)
        up = dot(data, up_w[...], ((1,), (1,)))
        act = (gate * jax.nn.sigmoid(gate) * up * scale[here, :]).astype(BF16)
        gate_out[0, here, :] = gate.astype(BF16)
        up_out[0, here, :] = up.astype(BF16)
        act_out[0, here, :] = act
        if at == 0:
            fetch.wait(2)
        result[0, here, :] = dot(act, down_w[...]).astype(BF16)


def backward_kernel(capacity, layout, rank, gates, cot, gate_ref, up_ref, act, *refs):
    weights, refs = regroup(refs, layout)
    count = len(layout)
    grad_gate_out, grad_up_out, grad_rows, gate_sums, store, sems = refs
    step = pl.program_id(0)
    fetch = Fetch(step, weights, store, sems)
    fetch.start((2, 0, 1))
    gate_w, up_w, down_w = [store.at[step % 2, i] for i in range(3)]
    scale = row_scale(capacity, rank[0], gates[0])
    slots = cot.shape[1]
    part = slots // 2
    blocks, rows = rank.shape[1:]
    slot = lax.broadcasted_iota(jnp.int32, (capacity, rows), 0)
    for at in range(0, slots, part):
        here = slice(at, at + part)
        if at == 0:
            fetch.wait(2)
        back = dot(cot[0, here, :], down_w[...], ((1,), (1,)))
        sums = jnp.sum(act[0, here, :].astype(F32) * back, axis=1, keepdims=True)
        for b in range(at // capacity, (at + part) // capacity):
            hit = slot == rank[0, b : b + 1, :]
            piece = sums[b * capacity - at : (b + 1) * capacity - at, :]
            gate_sums[0, b : b + 1, :] = jnp.sum(jnp.where(hit, piece, 0.0), axis=0, keepdims=True)
        gate = gate_ref[0, here, :].astype(F32)
        sigmoid_gate = jax.nn.sigmoid(gate)
        grad_act = back * scale[here, :]
        grad_up = (grad_act * gate * sigmoid_gate).astype(BF16)
        grad_gate = (
            grad_act * up_ref[0, here, :].astype(F32) * sigmoid_gate * (1.0 + gate * (1.0 - sigmoid_gate))
        ).astype(BF16)
        grad_up_out[0, here, :] = grad_up
        grad_gate_out[0, here, :] = grad_gate
        if at == 0:
            fetch.wait(0)
            fetch.wait(1)
        grad_rows[0, here, :] = (dot(grad_gate, gate_w[...]) + dot(grad_up, up_w[...])).astype(BF16)


def expert_call(
    kernel, name, first, rows_in, parts, weights, out_cols, sums, rank, gates, capacity, skip=0
):
    _, shards, rows = rank.shape
    width, inner = rows_in.shape[2], weights[0][0][0].shape[-2]
    count = len(weights)
    slots = shards * capacity
    layout = [[len(pieces) for pieces in group] for group in weights]
    flat = [piece for group in weights for pieces in group for piece in pieces]
    copies = 2 * shards + PARTS

    def of_all(shape):
        return pl.BlockSpec((1,) + shape, lambda i: (first + i, 0, 0))

    def of_these(shape):
        return pl.BlockSpec((1,) + shape, lambda i: (i, 0, 0))

    def of_parts(shape):
        return pl.BlockSpec((1,) + shape, lambda i: (skip + i, 0, 0))

    return pl.pallas_call(
        functools.partial(kernel, capacity, layout),
        grid=(count,),
        in_specs=[of_all((shards, rows)), of_all((shards, rows)), of_all((slots, width))]
        + [of_parts((slots, inner)) for _ in parts]
        + [pl.BlockSpec(memory_space=pl.ANY)] * len(flat),
        out_specs=[of_these((slots, cols)) for cols in out_cols] + [of_these((shards, rows))] * sums,
        out_shape=[jax.ShapeDtypeStruct((count, slots, cols), BF16) for cols in out_cols]
        + [jax.ShapeDtypeStruct((count, shards, rows), F32)] * sums,
        scratch_shapes=[pltpu.VMEM((2, 3, inner, width), BF16), pltpu.SemaphoreType.DMA((2, copies))],
        compiler_params=pltpu.CompilerParams(vmem_limit_bytes=VMEM_LIMIT),
        cost_estimate=cost(10 * count),
        name=name,
    )(rank, gates, rows_in, *parts, *flat)


def combine_kernel(capacity, extra, rank, *refs):
    rows, experts = rank.shape
    if extra:
        sums, gates, router, hidden, refs = refs[0], refs[1], refs[2], refs[3], refs[4:]
        *parts, out, small = refs
    else:
        *parts, out = refs
    rows = rows // PAIR
    slot = lax.broadcasted_iota(jnp.int32, (rows, experts * capacity), 1)
    if extra:

        @pl.when(pl.program_id(0) == 0)
        def _():
            small[...] = jnp.zeros_like(small)

    for b in range(PAIR):
        here = slice(b * rows, (b + 1) * rows)
        ranks = rank[here, :]
        pick = jnp.zeros(slot.shape, F32)
        for k in range(experts):
            at = jnp.where(ranks[:, k : k + 1] >= 0, ranks[:, k : k + 1] + k * capacity, -1)
            pick = pick + (slot == at).astype(F32)
        mine = slice(b * capacity, (b + 1) * capacity)
        data = jnp.concatenate([part[i, mine, :] for part in parts for i in range(part.shape[0])], axis=0)
        total = dot(pick.astype(BF16), data)
        if extra:
            grads = sums[b] - gates[b] * jnp.sum(sums[b], axis=0, keepdims=True)
            pad = router.shape[0] - experts
            grads = jnp.concatenate([grads, jnp.zeros((pad, rows), F32)], axis=0).astype(BF16)
            total = total + dot(grads, router[...], ((0,), (0,)))
            small[...] += dot(grads, hidden[here, :])
        out[here, :] = total.astype(BF16)


def combine(rank_cols, parts, rows, capacity, extra=()):
    total_rows, experts = rank_cols.shape
    width = parts[0].shape[2]
    out_specs = [tiles((PAIR * rows, width))]
    out_shape = [jax.ShapeDtypeStruct((total_rows, width), BF16)]
    in_specs = [tiles((PAIR * rows, experts))]
    if extra:
        router = extra[2]
        in_specs += [
            tiles((PAIR, experts, rows)), tiles((PAIR, experts, rows)), whole(router.shape),
            tiles((PAIR * rows, width)),
        ]
        out_specs.append(whole(router.shape))
        out_shape.append(jax.ShapeDtypeStruct(router.shape, F32))
    return pl.pallas_call(
        functools.partial(combine_kernel, capacity, bool(extra)),
        grid=(total_rows // rows // PAIR,),
        in_specs=in_specs
        + [pl.BlockSpec((part.shape[0], PAIR * capacity, width), lambda i: (0, i, 0)) for part in parts],
        out_specs=out_specs,
        out_shape=out_shape,
        compiler_params=pltpu.CompilerParams(vmem_limit_bytes=VMEM_LIMIT),
        cost_estimate=cost(10),
        name="combine",
    )(rank_cols, *extra, *parts)


def body(
    tokens_in,
    cotangent,
    norm1_gain,
    kv_weight,
    query_weight,
    attn_out_weight,
    attn_router,
    norm2_gain,
    in_weight,
    out_weight,
    mlp_router,
    attn_routes,
    mlp_routes,
    place_order,
    seq_lengths,
):
    experts = lax.axis_size("expert")
    shards = lax.axis_size("shard")
    rows, width = tokens_in.shape
    total_rows = rows * shards
    chips = experts // 2
    capacity = -(-5 * rows // (2 * experts) // 16) * 16
    span = query_weight.shape[2] // shards
    inner = out_weight.shape[1]
    depth = in_weight.shape[1]
    order = jnp.stack(expert_order())
    own_expert = order[0]

    chunk = depth // experts
    kv_chunk = lax.dynamic_slice_in_dim(kv_weight, own_expert * chunk, chunk, axis=0)
    kv_chunk = kv_chunk.reshape(chunk, 2, shards, span).transpose(2, 1, 0, 3)
    query_blocks = query_weight[0].reshape(depth, shards, span).transpose(1, 0, 2)
    first_blocks = jnp.concatenate([query_blocks, kv_chunk.reshape(shards, 2 * chunk, span)], axis=1)

    info = jnp.concatenate(
        [place_order, attn_routes.T, mlp_routes.T, jnp.zeros((3, rows), jnp.int32)], axis=0
    )
    rounds = []
    for i, step in enumerate(powers(shards)):
        source = (lambda info=info: info[None]) if i == 0 else (lambda i=i: rounds[i - 1].value)
        rounds.append(Transfer(lambda v, step=step: doubled(v, step), source))
    inverse = jnp.argsort(order)

    stream = tokens_in.astype(F32)
    normed1, row_scale1 = norm_rows(stream, norm1_gain)
    hidden1_own = normed1.astype(BF16)
    first = Transfer(shard_exchange, lambda: first_blocks)
    out_far = fetch_far(lambda: attn_out_weight[0])
    first_far = [fetch_far(lambda: first.value, i, 2) for i in range(2)]
    (hidden1_own,) = begin([hidden1_own], [first])
    gate_blocks, up_blocks = split_columns(in_weight[0], shards)
    down_parts = [part_of(out_weight[0], i) for i in range(PARTS)]
    down_far = [fetch_far(lambda i=i: down_parts[i]) for i in range(PARTS)]
    ring = RingGather(hidden1_own)
    ring.tie([], out_far + rounds[:1])
    ring.step()
    ring.tie([], (), [first, gate_blocks, *down_parts] + out_far + rounds[:1])
    ring.tie([], first_far[0] + rounds[1:2])
    ring.step()
    ring.tie([], (), first_far[0] + rounds[1:2])
    ring.tie([], first_far[1] + rounds[2:3])
    ring.step()
    ring.tie([], (), rounds[2:3])
    for item in rounds[3:]:
        item.value = item.source()
        item.begin()
    info = ring_sorted(rounds[-1].value)
    lengths = seq_lengths[0]
    places = info[:, 0].reshape(total_rows)
    cosine, sine_table, seq_ids = rope_tables(places, lengths)
    starts = jnp.sum(
        jnp.where(jnp.arange(lengths.shape[0])[None, :] < seq_ids[:, None], lengths[None, :], 0), axis=1
    )
    cosine = jnp.concatenate([cosine, cosine], axis=1)
    sine_table = jnp.concatenate([-sine_table, sine_table], axis=1)
    bounds = jnp.stack([starts, places])

    def routes_of(first):
        return info[:, first : first + 2].transpose(0, 2, 1).reshape(total_rows, 2)

    routes_attn = routes_of(1)
    named = jnp.any(info[:, 3:5, None, :] == order[None, None, :, None], axis=1)
    earlier = (jnp.arange(rows)[:, None] < jnp.arange(rows)[None, :]).astype(BF16)
    rank = jnp.einsum("bku,ut->bkt", named.astype(BF16), earlier, preferred_element_type=F32)
    rank = jnp.where(named, rank, -1.0).astype(jnp.int32)
    rank_cols = rank.transpose(0, 2, 1).reshape(total_rows, experts)
    rank_rows = rank.transpose(1, 0, 2)
    attn_router_rel = jnp.take(attn_router, order, axis=1)
    mlp_router_rel = jnp.take(mlp_router, order, axis=1)

    router_wide = jnp.pad(attn_router_rel, ((0, 0), (0, 128 - experts)))
    tables = [cosine, sine_table, bounds, routes_attn, rank, router_wide]
    ring.step()
    ring.tie([], (), tables + first_far[1])
    hidden1_blocks = ring.blocks()
    gate_own = Transfer(shard_exchange, lambda: gate_blocks)
    hidden1_blocks = begin(hidden1_blocks, [gate_own])
    first_all = []
    for pieces in [[first.value]] + [[a.value, b.value] for a, b in zip(*first_far)]:
        first_all += [pieces, [core_swap(piece) for piece in pieces]]
    attn_out_w = with_swaps([attn_out_weight[0]] + [item.value for item in out_far])
    hidden1_blocks = begin(hidden1_blocks, down_far[1] + down_far[2])
    up_own = Transfer(shard_exchange, lambda: up_blocks)
    gate_far = [fetch_far(lambda: gate_own.value, i, PARTS) for i in range(PARTS)]
    up_far = [fetch_far(lambda: up_own.value, i, PARTS) for i in range(PARTS)]

    def first_parts(grad):
        key_grad, value_grad = [
            grad[:, (experts + i) * span : (experts + i + 1) * span].reshape(shards, experts, chunk, span)
            for i in range(2)
        ]
        parts = []
        for k in range(experts):
            query_grad = grad[:, k * span : (k + 1) * span].reshape(shards, depth, span)
            own = [
                lax.dynamic_index_in_dim(item, order[k], axis=1, keepdims=False)
                for item in (key_grad, value_grad)
            ]
            parts.append(jnp.concatenate([query_grad, *own], axis=1))
        return expert_sums(parts, range(0, experts, 2))

    mixed, query, keys, values, vec_wide, gates_attn, hidden1, kv_w = attend(
        hidden1_blocks, first_all, attn_out_w, router_wide, routes_attn, order[None], bounds.T,
        places[None], cosine, sine_table, chunk,
    )
    (mixed,) = tie([mixed], [gate_own] + down_far[1] + down_far[2])
    middle = stream + ring_scatter(
        mixed,
        {
            0: ([up_own] + gate_far[0] + gate_far[1] + gate_far[2], gate_far[0] + gate_far[1] + gate_far[2]),
            1: (gate_far[3], [up_own] + gate_far[3]),
            2: (up_far[0], up_far[0]),
            3: (up_far[1], up_far[1]),
        },
    )

    normed2, row_scale2 = norm_rows(middle, norm2_gain)
    hidden2_own = normed2.astype(BF16)
    cot_steps = RingGather(cotangent)
    ring = RingGather(hidden2_own)
    for part in (up_far[2], up_far[3], down_far[3]):
        ring.tie([], part)
        ring.step()
        ring.tie([], (), part)
    ring.step()
    cot_steps.ahead[0], *ring.last = tie([cotangent, *ring.last], [])
    cot_steps.behind[0] = cot_steps.ahead[0]
    hidden2_blocks = ring.blocks()
    cot_steps.step()
    router_rows = jnp.pad(mlp_router_rel.T, ((0, 16 - experts), (0, 0)))
    rows_in, gates_mlp, hidden2 = dispatch(hidden2_blocks, rank, capacity, router_rows)
    gate_rows = gates_mlp.transpose(1, 0, 2)
    down_own = Transfer(None, None, out_weight[0])
    halves = []
    forwards = []
    rows_now = rows_in
    for first in range(0, experts, 2):
        (rows_now,) = cot_steps.tie([rows_now], () if first else down_far[0])
        cot_steps.step()
        at = first // 2 - 1
        these = [
            [[own.value]] if first == 0 else [[part[at].value for part in far]]
            for own, far in ((gate_own, gate_far), (up_own, up_far), (down_own, down_far))
        ]
        these = [(near[0], [core_swap(piece) for piece in near[0]]) for near in these]
        these = list(zip(*these))
        halves.append((first, these))
        forwards.append(
            list(
                expert_call(
                forward_kernel, "expert_forward", first, rows_now, [], these,
                [inner, inner, inner, width], 0, rank_rows, gate_rows, capacity,
                )
            )
        )
        (forwards[-1][3],) = cot_steps.tie([forwards[-1][3]], (), () if first else down_far[0])
        rows_now = after(rows_now, forwards[-1][3])
    gates_low, ups_low, acts, results = zip(*forwards)
    cot_steps.step()
    combined = combine(rank_cols, results, rows, capacity)[0]
    (combined,) = cot_steps.tie([combined])
    cot_blocks = cot_steps.blocks()
    cot_blocks[0] = after(cot_blocks[0], combined)
    result_steps = RingScatter(combined)
    result_steps.step()
    rows_cot = dispatch(cot_blocks, rank, capacity)[0]
    rows_cot = dispatch(cot_blocks, rank, capacity)[0]
    backs, gate_w_grads = {}, {}
    cot_now = rows_cot
    calls = halves[:0:-1] + [(1, halves[0][1][1:]), (0, halves[0][1][:1])]
    for first, these in calls:
        at = first // 2
        (cot_now,) = result_steps.tie([cot_now], gate_hand[1 - first] if first < 2 else ())
        result_steps.step()
        back = [*expert_call(
            backward_kernel, "expert_backward", first, cot_now, [gates_low[at], ups_low[at], acts[at]],
            these, [inner, inner, width], 1, rank_rows, gate_rows, capacity, first % 2,
        )]
        (back[2],) = result_steps.tie([back[2]], (), gate_hand[1 - first] if first < 2 else ())
        cot_now = after(cot_now, back[2])
        for k in range(len(these)):
            backs[first + k] = [back[0][k], back[1][k], back[2], back[3]]
        if first >= 2:
            for k in (first + 1, first):
                gate_w_grads[k] = dot(backs[k][0], rows_in[k], ((0,), (0,))).astype(BF16)
                cot_now = after(cot_now, gate_w_grads[k])
            gate_sums_far = expert_sums(gate_w_grads, range(2, experts, 2)) if first == 2 else None
            gate_hand = [hand_far(lambda: gate_sums_far, i, PARTS) for i in range(PARTS)]
    grad_gates, grad_ups = [[backs[k][i] for k in range(experts)] for i in range(2)]
    groups = [0, 1] + list(range(2, experts, 2))
    grads, gate_sums = [[backs[k][i] for k in groups] for i in (2, 3)]
    acts = [item[i] for item in acts for i in range(2)]
    gate_sums = jnp.concatenate(gate_sums, axis=0).transpose(1, 0, 2)
    grads = begin(grads[:1], gate_hand[2]) + grads[1:]
    combined, mlp_part = combine(
        rank_cols, grads, rows, capacity, (gate_sums, gates_mlp, router_rows, hidden2)
    )
    result_rows = result_steps.total()
    output = (middle + result_rows).astype(BF16)
    up_w_grads, down_w_grads = {}, {}

    def weight_grad(into, left, right, k, late):
        into[k] = dot(after(left[k], late), right[k], ((0,), (0,))).astype(BF16)
        return into[k]

    gate_back = Transfer(
        lambda v: shard_exchange(v.reshape(inner, shards, depth).transpose(1, 0, 2)),
        lambda: gate_total,
    )
    up_back = Transfer(shard_exchange, lambda: up_total)
    ring = RingScatter(combined)
    (late,) = ring.tie([after(rank, result_rows)], (), gate_hand[2])
    (late,) = ring.tie([late], gate_hand[3])
    for k in range(experts - 1, 3, -1):
        weight_grad(up_w_grads, grad_ups, rows_in, k, late)
    ring.step()
    weight_grad(up_w_grads, grad_ups, rows_in, 3, late)
    (late,) = ring.tie([late], (), [up_w_grads[3]])
    ring.step()
    weight_grad(up_w_grads, grad_ups, rows_in, 2, late)
    (late,) = ring.tie([late], (), [up_w_grads[2]] + gate_hand[3])
    ring.step()
    up_sums_far = expert_sums(up_w_grads, range(2, experts, 2))
    up_hand = [hand_far(lambda: up_sums_far, i, PARTS) for i in range(PARTS)]
    weight_grad(gate_w_grads, grad_gates, rows_in, 1, late)
    (late,) = ring.tie([late], (), [gate_w_grads[1], *up_sums_far])
    ring.step()
    weight_grad(gate_w_grads, grad_gates, rows_in, 0, late)
    gate_near = expert_sums(gate_w_grads, [0])[0].astype(F32)
    (late,) = ring.tie([late], (), [gate_w_grads[0]])
    back_rows = ring.total()
    grad_hidden2 = back_rows
    grad_middle, grad_gain2 = norm_back(grad_hidden2, middle, row_scale2, norm2_gain)
    grad_middle = grad_middle + cotangent.astype(F32)

    gate_total = total_of(gate_near, gate_hand).astype(BF16)
    gate_total = total_of(gate_near, gate_hand).astype(BF16)
    ring = RingGather(grad_middle.astype(BF16))
    (late,) = ring.tie([late], [gate_back] + up_hand[0] + up_hand[1])
    ring.step()
    weight_grad(up_w_grads, grad_ups, rows_in, 1, late)
    weight_grad(down_w_grads, acts, rows_cot, 1, late)
    (late,) = ring.tie([late], (), [up_w_grads[1], down_w_grads[1]] + up_hand[0] + up_hand[1])
    (late,) = ring.tie([late], up_hand[2] + up_hand[3])
    ring.step()
    weight_grad(up_w_grads, grad_ups, rows_in, 0, late)
    up_near = expert_sums(up_w_grads, [0])[0].astype(F32)
    for k in [*range(experts - 1, 1, -1), 0]:
        weight_grad(down_w_grads, acts, rows_cot, k, late)
    down_sums_far = expert_sums(down_w_grads, range(2, experts, 2))
    down_hand = [hand_far(lambda: down_sums_far, i, PARTS) for i in range(PARTS)]
    (late,) = ring.tie([late], (), [up_w_grads[0], down_w_grads[0], *down_sums_far, gate_back] + up_hand[2] + up_hand[3])
    (late,) = ring.tie([late], down_hand[0])
    ring.step()
    up_total = total_of(up_near, up_hand).astype(BF16)
    up_total = up_total.reshape(inner, shards, depth).transpose(1, 0, 2)
    (late,) = ring.tie([late], (), [up_total] + down_hand[0])
    ring.step()
    (late,) = ring.tie([late])
    mid_blocks = ring.blocks()
    mid_blocks = begin(mid_blocks, [up_back] + down_hand[1] + down_hand[2] + down_hand[3])
    grad_rows1, grad_first, attn_part, grad_mid = attend_back(
        mid_blocks, first_all, kv_w, attn_out_w, router_wide, hidden1, routes_attn, order[None], gates_attn, bounds,
        places[:, None], cosine, sine_table, query, keys, values, vec_wide,
    )
    grad_rows1, grad_first, attn_part, late = tie(
        [grad_rows1, grad_first, attn_part, late], down_hand[1] + down_hand[2] + down_hand[3]
    )
    sums = jnp.concatenate(
        [
            jnp.sum(attn_part[-8:], axis=0, keepdims=True) / norm1_gain,
            grad_gain2[None],
            jnp.take(attn_part, inverse, axis=0),
            jnp.take(mlp_part, inverse, axis=0),
        ],
        axis=0,
    )
    rounds = [("expert", step) for step in powers(experts)] + [("shard", step) for step in powers(shards)]
    small = []
    for i, (axis, step) in enumerate(rounds):
        source = (lambda: sums) if i == 0 else (lambda i=i: small[i - 1].value)
        small.append(Transfer(lambda v, axis=axis, step=step: sum_pairs(v, axis, step), source))
    ring = RingScatter(grad_rows1)
    late, grad_first = ring.tie([late, grad_first], small[:1])
    ring.step()
    grad_first_w = dot(hidden1, grad_first, ((0,), (0,))).astype(BF16)
    first_sums = first_parts(grad_first_w)
    first_hand = [hand_far(lambda: first_sums[1:], i, 2) for i in range(2)]
    (late,) = tie([late], [grad_first_w] + small[:1])
    (late,) = begin([late], small[1:2])
    (late,) = ring.tie([late], (), [up_back] + first_sums + small[1:2])
    (late,) = ring.tie([late], first_hand[0] + small[2:3])
    ring.step()
    (late,) = ring.tie([late], (), first_hand[0] + small[2:3])
    (late,) = ring.tie([late], first_hand[1] + small[3:4])
    ring.step()
    ring.step()
    grad_second_w = dot(after(vec_wide, late), grad_mid, ((0,), (0,))).astype(BF16)
    (late,) = ring.tie([late], (), first_hand[1] + small[3:4] + [grad_second_w])
    came = [jnp.concatenate([a.value, b.value], axis=0) for a, b in zip(*first_hand)]
    first_grad = sum_f32(first_sums[:1] + came).astype(BF16)
    first_back = Transfer(shard_exchange, lambda: first_grad)
    second_sums = expert_sums(jnp.split(grad_second_w, experts, axis=0), range(0, experts, 2))
    second_hand = hand_far(lambda: second_sums[1:])
    ring.tie([], [first_back])
    came_back = [gate_back, up_back] + [item for part in down_hand for item in part]
    for item, value in zip(came_back, begin([item.value for item in came_back], second_hand)):
        item.value = value
    for item in small[4:]:
        (late,) = tie(begin([late], [item]), [item])
    back_rows1 = ring.total()
    in_grad = join_columns(gate_back.value, up_back.value)[None]
    attn_grad = sum_f32(second_sums[:1] + [item.value for item in second_hand])[None]
    out_grad = total_of(expert_sums(down_w_grads, [0])[0].astype(F32), down_hand)[None]
    sums = small[-1].value
    grad_hidden1 = back_rows1
    grad_stream, _ = norm_back(grad_hidden1, stream, row_scale1, norm1_gain)
    grad_input = grad_stream + grad_middle

    first_grad = first_back.value
    query_grad = first_grad[:, :depth].transpose(1, 0, 2).reshape(1, depth, shards * span).astype(F32)
    kv_grad = first_grad[:, depth:].reshape(shards, 2, chunk, span)
    kv_grad = kv_grad.transpose(2, 1, 0, 3).reshape(chunk, 2 * shards * span)
    pieces = expert_gather(kv_grad.astype(BF16))
    kv_grad = jnp.zeros((depth, 2 * shards * span), F32)
    for k, piece in enumerate(pieces):
        kv_grad = lax.dynamic_update_slice_in_dim(kv_grad, piece.astype(F32), order[k] * chunk, axis=0)

    return (
        output,
        grad_input,
        sums[0],
        kv_grad,
        query_grad,
        attn_grad,
        sums[2 : 2 + experts].T,
        sums[1],
        in_grad,
        out_grad,
        sums[2 + experts :].T,
    )


def solution(mesh):
    return jax.shard_map(
        body,
        mesh=mesh,
        in_specs=(
            P(("expert", "shard"), None),
            P(("expert", "shard"), None),
            P(),
            P("shard", None),
            P("expert", "shard", None),
            P("expert", "shard", None),
            P(),
            P(),
            P("expert", "shard", None),
            P("expert", "shard", None),
            P(),
            P(("expert", "shard"), None),
            P(("expert", "shard"), None),
            P("expert", "shard"),
            P("expert", None),
        ),
        out_specs=(
            P(("expert", "shard"), None),
            P(("expert", "shard"), None),
            P(),
            P("shard", None),
            P("expert", "shard", None),
            P("expert", "shard", None),
            P(),
            P(),
            P("expert", "shard", None),
            P("expert", "shard", None),
            P(),
        ),
        check_vma=False,
    )
```
